32 devices in a mesh: dp: 8 (over y, x, core), mp: 4 (over z).
Axes of the slice: x: 2, y: 2, z: 4, core: 2. Of those that a mesh axis runs over, the one named last changes fastest.
Arguments:
- tokens: bfloat16 [512, 40, 768], P(('dp', 'mp')), may hold values from -6 to 6
- patches: bfloat16 [128, 145, 1024], P('dp'), may hold values from -6 to 6
- image_rows: int32 [8, 16], P('dp'), may hold values from 1 to 7, 64 in all within a row
- row_lengths: int32 [512], P('dp'), may hold values from 4 to 40, as said below
- box_mask: int32 [512, 145], P('dp'), may hold values from 0 to 1, as said below
- self_project: bfloat16 [3, 768, 768], P(None, None, 'mp'), may hold values from -0.21875 to 0.21875
- self_output: bfloat16 [768, 768], P('mp'), may hold values from -0.875 to 0.875
- first_gain: float32 [768], replicated, may hold values from 0.5 to 1.5
- first_shift: float32 [768], replicated, may hold values from -2 to 2
- cross_query: bfloat16 [768, 768], P(None, 'mp'), may hold values from -0.21875 to 0.21875
- cross_keyval: bfloat16 [2, 1024, 768], P(None, None, 'mp'), may hold values from -0.1875 to 0.1875
- cross_output: bfloat16 [768, 768], P('mp'), may hold values from -0.875 to 0.875
- second_gain: float32 [768], replicated, may hold values from 0.5 to 1.5
- second_shift: float32 [768], replicated, may hold values from -2 to 2
- expand_weight: bfloat16 [768, 3072], P(None, 'mp'), may hold values from -0.21875 to 0.21875
- expand_bias: float32 [3072], P('mp'), may hold values from -3 to 3
- shrink_weight: bfloat16 [3072, 768], P('mp'), may hold values from -0.109375 to 0.109375
- third_gain: float32 [768], replicated, may hold values from 0.5 to 1.5
- third_shift: float32 [768], replicated, may hold values from -2 to 2
- cotangent: bfloat16 [512, 40, 768], P(('dp', 'mp')), may hold values from -6 to 6
Outputs:
- joined_text: bfloat16 [512, 40, 768], P(('dp', 'mp'))
- text_grad: float32 [512, 40, 768], P(('dp', 'mp'))
- patch_grad: float32 [128, 145, 1024], P('dp', None, 'mp')
- self_project_grad: float32 [3, 768, 768], P(None, None, 'mp')
- self_output_grad: float32 [768, 768], P('mp')
- first_gain_grad: float32 [768], replicated
- first_shift_grad: float32 [768], replicated
- cross_query_grad: float32 [768, 768], P(None, 'mp')
- cross_keyval_grad: float32 [2, 1024, 768], P(None, None, 'mp')
- cross_output_grad: float32 [768, 768], P('mp')
- second_gain_grad: float32 [768], replicated
- second_shift_grad: float32 [768], replicated
- expand_weight_grad: float32 [768, 3072], P(None, 'mp')
- expand_bias_grad: float32 [3072], P('mp')
- shrink_weight_grad: float32 [3072, 768], P('mp')
- third_gain_grad: float32 [768], replicated
- third_shift_grad: float32 [768], replicated
The draws below stay inside these ranges and needn't reach their ends.
Inputs may be any that keep to these rules, and one draw needn't show every extreme that they name: `image_rows`: rows of each image, in the order of the 64 rows of its index of dp; each index's counts sum to 64. An image's first row is its caption, the others are its box phrases. `row_lengths`: tokens in use at the start of each row; every row whose number is a multiple of 16 uses all 40. `box_mask`: 1 at patch 0 and at the patches 1 + 12 * i + j of a rectangle of 3 or more by 3 or more cells of the 12 by 12 grid; read only for rows that are not captions.
All inputs are finite; a program needn't handle non-finite values.
Results may differ from the reference program's by a relative error of at most 0.02.
Values may be sent and summed in bfloat16 or wider, within the bound.
A program may use at most 256 MiB of HBM per device.

```python
import math
import jax
import jax.numpy as jnp
import numpy as np
from jax import lax

D = 768
HEAD_DIM = 64
FF = 3072
PATCH_DIM = 1024
GRID = 12
ROW_LEN = 40
ROWS_MAX = 7
ROW_DEV = 16
ROW_GROUP = 64
IMG_DEV = 16
GROUPS = 8
ROWS = 512
IMAGES = 128
PATCHES = 145
N_DP = 8


def draw_row_lengths(key, part):
    key = jax.random.fold_in(key, 11)
    drawn = jax.random.randint(key, (ROWS,), 4, ROW_LEN + 1, dtype=jnp.int32)
    row_index = jnp.arange(ROWS, dtype=jnp.int32)
    return jnp.where(row_index % ROW_DEV == 0, ROW_LEN, drawn).astype(jnp.int32)


def draw_box_mask(key, part):
    key = jax.random.fold_in(key, 23)
    subkeys = jax.random.split(key, 4)
    col_start = jax.random.randint(subkeys[0], (ROWS, 1), 0, GRID - 2, dtype=jnp.int32)
    col_width = jax.random.randint(subkeys[1], (ROWS, 1), 3, GRID - col_start + 1, dtype=jnp.int32)
    row_start = jax.random.randint(subkeys[2], (ROWS, 1), 0, GRID - 2, dtype=jnp.int32)
    row_height = jax.random.randint(subkeys[3], (ROWS, 1), 3, GRID - row_start + 1, dtype=jnp.int32)
    patch_index = jnp.arange(PATCHES - 1, dtype=jnp.int32)[None, :]
    patch_col = patch_index % GRID
    patch_row = patch_index // GRID
    inside = (patch_col >= col_start) & (patch_col < col_start + col_width) & (patch_row >= row_start) & (patch_row < row_start + row_height)
    return jnp.concatenate([jnp.ones((ROWS, 1), jnp.int32), inside.astype(jnp.int32)], axis=1)


def block_levels(key, shape, shards, low, high):
    level, own = 1.0, jax.random.fold_in(key, 6)
    for position, blocks in shards:
        steps = jnp.exp(jax.random.uniform(jax.random.fold_in(own, position), (blocks,), jnp.float32, low / len(shards), high / len(shards)))
        level = level * jnp.repeat(steps, shape[position] // blocks).reshape([-1 if axis == position else 1 for axis in range(len(shape))])
    return level


def profile(amount, total, reach, slope):
    portions = [(1 << 20) // math.isqrt(rank ** slope) + 1 for rank in range(2, amount + 1)]
    rest, holding = total - reach - (amount - 1), [1] * (amount - 1)
    while rest > 0:
        candidates = [i for i in range(amount - 1) if holding[i] < reach]
        whole, left = sum([portions[i] for i in candidates]), rest
        for i in candidates:
            extra = min(reach - holding[i], max(1, left * portions[i] // whole), rest)
            holding[i] = holding[i] + extra
            rest = rest - extra
    return np.array([reach] + holding)


def ragged(key, count, total, limit, skew):
    if count == 2:
        one = jax.random.randint(key, (), max(1, total - limit), min(limit, total - 1) + 1)
        return jnp.stack([one, total - one])
    tallies = jnp.asarray(profile(count, total, limit, skew), jnp.int32)
    pairs = (count - 1) // 2
    donor, receiver = tallies[1:1 + 2 * pairs:2], tallies[2:2 + 2 * pairs:2]
    slack = jnp.minimum(donor - 1, limit - receiver)
    moved = jax.random.randint(jax.random.fold_in(key, 1), (pairs,), 0, 1 << 20) % (slack + 1)
    tallies = tallies.at[1:1 + 2 * pairs:2].set(donor - moved).at[2:2 + 2 * pairs:2].set(receiver + moved)
    return tallies[jax.random.permutation(jax.random.fold_in(key, 2), count)]


def scatter_about(own_key, shape, scale, bound, shards=(), kind=jnp.bfloat16):
    level = block_levels(own_key, shape, shards, -0.22, 0.18) if shards else 1.0
    values = jax.random.normal(own_key, shape, jnp.float32) * scale * level
    return jnp.minimum(jnp.maximum(values, -bound), bound).astype(kind)


def setup_inputs(seed: int = 0) -> dict:
    seeds = jax.random.split(jax.random.key(seed), 21)
    return {
        "tokens": scatter_about(seeds[0], (ROWS, ROW_LEN, D), 1.0, 6.0, ((0, 32),)),
        "patches": scatter_about(seeds[1], (IMAGES, PATCHES, PATCH_DIM), 1.0, 6.0, ((0, 8),)),
        "image_rows": jax.vmap(lambda own: ragged(own, IMG_DEV, ROW_GROUP, ROWS_MAX, 2))(jax.random.split(seeds[2], GROUPS)).reshape((GROUPS, IMG_DEV)).astype(jnp.int32),
        "row_lengths": draw_row_lengths(jax.random.fold_in(seeds[20], 71), 0),
        "box_mask": draw_box_mask(jax.random.fold_in(seeds[20], 71), 0),
        "self_project": scatter_about(seeds[5], (3, D, D), D ** -0.5, 0.21875, ((2, 4),)),
        "self_output": scatter_about(seeds[6], (D, D), (D // 16) ** -0.5, 0.875, ((0, 4),)),
        "first_gain": jnp.clip(1.0 + 0.1 * jax.random.normal(seeds[7], (D,), jnp.float32), 0.5, 1.5),
        "first_shift": scatter_about(seeds[8], (D,), 0.3, 2.0, (), jnp.float32),
        "cross_query": scatter_about(seeds[9], (D, D), D ** -0.5, 0.21875, ((1, 4),)),
        "cross_keyval": scatter_about(seeds[10], (2, PATCH_DIM, D), PATCH_DIM ** -0.5, 0.1875, ((2, 4),)),
        "cross_output": scatter_about(seeds[11], (D, D), (D // 16) ** -0.5, 0.875, ((0, 4),)),
        "second_gain": jnp.clip(1.0 + 0.1 * jax.random.normal(seeds[12], (D,), jnp.float32), 0.5, 1.5),
        "second_shift": scatter_about(seeds[13], (D,), 0.3, 2.0, (), jnp.float32),
        "expand_weight": scatter_about(seeds[14], (D, FF), D ** -0.5, 0.21875, ((1, 4),)),
        "expand_bias": scatter_about(seeds[15], (FF,), 0.5, 3.0, ((0, 4),), jnp.float32),
        "shrink_weight": scatter_about(seeds[16], (FF, D), FF ** -0.5, 0.109375, ((0, 4),)),
        "third_gain": jnp.clip(1.0 + 0.1 * jax.random.normal(seeds[17], (D,), jnp.float32), 0.5, 1.5),
        "third_shift": scatter_about(seeds[18], (D,), 0.3, 2.0, (), jnp.float32),
        "cotangent": scatter_about(seeds[19], (ROWS, ROW_LEN, D), 1.0, 6.0, ((0, 32),)),
    }


@jax.custom_vjp
def low(v):
    return lax.optimization_barrier(v.astype(jnp.bfloat16)).astype(jnp.float32)

@jax.custom_vjp
def low_back(v):
    return v

def low_keep(v):
    return (low(v), None)

def low_pass(kept, grad):
    return (grad,)

def back_keep(v):
    return (v, None)

def back_low(kept, grad):
    return (low(grad),)
low.defvjp(low_keep, low_pass)
low_back.defvjp(back_keep, back_low)
highest = lax.Precision.HIGHEST

def matmul(left_side, right_side):
    return jnp.matmul(left_side, right_side, precision=highest)

def rows_structure(counts, group_rows):
    counts = counts.astype(jnp.int32)
    row_ends = jnp.cumsum(counts).astype(jnp.int32)
    starts = (row_ends - counts).astype(jnp.int32)
    row_index = jnp.arange(group_rows, dtype=jnp.int32)[:, None]
    member = (row_index >= starts[None, :]) & (row_index < row_ends[None, :])
    caption = jnp.any(row_index == starts[None, :], axis=1)
    return (member, caption)

def layer_norm(hidden, norm_gain, norm_shift):
    center = hidden - lax.optimization_barrier(jnp.mean(hidden, axis=-1, keepdims=True))
    scaled = center * lax.rsqrt(lax.optimization_barrier(jnp.mean(center * center, axis=-1, keepdims=True)) + 1e-06)
    return scaled * norm_gain + norm_shift

def split_heads(values):
    return values.reshape(values.shape[0], values.shape[1], values.shape[2] // HEAD_DIM, HEAD_DIM)

def attention(query_rows, key_rows, value_rows, allowed):
    scores = jnp.einsum('gqhe,gkhe->ghqk', split_heads(query_rows), split_heads(key_rows), precision=highest) * HEAD_DIM ** (-0.5)
    scores = jnp.where(allowed[:, None, None, :], scores, -1000000000.0)
    scores = low_back(scores)
    probs = jax.nn.softmax(scores, axis=-1)
    weights = low(probs)
    context = jnp.einsum('ghqk,gkhe->gqhe', weights, split_heads(value_rows), precision=highest)
    context = context.reshape(query_rows.shape)
    return low(low_back(context))

def forward(params, text_rows, pixels, member, key_ok, cross_ok):
    self_project, self_output, first_gain, first_shift, cross_query, cross_keyval, cross_output, second_gain, second_shift, expand_weight, expand_bias, shrink_weight, third_gain, third_shift = params
    text_low = low(text_rows)
    query_rows = low(low_back(matmul(text_low, self_project[0])))
    key_rows = low(low_back(matmul(text_low, self_project[1])))
    value_rows = low(low_back(matmul(text_low, self_project[2])))
    self_context = attention(query_rows, key_rows, value_rows, key_ok)
    after_first = layer_norm(text_rows + low_back(matmul(self_context, self_output)), first_gain, first_shift)
    cross_queries = low(low_back(matmul(low(after_first), cross_query)))
    pixel_low = low(pixels)
    image_keys = low(low_back(matmul(pixel_low, cross_keyval[0])))
    image_values = low(low_back(matmul(pixel_low, cross_keyval[1])))
    row_keys = jnp.einsum('gi,ipd->gpd', member, image_keys, precision=highest)
    row_values = jnp.einsum('gi,ipd->gpd', member, image_values, precision=highest)
    cross_context = attention(cross_queries, row_keys, row_values, cross_ok)
    second = layer_norm(after_first + low_back(matmul(cross_context, cross_output)), second_gain, second_shift)
    expanded = low_back(matmul(low(second), expand_weight) + expand_bias)
    activated = low(jax.nn.gelu(expanded, approximate=False))
    return layer_norm(second + low_back(matmul(activated, shrink_weight)), third_gain, third_shift)

def reference(tokens, patches, image_rows, row_lengths, box_mask, self_project, self_output, first_gain, first_shift, cross_query, cross_keyval, cross_output, second_gain, second_shift, expand_weight, expand_bias, shrink_weight, third_gain, third_shift, cotangent):
    params = tuple((weight.astype(jnp.float32) for weight in (self_project, self_output, first_gain, first_shift, cross_query, cross_keyval, cross_output, second_gain, second_shift, expand_weight, expand_bias, shrink_weight, third_gain, third_shift)))

    def step(totals, inputs):
        text_rows, pixels, counts, lengths, box_rows, upstream = inputs
        member, caption = rows_structure(counts, ROW_GROUP)
        key_ok = jnp.arange(ROW_LEN, dtype=jnp.int32)[None, :] < lengths[:, None]
        cross_ok = caption[:, None] | (box_rows > 0)
        member_float = member.astype(jnp.float32)

        def run(weights_in, text_in, pixels_in):
            return forward(weights_in, text_in, pixels_in, member_float, key_ok, cross_ok)
        result, pullback = jax.vjp(run, params, text_rows.astype(jnp.float32), pixels.astype(jnp.float32))
        gradients, text_part, pixel_part = pullback(upstream.astype(jnp.float32))
        totals = jax.tree.map(lambda left_term, right_term: left_term + right_term, totals, gradients)
        return (totals, (result.astype(jnp.bfloat16), text_part, pixel_part))
    initial = jax.tree.map(jnp.zeros_like, params)
    inputs = (tokens.reshape(N_DP, ROW_GROUP, ROW_LEN, D), patches.reshape(N_DP, IMG_DEV, PATCHES, PATCH_DIM), image_rows, row_lengths.reshape(N_DP, ROW_GROUP), box_mask.reshape(N_DP, ROW_GROUP, PATCHES), cotangent.reshape(N_DP, ROW_GROUP, ROW_LEN, D))
    totals, (joined, text_grad, pixel_grad) = lax.scan(step, initial, inputs)
    return (joined.reshape(ROWS, ROW_LEN, D), text_grad.reshape(ROWS, ROW_LEN, D), pixel_grad.reshape(IMAGES, PATCHES, PATCH_DIM), totals[0], totals[1], totals[2], totals[3], totals[4], totals[5], totals[6], totals[7], totals[8], totals[9], totals[10], totals[11], totals[12], totals[13])
```

```python
import functools

import jax
import jax.numpy as jnp
from jax import lax
from jax.experimental import pallas as pl
from jax.experimental.pallas import tpu as pltpu
from jax.sharding import PartitionSpec as P

HEAD_DIM = 64
ROWS_MAX = 7
MESH = pl.DeviceIdType.MESH


def place():
    index = lax.axis_index("dp")
    plane = lax.axis_index("mp")
    y, x, c = index // 4, (index // 2) % 2, index % 2
    return index, plane, y, x, c


def partners(index, plane):
    core = (index + 1 - 2 * (index % 2), plane)
    across = (index + 2 - 4 * ((index // 2) % 2), plane)
    along = (index + 4 - 8 * (index // 4), plane)
    planes = [(index, lax.rem(plane + step, 4)) for step in (1, 2, 3)]
    return core, across, along, planes


def greet(peers):
    barrier = pltpu.get_barrier_semaphore()
    for peer in peers:
        pl.semaphore_signal(barrier, inc=1, device_id=peer, device_id_type=MESH)
    pl.semaphore_wait(barrier, len(peers))


def gather_kernel(chunks, count, *refs):
    shards, outs, wholes = refs[:count], refs[count : 2 * count], refs[2 * count : 3 * count]
    final_sem, local_sem, plane_send, plane_recv, near_send, near_recv, far_send, far_recv, core_send, core_recv = refs[3 * count :]
    index, plane, y, x, c = place()
    core, across, along, planes = partners(index, plane)
    greet([core, across, along] + planes)
    others = [lax.rem(plane + step, 4) for step in (1, 2, 3)]
    total = len(chunks)

    def send(source, target, sends, recvs, peer):
        copy = pltpu.make_async_remote_copy(
            src_ref=source, dst_ref=target, send_sem=sends, recv_sem=recvs, device_id=peer, device_id_type=MESH
        )
        copy.start()
        return copy

    copies = {}
    sent = []

    def keep(name, k, items):
        copies[name, k] = items
        sent.extend(items)

    def arrived(name, k):
        for copy in copies[name, k]:
            copy.wait_recv()

    def sizes(k):
        which, base, rows = chunks[k]
        return which, base, rows // 8, shards[which].shape[1] // 2

    def level(k):
        which, base, r, w = sizes(k)
        items = []
        for h, first in enumerate((x * 2 + y, y * 2 + x)):
            row = pl.multiple_of(base + (c * 4 + first) * r, 16)
            here = (pl.ds(row, r), pl.ds(h * w, w))
            for j, peer in enumerate(planes):
                items.append(
                    send(
                        shards[which].at[here],
                        wholes[which].at[(plane,) + here],
                        plane_send.at[k, h, j],
                        plane_recv.at[k, h, j],
                        peer,
                    )
                )
        keep("plane", k, items)

    def near(k):
        which, base, r, w = sizes(k)
        arrived("plane", k)
        if k + window < total:
            level(k + window)
        items = []
        for h, first in enumerate((x * 2 + y, y * 2 + x)):
            row = pl.multiple_of(base + (c * 4 + first) * r, 16)
            for j, other in enumerate(others):
                piece = wholes[which].at[other, pl.ds(row, r), pl.ds(h * w, w)]
                items.append(send(piece, piece, near_send.at[k, h, j], near_recv.at[k, h, j], (along, across)[h]))
        keep("near", k, items)

    def far(k):
        which, base, r, w = sizes(k)
        arrived("near", k)
        items = []
        for h, first in enumerate((x, y)):
            row = pl.multiple_of(base + (c * 4 + first * 2) * r, 16)
            for j, other in enumerate(others):
                piece = wholes[which].at[other, pl.ds(row, 2 * r), pl.ds(h * w, w)]
                items.append(send(piece, piece, far_send.at[k, h, j], far_recv.at[k, h, j], (across, along)[h]))
        keep("far", k, items)

    def cross(k):
        which, base, r, w = sizes(k)
        arrived("far", k)
        row = pl.multiple_of(base + c * 4 * r, 16)
        items = []
        for j, other in enumerate(others):
            piece = wholes[which].at[other, pl.ds(row, 4 * r), :]
            items.append(send(piece, piece, core_send.at[k, j], core_recv.at[k, j], core))
        keep("core", k, items)

    final = []

    def end(k):
        which, base, r, w = sizes(k)
        arrived("core", k)
        if k + 1 == total or chunks[k + 1][0] != which:
            local[which].wait()
            copy = pltpu.make_async_copy(wholes[which], outs[which], final_sem.at[which])
            copy.start()
            final.append(copy)

    window, gap = 3, 2
    for k in range(window):
        level(k)
    local = []
    for which in range(count):
        copy = pltpu.make_async_copy(shards[which], wholes[which].at[plane], local_sem.at[which])
        copy.start()
        local.append(copy)
    stages = [near, far, cross, end]
    for t in range(total + gap * (len(stages) - 1)):
        for s in reversed(range(len(stages))):
            if 0 <= t - gap * s < total:
                stages[s](t - gap * s)
    for copy in sent:
        copy.wait_send()
    for copy in final:
        copy.wait()


def gather_weights(shards, chunks, collective_id=0):
    count = len(shards)
    total = len(chunks)
    dma = pltpu.SemaphoreType.DMA
    return pl.pallas_call(
        functools.partial(gather_kernel, chunks, count),
        out_shape=[jax.ShapeDtypeStruct((4,) + s.shape, s.dtype) for s in shards],
        in_specs=[pl.BlockSpec(memory_space=pl.ANY)] * count,
        out_specs=[pl.BlockSpec(memory_space=pl.ANY)] * count,
        scratch_shapes=[pltpu.VMEM((4,) + s.shape, s.dtype) for s in shards]
        + [dma((count,))] * 2 + [dma((total, 2, 3))] * 6 + [dma((total, 3))] * 2,
        compiler_params=pltpu.CompilerParams(
            collective_id=collective_id, has_side_effects=True, vmem_limit_bytes=60 << 20
        ),
        name="gather_weights",
    )(*shards)


def reduce_kernel(count, *refs):
    grads, sums = refs[:count], refs[count : 2 * count]
    rest = refs[2 * count :]
    bufs = [rest[i * count : (i + 1) * count] for i in range(6)]
    mine, core_in, near_in, far_in, plane_in, done = bufs
    (local_sem, core_send, core_recv, near_send, near_recv, far_send, far_recv, plane_send, plane_recv,
     out_near_send, out_near_recv, out_far_send, out_far_recv, out_core_send, out_core_recv, final_sem) = rest[6 * count :]
    index, plane, y, x, c = place()
    core, across, along, planes = partners(index, plane)
    greet([core, across, along] + planes)
    others = [lax.rem(plane + step, 4) for step in (1, 2, 3)]

    def send(source, target, sends, recvs, peer):
        copy = pltpu.make_async_remote_copy(
            src_ref=source, dst_ref=target, send_sem=sends, recv_sem=recvs, device_id=peer, device_id_type=MESH
        )
        copy.start()
        return copy

    def blocks(k):
        _, rows, width = grads[k].shape
        return rows // 8, width // 2

    def add(total, total_row, total_col, part, part_col, rows, cols):
        step = 16
        @pl.loop(0, rows // step)
        def _(i):
            for shard in range(4):
                here = (shard, pl.ds(pl.multiple_of(total_row + i * step, 16), step), pl.ds(total_col, cols))
                there = (shard, pl.ds(pl.multiple_of(i * step, 16), step), pl.ds(part_col, cols))
                total[here] = (total[here].astype(jnp.float32) + part[there].astype(jnp.float32)).astype(jnp.bfloat16)

    copies = {}
    sends = []

    def keep(name, k, items):
        copies[name, k] = items
        sends.extend(items)

    def arrived(name, k):
        for copy in copies[name, k]:
            copy.wait_recv()

    local = {}

    def begin(k):
        r, w = blocks(k)
        theirs = pl.multiple_of((1 - c) * 4 * r, 16)
        ours = pl.multiple_of(c * 4 * r, 16)
        keep("core", k, [send(grads[k].at[:, pl.ds(theirs, 4 * r), :], core_in[k], core_send.at[k], core_recv.at[k], core)])
        local[k] = pltpu.make_async_copy(grads[k].at[:, pl.ds(ours, 4 * r), :], mine[k], local_sem.at[k])
        local[k].start()

    def near(k):
        r, w = blocks(k)
        local[k].wait()
        arrived("core", k)
        add(mine[k], 0, 0, core_in[k], 0, 4 * r, 2 * w)
        items = []
        for h, (bit, peer) in enumerate([(x, across), (y, along)]):
            row = pl.multiple_of((1 - bit) * 2 * r, 16)
            items.append(send(mine[k].at[:, pl.ds(row, 2 * r), pl.ds(h * w, w)], near_in[k].at[h], near_send.at[k, h], near_recv.at[k, h], peer))
        keep("near", k, items)

    def far(k):
        r, w = blocks(k)
        arrived("near", k)
        items = []
        for h, (bit, second, peer) in enumerate([(x, y, along), (y, x, across)]):
            row = bit * 2 * r
            add(mine[k], row, h * w, near_in[k].at[h], 0, 2 * r, w)
            row = pl.multiple_of(row + (1 - second) * r, 16)
            items.append(send(mine[k].at[:, pl.ds(row, r), pl.ds(h * w, w)], far_in[k].at[h], far_send.at[k, h], far_recv.at[k, h], peer))
        keep("far", k, items)

    def places(k):
        r, w = blocks(k)
        return [((x * 2 + y) * r, 0), ((y * 2 + x) * r, w)]

    def level(k):
        r, w = blocks(k)
        arrived("far", k)
        items = []
        for h, (row, col) in enumerate(places(k)):
            add(mine[k], row, col, far_in[k].at[h], 0, r, w)
            row = pl.multiple_of(row, 16)
            for j in range(3):
                items.append(send(mine[k].at[others[j], pl.ds(row, r), pl.ds(col, w)], plane_in[k].at[h, j], plane_send.at[k, h, j], plane_recv.at[k, h, j], planes[j]))
        keep("plane", k, items)

    def out_near(k):
        r, w = blocks(k)
        arrived("plane", k)
        items = []
        for h, (row, col) in enumerate(places(k)):
            @pl.loop(0, r // 16)
            def _(i):
                step = pl.multiple_of(i * 16, 16)
                total = mine[k][plane, pl.ds(pl.multiple_of(row + i * 16, 16), 16), pl.ds(col, w)].astype(jnp.float32)
                for j in range(3):
                    total = total + plane_in[k][h, j, pl.ds(step, 16), :].astype(jnp.float32)
                done[k][pl.ds(pl.multiple_of(c * 4 * r + row + i * 16, 16), 16), pl.ds(col, w)] = total.astype(jnp.bfloat16)
            piece = done[k].at[pl.ds(pl.multiple_of(c * 4 * r + row, 16), r), pl.ds(col, w)]
            items.append(send(piece, piece, out_near_send.at[k, h], out_near_recv.at[k, h], (along, across)[h]))
        keep("out_near", k, items)

    def out_far(k):
        r, w = blocks(k)
        arrived("out_near", k)
        items = []
        for h, (bit, peer) in enumerate([(x, across), (y, along)]):
            piece = done[k].at[pl.ds(pl.multiple_of((c * 4 + bit * 2) * r, 16), 2 * r), pl.ds(h * w, w)]
            items.append(send(piece, piece, out_far_send.at[k, h], out_far_recv.at[k, h], peer))
        keep("out_far", k, items)

    def out_core(k):
        r, w = blocks(k)
        arrived("out_far", k)
        piece = done[k].at[pl.ds(pl.multiple_of(c * 4 * r, 16), 4 * r), :]
        keep("out_core", k, [send(piece, piece, out_core_send.at[k], out_core_recv.at[k], core)])

    final = []

    def end(k):
        arrived("out_core", k)
        copy = pltpu.make_async_copy(done[k], sums[k], final_sem.at[k])
        copy.start()
        final.append(copy)

    stages = [begin, near, far, level, out_near, out_far, out_core, end]
    for t in range(count + len(stages) - 1):
        for s in reversed(range(len(stages))):
            if 0 <= t - s < count:
                stages[s](t - s)
    for copy in sends:
        copy.wait_send()
    for copy in final:
        copy.wait()


def reduce_grads(grads, collective_id=1):
    count = len(grads)
    bf = jnp.bfloat16
    shapes = [g.shape for g in grads]
    scratch = []
    scratch += [pltpu.VMEM((4, R // 2, W), bf) for _, R, W in shapes]
    scratch += [pltpu.VMEM((4, R // 2, W), bf) for _, R, W in shapes]
    scratch += [pltpu.VMEM((2, 4, R // 4, W // 2), bf) for _, R, W in shapes]
    scratch += [pltpu.VMEM((2, 4, R // 8, W // 2), bf) for _, R, W in shapes]
    scratch += [pltpu.VMEM((2, 3, R // 8, W // 2), bf) for _, R, W in shapes]
    scratch += [pltpu.VMEM((R, W), bf) for _, R, W in shapes]
    D = pltpu.SemaphoreType.DMA
    scratch += [D((count,))] * 3 + [D((count, 2))] * 4 + [D((count, 2, 3))] * 2 + [D((count, 2))] * 4 + [D((count,))] * 3
    return pl.pallas_call(
        functools.partial(reduce_kernel, count),
        out_shape=[jax.ShapeDtypeStruct(s[1:], bf) for s in shapes],
        in_specs=[pl.BlockSpec(memory_space=pl.ANY)] * count,
        out_specs=[pl.BlockSpec(memory_space=pl.ANY)] * count,
        scratch_shapes=scratch,
        compiler_params=pltpu.CompilerParams(collective_id=collective_id, has_side_effects=True, vmem_limit_bytes=60 << 20),
        name="reduce_grads",
    )(*grads)


highest = lax.Precision.HIGHEST


def rows_structure(counts, group_rows):
    row_ends = jnp.cumsum(counts)
    starts = row_ends - counts
    row_index = jnp.arange(group_rows, dtype=jnp.int32)[:, None]
    member = (row_index >= starts[None, :]) & (row_index < row_ends[None, :])
    caption = jnp.any(row_index == starts[None, :], axis=1)
    return (member, caption)


def normalize(hidden):
    center = hidden - jnp.mean(hidden, axis=-1, keepdims=True)
    inverse = lax.rsqrt(jnp.mean(center * center, axis=-1, keepdims=True) + 1e-06)
    return (center * inverse, inverse)


def norm_back(upstream, scaled, inverse, norm_gain):
    scaled_grad = upstream * norm_gain
    return inverse * (
        scaled_grad
        - jnp.mean(scaled_grad, axis=-1, keepdims=True)
        - scaled * jnp.mean(scaled_grad * scaled, axis=-1, keepdims=True)
    )


def split_heads(values):
    return values.reshape(values.shape[0], values.shape[1], values.shape[2] // HEAD_DIM, HEAD_DIM)


def masked_scores(queries, key_rows, allowed):
    scores = jnp.einsum(
        "gqhe,gkhe->ghqk",
        split_heads(queries),
        split_heads(key_rows),
        preferred_element_type=jnp.float32,
    ) * HEAD_DIM ** (-0.5)
    return jnp.where(allowed[:, None, None, :], scores, -1000000000.0)


def attend(queries, key_rows, value_rows, allowed):
    scores = masked_scores(queries, key_rows, allowed)
    row_peak = jnp.max(scores, axis=-1, keepdims=True)
    raised = jnp.exp(scores - row_peak)
    row_total = jnp.sum(raised, axis=-1, keepdims=True)
    weights = (raised / row_total).astype(jnp.bfloat16)
    context = jnp.einsum(
        "ghqk,gkhe->gqhe", weights, split_heads(value_rows), preferred_element_type=jnp.float32
    )
    return (context.reshape(queries.shape), row_peak + jnp.log(row_total))


def attend_back(queries, key_rows, value_rows, allowed, row_lse, context_grad):
    scores = masked_scores(queries, key_rows, allowed)
    probs = jnp.exp(scores - row_lse)
    weights = probs.astype(jnp.bfloat16)
    grad_heads = split_heads(context_grad)
    prob_grad = jnp.einsum(
        "gqhe,gkhe->ghqk", grad_heads, split_heads(value_rows), preferred_element_type=jnp.float32
    )
    score_low = (probs * (prob_grad - jnp.sum(probs * prob_grad, axis=-1, keepdims=True))).astype(
        jnp.bfloat16
    )
    query_grad = jnp.einsum(
        "ghqk,gkhe->gqhe", score_low, split_heads(key_rows), preferred_element_type=jnp.float32
    ) * HEAD_DIM ** (-0.5)
    key_grad = jnp.einsum(
        "ghqk,gqhe->gkhe", score_low, split_heads(queries), preferred_element_type=jnp.float32
    ) * HEAD_DIM ** (-0.5)
    value_grad = jnp.einsum(
        "ghqk,gqhe->gkhe", weights, grad_heads, preferred_element_type=jnp.float32
    )
    return (
        query_grad.reshape(queries.shape),
        key_grad.reshape(key_rows.shape),
        value_grad.reshape(value_rows.shape),
    )

def most_images(rows, group_rows, group_images):
    best = 1
    for touched in range(2, min(rows, group_images) + 1):
        inner, outer = touched - 2, group_images - touched + 2
        if inner + 2 <= rows and group_rows - (rows - 2) <= ROWS_MAX * outer:
            best = touched
    return best


def gather_shards(shards, chunks, own):
    if own:
        return gather_weights(shards, chunks)
    return [lax.all_gather(shard, "mp", axis=0) for shard in shards]


def reduce_shards(grads, own):
    if own:
        return [total.astype(jnp.float32) for total in reduce_grads(grads)]
    return [
        lax.psum(lax.psum_scatter(grad.astype(jnp.float32), "mp", scatter_dimension=0, tiled=True)[0], "dp")
        for grad in grads
    ]


def spread(inputs, blocks):
    result = lax.dot_general(inputs, blocks, (((1,), (2,)), ((), ())), preferred_element_type=jnp.float32)
    return result.reshape(inputs.shape[0], -1)


def join(inputs, blocks):
    split = inputs.reshape(inputs.shape[0], blocks.shape[0], blocks.shape[1])
    return lax.dot_general(split, blocks, (((1, 2), (0, 1)), ((), ())), preferred_element_type=jnp.float32)


def outer(left, right, parts):
    result = lax.dot_general(left, right, (((0,), (0,)), ((), ())), preferred_element_type=jnp.float32)
    return result.astype(jnp.bfloat16).reshape(parts, left.shape[1] // parts, right.shape[1])


def per_device(
    tokens, patches, image_rows, row_lengths, box_mask, self_project, self_output, first_gain, first_shift, cross_query,
    cross_keyval, cross_output, second_gain, second_shift, expand_weight, expand_bias, shrink_weight, third_gain,
    third_shift, cotangent, *, parts, own,
):
    bf16 = jnp.bfloat16
    rows, slots, width = tokens.shape
    group_rows = row_lengths.shape[0]
    group_images, cells = patches.shape[0], patches.shape[1]
    window = most_images(rows, group_rows, group_images)
    plane = lax.axis_index("mp")

    inner = self_output.shape[0]
    small = jnp.concatenate(
        [self_project[c].T for c in range(3)] + [self_output, cross_query.T, cross_output], axis=0
    )
    keyval = jnp.concatenate([cross_keyval[0].T, cross_keyval[1].T], axis=0)
    chunks = [(0, i * 384, 384) for i in range(3)] + [(1, 0, 384)]
    chunks += [(2, i * 384, 384) for i in range(2)] + [(3, i * 384, 384) for i in range(2)]
    small, keyval, expand, shrink = gather_shards([small, keyval, expand_weight.T, shrink_weight], chunks, own)
    project = [small[:, c * inner : (c + 1) * inner] for c in range(3)]
    self_out, query_weight, cross_out = (small[:, c * inner : (c + 1) * inner] for c in range(3, 6))
    key_weight, value_weight = keyval[:, :inner], keyval[:, inner:]
    bias = lax.all_gather(expand_bias, "mp", axis=0, tiled=True)

    member, caption = rows_structure(image_rows[0], group_rows)
    member = lax.dynamic_slice_in_dim(member, plane * rows, rows, 0)
    caption = lax.dynamic_slice_in_dim(caption, plane * rows, rows, 0)
    lengths = lax.dynamic_slice_in_dim(row_lengths, plane * rows, rows, 0)
    boxes = lax.dynamic_slice_in_dim(box_mask, plane * rows, rows, 0)
    start = jnp.minimum(jnp.argmax(member[0]).astype(jnp.int32), group_images - window)
    member = lax.dynamic_slice_in_dim(member, start, window, 1)
    member_low, member_full = member.astype(bf16), member.astype(jnp.float32)
    near = lax.dynamic_slice_in_dim(patches, start, window, 0).reshape(window * cells, -1)
    key_ok = jnp.arange(slots, dtype=jnp.int32)[None, :] < lengths[:, None]
    cross_ok = caption[:, None] | (boxes > 0)

    text = tokens.reshape(rows * slots, width)
    shape = (rows, slots, width)
    queries, key_rows, value_rows = (spread(text, weight).astype(bf16).reshape(shape) for weight in project)
    self_context, self_lse = attend(queries, key_rows, value_rows, key_ok)
    self_low = self_context.astype(bf16).reshape(text.shape)
    after_self = text.astype(jnp.float32) + join(self_low, self_out)
    first_scaled, first_inverse = normalize(after_self)
    first_value = first_scaled * first_gain + first_shift
    first_low = first_value.astype(bf16)
    cross_queries = spread(first_low, query_weight).astype(bf16).reshape(shape)
    image_keys = spread(near, key_weight).astype(bf16).reshape(window, cells, width)
    image_values = spread(near, value_weight).astype(bf16).reshape(window, cells, width)
    row_keys, row_values = (
        jnp.einsum("gi,ipe->gpe", member_low, part, preferred_element_type=jnp.float32).astype(bf16)
        for part in (image_keys, image_values)
    )
    cross_context, cross_lse = attend(cross_queries, row_keys, row_values, cross_ok)
    cross_low = cross_context.astype(bf16).reshape(text.shape)
    after_cross = first_value + join(cross_low, cross_out)
    second_scaled, second_inverse = normalize(after_cross)
    second_value = second_scaled * second_gain + second_shift
    second_low = second_value.astype(bf16)
    expanded = spread(second_low, expand) + bias
    activated = jax.nn.gelu(expanded, approximate=False).astype(bf16)
    after_feed = second_value + join(activated, shrink)
    third_scaled, third_inverse = normalize(after_feed)
    joined = (third_scaled * third_gain + third_shift).astype(bf16)

    upstream = cotangent.reshape(text.shape).astype(jnp.float32)
    third_gain_grad = jnp.sum(upstream * third_scaled, axis=0)
    third_shift_grad = jnp.sum(upstream, axis=0)
    feed_grad = norm_back(upstream, third_scaled, third_inverse, third_gain)
    feed_low = feed_grad.astype(bf16)
    gelu_back = jax.vjp(lambda inner: jax.nn.gelu(inner, approximate=False), expanded)[1]
    shrink_grad = outer(activated, feed_low, parts)
    expand_low = gelu_back(spread(feed_low, shrink))[0].astype(bf16)
    expand_bias_grad = jnp.sum(expand_low.astype(jnp.float32), axis=0)
    expand_grad = outer(expand_low, second_low, parts)
    second_up = feed_grad + join(expand_low, expand)
    second_gain_grad = jnp.sum(second_up * second_scaled, axis=0)
    second_shift_grad = jnp.sum(second_up, axis=0)
    cross_grad = norm_back(second_up, second_scaled, second_inverse, second_gain)
    cross_grad_low = cross_grad.astype(bf16)
    cross_output_grad = outer(cross_low, cross_grad_low, parts)
    context_low = spread(cross_grad_low, cross_out).astype(bf16).reshape(shape)
    cross_qpart, cross_kpart, cross_vpart = attend_back(
        cross_queries, row_keys, row_values, cross_ok, cross_lse, context_low
    )
    cross_query_low = cross_qpart.astype(bf16).reshape(text.shape)
    key_low, value_low = (
        jnp.einsum("gi,gpe->ipe", member_full, part, precision=highest).astype(bf16).reshape(window * cells, width)
        for part in (cross_kpart, cross_vpart)
    )
    cross_query_grad = outer(cross_query_low, first_low, parts)
    key_weight_grad, value_weight_grad = outer(key_low, near, parts), outer(value_low, near, parts)
    patch_part = (join(key_low, key_weight) + join(value_low, value_weight)).astype(bf16)
    patch_part = patch_part.reshape(window, cells, -1)
    patch_whole = lax.dynamic_update_slice_in_dim(jnp.zeros(patches.shape, bf16), patch_part, start, 0)
    patch_grad = lax.psum_scatter(patch_whole, "mp", scatter_dimension=2, tiled=True).astype(jnp.float32)
    first_up = cross_grad + join(cross_query_low, query_weight)
    first_gain_grad = jnp.sum(first_up * first_scaled, axis=0)
    first_shift_grad = jnp.sum(first_up, axis=0)
    self_grad = norm_back(first_up, first_scaled, first_inverse, first_gain)
    self_grad_low = self_grad.astype(bf16)
    self_output_grad = outer(self_low, self_grad_low, parts)
    self_context_low = spread(self_grad_low, self_out).astype(bf16).reshape(shape)
    part_low = [
        part.astype(bf16).reshape(text.shape)
        for part in attend_back(queries, key_rows, value_rows, key_ok, self_lse, self_context_low)
    ]
    project_grads = [outer(part, text, parts) for part in part_low]
    text_grad = self_grad + sum(join(part, weight) for part, weight in zip(part_low, project))

    small_grad = jnp.concatenate(project_grads + [self_output_grad, cross_query_grad, cross_output_grad], axis=1)
    keyval_grad = jnp.concatenate([key_weight_grad, value_weight_grad], axis=1)
    small_sum, keyval_sum, expand_sum, shrink_sum = reduce_shards([small_grad, keyval_grad, expand_grad, shrink_grad], own)
    cuts = [small_sum[c * inner : (c + 1) * inner] for c in range(6)]
    vectors = lax.psum(
        jnp.concatenate(
            [
                expand_bias_grad, first_gain_grad, first_shift_grad, second_gain_grad, second_shift_grad,
                third_gain_grad, third_shift_grad,
            ]
        ),
        ("dp", "mp"),
    )
    hidden = expand_bias_grad.shape[0]
    bias_grad = lax.dynamic_slice_in_dim(vectors, plane * (hidden // parts), hidden // parts, 0)
    norms = [vectors[hidden + i * width : hidden + (i + 1) * width] for i in range(6)]
    return (
        joined.reshape(shape),
        text_grad.reshape(shape),
        patch_grad,
        jnp.stack([cut.T for cut in cuts[:3]]),
        cuts[3],
        norms[0],
        norms[1],
        cuts[4].T,
        jnp.stack([keyval_sum[:inner].T, keyval_sum[inner:].T]),
        cuts[5],
        norms[2],
        norms[3],
        expand_sum.T,
        bias_grad,
        shrink_sum,
        norms[4],
        norms[5],
    )


def solution(mesh):
    parts = mesh.shape["mp"]
    own = mesh.shape["dp"] == 8 and parts == 4
    return jax.shard_map(
        functools.partial(per_device, parts=parts, own=own),
        mesh=mesh,
        in_specs=(
            P(("dp", "mp"), None, None),
            P("dp", None, None),
            P("dp", None),
            P("dp"),
            P("dp", None),
            P(None, None, "mp"),
            P("mp", None),
            P(),
            P(),
            P(None, "mp"),
            P(None, None, "mp"),
            P("mp", None),
            P(),
            P(),
            P(None, "mp"),
            P("mp"),
            P("mp", None),
            P(),
            P(),
            P(("dp", "mp"), None, None),
        ),
        out_specs=(
            P(("dp", "mp"), None, None),
            P(("dp", "mp"), None, None),
            P("dp", None, "mp"),
            P(None, None, "mp"),
            P("mp", None),
            P(),
            P(),
            P(None, "mp"),
            P(None, None, "mp"),
            P("mp", None),
            P(),
            P(),
            P(None, "mp"),
            P("mp"),
            P("mp", None),
            P(),
            P(),
        ),
        check_vma=False,
    )
```

```python
import functools

import jax
import jax.numpy as jnp
from jax import lax
from jax.experimental import pallas as pl
from jax.experimental.pallas import tpu as pltpu
from jax.sharding import PartitionSpec as P

HEAD_DIM = 64
ROWS_MAX = 7
MESH = pl.DeviceIdType.MESH


def place():
    index = lax.axis_index("dp")
    plane = lax.axis_index("mp")
    y, x, c = index // 4, (index // 2) % 2, index % 2
    return index, plane, y, x, c


def partners(index, plane):
    core = (index + 1 - 2 * (index % 2), plane)
    across = (index + 2 - 4 * ((index // 2) % 2), plane)
    along = (index + 4 - 8 * (index // 4), plane)
    planes = [(index, lax.rem(plane + step, 4)) for step in (1, 2, 3)]
    return core, across, along, planes


def greet(peers):
    barrier = pltpu.get_barrier_semaphore()
    for peer in peers:
        pl.semaphore_signal(barrier, inc=1, device_id=peer, device_id_type=MESH)
    pl.semaphore_wait(barrier, len(peers))


class Sends:
    def __init__(self):
        self.stages, self.all = {}, []

    def start(self, name, k, items):
        copies = []
        for source, target, sends, recvs, peer in items:
            copy = pltpu.make_async_remote_copy(
                src_ref=source, dst_ref=target, send_sem=sends, recv_sem=recvs, device_id=peer, device_id_type=MESH
            )
            copy.start()
            copies.append(copy)
        self.stages[name, k] = copies
        self.all.extend(copies)

    def arrived(self, name, k):
        for copy in self.stages[name, k]:
            copy.wait_recv()

    def close(self):
        for copy in self.all:
            copy.wait_send()


class Gather:
    stages = 4

    def __init__(self, chunks, shards, wholes, sems, window):
        self.chunks, self.shards, self.wholes, self.window = chunks, shards, wholes, window
        self.sems = sems
        self.index, self.plane, self.y, self.x, self.c = place()
        self.core, self.across, self.along, self.planes = partners(self.index, self.plane)
        self.others = [lax.rem(self.plane + step, 4) for step in (1, 2, 3)]
        self.sends = Sends()

    def sizes(self, k):
        which, base, rows = self.chunks[k]
        return which, base, rows // 8, self.shards[which].shape[1] // 2

    def level(self, k):
        which, base, r, w = self.sizes(k)
        _, _, send, recv = self.sems[:4]
        items = []
        for h, first in enumerate((self.x * 2 + self.y, self.y * 2 + self.x)):
            here = (pl.ds(pl.multiple_of(base + (self.c * 4 + first) * r, 16), r), pl.ds(h * w, w))
            for j, peer in enumerate(self.planes):
                target = self.wholes[which].at[(self.plane,) + here]
                items.append((self.shards[which].at[here], target, send.at[k, h, j], recv.at[k, h, j], peer))
        self.sends.start("level", k, items)

    def near(self, k):
        which, base, r, w = self.sizes(k)
        send, recv = self.sems[4:6]
        self.sends.arrived("level", k)
        if k + self.window < len(self.chunks):
            self.level(k + self.window)
        items = []
        for h, first in enumerate((self.x * 2 + self.y, self.y * 2 + self.x)):
            row = pl.multiple_of(base + (self.c * 4 + first) * r, 16)
            for j, other in enumerate(self.others):
                piece = self.wholes[which].at[other, pl.ds(row, r), pl.ds(h * w, w)]
                items.append((piece, piece, send.at[k, h, j], recv.at[k, h, j], (self.along, self.across)[h]))
        self.sends.start("near", k, items)

    def far(self, k):
        which, base, r, w = self.sizes(k)
        send, recv = self.sems[6:8]
        self.sends.arrived("near", k)
        items = []
        for h, first in enumerate((self.x, self.y)):
            row = pl.multiple_of(base + (self.c * 4 + first * 2) * r, 16)
            for j, other in enumerate(self.others):
                piece = self.wholes[which].at[other, pl.ds(row, 2 * r), pl.ds(h * w, w)]
                items.append((piece, piece, send.at[k, h, j], recv.at[k, h, j], (self.across, self.along)[h]))
        self.sends.start("far", k, items)

    def cross(self, k):
        which, base, r, w = self.sizes(k)
        send, recv = self.sems[8:10]
        self.sends.arrived("far", k)
        row = pl.multiple_of(base + self.c * 4 * r, 16)
        items = []
        for j, other in enumerate(self.others):
            piece = self.wholes[which].at[other, pl.ds(row, 4 * r), :]
            items.append((piece, piece, send.at[k, j], recv.at[k, j], self.core))
        self.sends.start("core", k, items)

    def begin(self):
        greet([self.core, self.across, self.along] + self.planes)
        for k in range(self.window):
            self.level(k)
        local_sem = self.sems[0]
        self.local = []
        for which, shard in enumerate(self.shards):
            copy = pltpu.make_async_copy(shard, self.wholes[which].at[self.plane], local_sem.at[which])
            copy.start()
            self.local.append(copy)

    def step(self, t):
        if 0 <= t - 4 < len(self.chunks):
            self.cross(t - 4)
        if 0 <= t - 2 < len(self.chunks):
            self.far(t - 2)
        if 0 <= t < len(self.chunks):
            self.near(t)

    @property
    def steps(self):
        return len(self.chunks) + 4

    def ready(self, k):
        self.sends.arrived("core", k)

    @staticmethod
    def scratch(count, total):
        dma = pltpu.SemaphoreType.DMA
        return [dma((count,)), dma((count,))] + [dma((total, 2, 3))] * 6 + [dma((total, 3))] * 2


def gather_kernel(chunks, count, *refs):
    shards, bias, outs, biases = refs[:count], refs[count], refs[count + 1 : 2 * count + 1], refs[2 * count + 1]
    rest = refs[2 * count + 2 :]
    wholes, bias_send, bias_recv, sems = rest[:count], rest[count], rest[count + 1], rest[count + 2 :]
    gather = Gather(chunks, shards, wholes, sems, 3)
    gather.begin()
    gather.sends.start(
        "bias", 0, [(bias, biases.at[gather.plane], bias_send.at[j], bias_recv.at[j], peer) for j, peer in enumerate(gather.planes)]
    )
    biases[gather.plane] = bias[...]
    final = []
    for t in range(gather.steps + 2):
        if 0 <= t - 6 < len(chunks):
            gather.ready(t - 6)
            which = chunks[t - 6][0]
            if t - 5 == len(chunks) or chunks[t - 5][0] != which:
                gather.local[which].wait()
                copy = pltpu.make_async_copy(wholes[which], outs[which], sems[1].at[which])
                copy.start()
                final.append(copy)
        gather.step(t)
    gather.sends.arrived("bias", 0)
    gather.sends.close()
    for copy in final:
        copy.wait()


def gather_weights(shards, bias, chunks):
    count, dma = len(shards), pltpu.SemaphoreType.DMA
    any_space, vmem = pl.BlockSpec(memory_space=pl.ANY), pl.BlockSpec(memory_space=pltpu.VMEM)
    *wholes, biases = pl.pallas_call(
        functools.partial(gather_kernel, chunks, count),
        out_shape=[jax.ShapeDtypeStruct((4,) + s.shape, s.dtype) for s in shards + [bias]],
        in_specs=[any_space] * count + [vmem],
        out_specs=[any_space] * count + [vmem],
        scratch_shapes=[pltpu.VMEM((4,) + s.shape, s.dtype) for s in shards]
        + [dma((3,)), dma((3,))]
        + Gather.scratch(count, len(chunks)),
        compiler_params=pltpu.CompilerParams(collective_id=0, has_side_effects=True, vmem_limit_bytes=62 << 20),
        name="gather_weights",
    )(*shards, bias)
    return wholes, biases


class Reduce:
    def __init__(self, chunks, grads, sums, buffers, sems):
        self.chunks, self.grads, self.sums, self.sems = chunks, grads, sums, sems
        total = len(chunks)
        self.mine, self.core_in, self.near_in, self.far_in, self.plane_in, self.done = (
            buffers[i * total : (i + 1) * total] for i in range(6)
        )
        self.index, self.plane, self.y, self.x, self.c = place()
        self.core, self.across, self.along, self.planes = partners(self.index, self.plane)
        self.others = [lax.rem(self.plane + step, 4) for step in (1, 2, 3)]
        self.sends = Sends()
        self.local, self.final = {}, []
        self.order = [self.begin, self.near, self.far, self.level, self.out_near, self.out_far, self.out_core, self.end]

    @staticmethod
    def scratch(sizes):
        low, dma, total = jnp.bfloat16, pltpu.SemaphoreType.DMA, len(sizes)
        shapes = [[(4, r // 2, w) for r, w in sizes]] * 2
        shapes += [[(2, 4, r // 4, w // 2) for r, w in sizes], [(2, 4, r // 8, w // 2) for r, w in sizes]]
        shapes += [[(2, 3, r // 8, w // 2) for r, w in sizes], [(r, w) for r, w in sizes]]
        buffers = [pltpu.VMEM(shape, low) for group in shapes for shape in group]
        sems = [dma((total,))] * 4 + [dma((total, 2))] * 8 + [dma((total, 2, 3))] * 2 + [dma((total,))] * 2
        return buffers, sems

    def sizes(self, k):
        which, base, rows = self.chunks[k]
        return which, base, rows // 8, self.grads[which].shape[2] // 2

    @staticmethod
    def add(total, total_row, total_col, part, part_col, rows, cols):
        @pl.loop(0, rows // 16)
        def _(i):
            for shard in range(4):
                here = (shard, pl.ds(pl.multiple_of(total_row + i * 16, 16), 16), pl.ds(total_col, cols))
                there = (shard, pl.ds(pl.multiple_of(i * 16, 16), 16), pl.ds(part_col, cols))
                total[here] = (total[here].astype(jnp.float32) + part[there].astype(jnp.float32)).astype(jnp.bfloat16)

    def places(self, r, w):
        return [((self.x * 2 + self.y) * r, 0), ((self.y * 2 + self.x) * r, w)]

    def begin(self, k):
        which, base, r, w = self.sizes(k)
        theirs = pl.multiple_of(base + (1 - self.c) * 4 * r, 16)
        ours = pl.multiple_of(base + self.c * 4 * r, 16)
        source = self.grads[which].at[:, pl.ds(theirs, 4 * r), :]
        self.sends.start("core", k, [(source, self.core_in[k], self.sems[0].at[k], self.sems[1].at[k], self.core)])
        self.local[k] = pltpu.make_async_copy(
            self.grads[which].at[:, pl.ds(ours, 4 * r), :], self.mine[k], self.sems[2].at[k]
        )
        self.local[k].start()

    def near(self, k):
        which, base, r, w = self.sizes(k)
        self.local[k].wait()
        self.sends.arrived("core", k)
        self.add(self.mine[k], 0, 0, self.core_in[k], 0, 4 * r, 2 * w)
        items = []
        for h, (bit, peer) in enumerate([(self.x, self.across), (self.y, self.along)]):
            row = pl.multiple_of((1 - bit) * 2 * r, 16)
            source = self.mine[k].at[:, pl.ds(row, 2 * r), pl.ds(h * w, w)]
            items.append((source, self.near_in[k].at[h], self.sems[4].at[k, h], self.sems[5].at[k, h], peer))
        self.sends.start("near", k, items)

    def far(self, k):
        which, base, r, w = self.sizes(k)
        self.sends.arrived("near", k)
        items = []
        for h, (bit, second, peer) in enumerate([(self.x, self.y, self.along), (self.y, self.x, self.across)]):
            row = bit * 2 * r
            self.add(self.mine[k], row, h * w, self.near_in[k].at[h], 0, 2 * r, w)
            row = pl.multiple_of(row + (1 - second) * r, 16)
            source = self.mine[k].at[:, pl.ds(row, r), pl.ds(h * w, w)]
            items.append((source, self.far_in[k].at[h], self.sems[6].at[k, h], self.sems[7].at[k, h], peer))
        self.sends.start("far", k, items)

    def level(self, k):
        which, base, r, w = self.sizes(k)
        self.sends.arrived("far", k)
        items = []
        for h, (row, col) in enumerate(self.places(r, w)):
            self.add(self.mine[k], row, col, self.far_in[k].at[h], 0, r, w)
            row = pl.multiple_of(row, 16)
            for j in range(3):
                source = self.mine[k].at[self.others[j], pl.ds(row, r), pl.ds(col, w)]
                items.append(
                    (source, self.plane_in[k].at[h, j], self.sems[12].at[k, h, j], self.sems[13].at[k, h, j], self.planes[j])
                )
        self.sends.start("level", k, items)

    def out_near(self, k):
        which, base, r, w = self.sizes(k)
        self.sends.arrived("level", k)
        items = []
        for h, (row, col) in enumerate(self.places(r, w)):

            @pl.loop(0, r // 16)
            def _(i):
                step = pl.ds(pl.multiple_of(i * 16, 16), 16)
                here = pl.ds(pl.multiple_of(row + i * 16, 16), 16)
                total = self.mine[k][self.plane, here, pl.ds(col, w)].astype(jnp.float32)
                for j in range(3):
                    total = total + self.plane_in[k][h, j, step, :].astype(jnp.float32)
                here = pl.ds(pl.multiple_of(self.c * 4 * r + row + i * 16, 16), 16)
                self.done[k][here, pl.ds(col, w)] = total.astype(jnp.bfloat16)

            piece = self.done[k].at[pl.ds(pl.multiple_of(self.c * 4 * r + row, 16), r), pl.ds(col, w)]
            peer = (self.along, self.across)[h]
            items.append((piece, piece, self.sems[8].at[k, h], self.sems[9].at[k, h], peer))
        self.sends.start("out_near", k, items)

    def out_far(self, k):
        which, base, r, w = self.sizes(k)
        self.sends.arrived("out_near", k)
        items = []
        for h, (bit, peer) in enumerate([(self.x, self.across), (self.y, self.along)]):
            row = pl.multiple_of((self.c * 4 + bit * 2) * r, 16)
            piece = self.done[k].at[pl.ds(row, 2 * r), pl.ds(h * w, w)]
            items.append((piece, piece, self.sems[10].at[k, h], self.sems[11].at[k, h], peer))
        self.sends.start("out_far", k, items)

    def out_core(self, k):
        which, base, r, w = self.sizes(k)
        self.sends.arrived("out_far", k)
        piece = self.done[k].at[pl.ds(pl.multiple_of(self.c * 4 * r, 16), 4 * r), :]
        self.sends.start("out_core", k, [(piece, piece, self.sems[14].at[k], self.sems[15].at[k], self.core)])

    def end(self, k):
        which, base, r, w = self.sizes(k)
        self.sends.arrived("out_core", k)
        copy = pltpu.make_async_copy(self.done[k], self.sums[which].at[pl.ds(base, 8 * r), :], self.sems[3].at[k])
        copy.start()
        self.final.append(copy)

    @property
    def steps(self):
        return len(self.chunks) + len(self.order) - 1

    def step(self, t):
        for s in reversed(range(len(self.order))):
            if 0 <= t - s < len(self.chunks):
                self.order[s](t - s)

    def close(self):
        self.sends.close()
        for copy in self.final:
            copy.wait()


def reduce_kernel(chunks, count, *refs):
    grads, patch, vectors = refs[:count], refs[count], refs[count + 1]
    sums, windows, vector_sum = refs[count + 2 : 2 * count + 2], refs[2 * count + 2], refs[2 * count + 3]
    rest = refs[2 * count + 4 :]
    total = 6 * len(chunks)
    buffers, sems = rest[:total], rest[total : total + 16]
    vector_in, patch_send, patch_recv, vector_send, vector_recv, patch_local = rest[total + 16 :]
    reduce = Reduce(chunks, grads, sums, buffers, sems)
    greet([reduce.core, reduce.across, reduce.along] + reduce.planes)
    reduce.sends.start(
        "patch",
        0,
        [
            (patch.at[other], windows.at[reduce.plane], patch_send.at[j], patch_recv.at[j], peer)
            for j, (other, peer) in enumerate(zip(reduce.others, reduce.planes))
        ],
    )
    copy = pltpu.make_async_copy(patch.at[reduce.plane], windows.at[reduce.plane], patch_local)
    copy.start()
    vector_sum[0] = vectors[...]
    for t in range(reduce.steps):
        if t < 3:
            peer = (reduce.core, reduce.across, reduce.along)[t]
            reduce.sends.start("vector", t, [(vector_sum.at[t], vector_in.at[t], vector_send.at[t], vector_recv.at[t], peer)])
        if t == 3:
            reduce.sends.start(
                "vector",
                t,
                [
                    (vector_sum.at[3], vector_in.at[3 + j], vector_send.at[3 + j], vector_recv.at[3 + j], peer)
                    for j, peer in enumerate(reduce.planes)
                ],
            )
        reduce.step(t)
        if t < 3:
            reduce.sends.arrived("vector", t)
            vector_sum[t + 1] = vector_sum[t] + vector_in[t]
        if t == 3:
            reduce.sends.arrived("vector", t)
            vector_sum[4] = vector_sum[3] + ((vector_in[3] + vector_in[4]) + vector_in[5])
    reduce.sends.arrived("patch", 0)
    reduce.close()
    copy.wait()


def reduce_grads(grads, patch, vectors, chunks):
    count, dma = len(grads), pltpu.SemaphoreType.DMA
    any_space, vmem = pl.BlockSpec(memory_space=pl.ANY), pl.BlockSpec(memory_space=pltpu.VMEM)
    buffers, sems = Reduce.scratch([(rows, grads[which].shape[2]) for which, _, rows in chunks])
    *sums, windows, vector_sum = pl.pallas_call(
        functools.partial(reduce_kernel, chunks, count),
        out_shape=[jax.ShapeDtypeStruct(g.shape[1:], g.dtype) for g in grads]
        + [jax.ShapeDtypeStruct(patch.shape, patch.dtype), jax.ShapeDtypeStruct((5,) + vectors.shape, vectors.dtype)],
        in_specs=[any_space] * (count + 1) + [vmem],
        out_specs=[any_space] * (count + 1) + [vmem],
        scratch_shapes=buffers
        + sems
        + [pltpu.VMEM((6,) + vectors.shape, vectors.dtype), dma((3,)), dma((3,)), dma((6,)), dma((6,)), dma(())],
        compiler_params=pltpu.CompilerParams(collective_id=1, has_side_effects=True, vmem_limit_bytes=62 << 20),
        name="reduce_grads",
    )(*grads, patch, vectors)
    return sums, windows, vector_sum[4]


def nn(left, right):
    return lax.dot_general(left, right, (((1,), (0,)), ((), ())), preferred_element_type=jnp.float32)


def nt(left, right):
    return lax.dot_general(left, right, (((1,), (1,)), ((), ())), preferred_element_type=jnp.float32)


def tn(left, right):
    return lax.dot_general(left, right, (((0,), (0,)), ((), ())), preferred_element_type=jnp.float32)


def part(ref, which):
    inner = ref.shape[2] // 4 if ref.shape[2] == 768 else 192
    return jnp.concatenate([ref[m, which * 192 : (which + 1) * 192, :] for m in range(4)], axis=0)


def store_part(ref, which, value):
    low = value.astype(jnp.bfloat16)
    for m in range(4):
        ref[m, which * 192 : (which + 1) * 192, :] = low[m * 192 : (m + 1) * 192]


def tiles(amount, step):
    def wrap(body):
        @pl.loop(0, amount // step)
        def _(i):
            body(pl.ds(pl.multiple_of(i * step, step), step))

    return wrap


def lanes():
    place = lax.broadcasted_iota(jnp.int32, (1, 2 * HEAD_DIM), 1)
    low = place < HEAD_DIM
    return low, low.astype(jnp.float32), 1.0 - low.astype(jnp.float32)


def norm_forward(total, unit, inverse, value, value_low, gain, shift):
    @tiles(total.shape[0], 80)
    def _(rows):
        hidden = total[rows, :]
        center = hidden - jnp.mean(hidden, axis=-1, keepdims=True)
        factor = lax.rsqrt(jnp.mean(center * center, axis=-1, keepdims=True) + 1e-06)
        scaled = center * factor
        result = scaled * gain[...] + shift[...]
        if unit is not None:
            unit[rows, :] = scaled
            inverse[rows, :] = jnp.broadcast_to(factor, (80, 128))
        if value is not None:
            value[rows, :] = result
        value_low[rows, :] = result.astype(jnp.bfloat16)


def norm_reverse(upstream, unit, inverse, gain, gain_grad, shift_grad, grad, grad_low):
    gain_grad[...] = jnp.zeros_like(gain_grad)
    shift_grad[...] = jnp.zeros_like(shift_grad)

    @tiles(upstream.shape[0], 80)
    def _(rows):
        up = upstream[rows, :].astype(jnp.float32)
        scaled = unit[rows, :]
        factor = inverse[rows, :][:, :1]
        gain_grad[...] += jnp.sum(up * scaled, axis=0, keepdims=True)
        shift_grad[...] += jnp.sum(up, axis=0, keepdims=True)
        inner = up * gain[...]
        result = factor * (
            inner
            - jnp.mean(inner, axis=-1, keepdims=True)
            - scaled * jnp.mean(inner * scaled, axis=-1, keepdims=True)
        )
        grad[rows, :] = result
        grad_low[rows, :] = result.astype(jnp.bfloat16)


def softmax(scores):
    raised = jnp.exp(scores - jnp.max(scores, axis=-1, keepdims=True))
    return (raised * (1.0 / jnp.sum(raised, axis=-1, keepdims=True))).astype(jnp.bfloat16)


def attend_self(queries, keys, values, pair_ok, probs, context):
    low, first, second = lanes()
    first_low, second_low = first.astype(jnp.bfloat16), second.astype(jnp.bfloat16)

    @pl.loop(0, pair_ok.shape[0])
    def _(pair):
        rows = pl.ds(pl.multiple_of(pair * 80, 80), 80)
        allowed = pair_ok[pair] > 0
        allowed = jnp.concatenate([allowed, allowed], axis=0)
        for tile in range(6):
            cols = slice(tile * 128, (tile + 1) * 128)
            query = queries[rows, cols]
            both = jnp.concatenate([query * first_low, query * second_low], axis=0)
            scores = jnp.where(allowed, nt(both, keys[rows, cols]) * HEAD_DIM ** (-0.5), -1000000000.0)
            weights = softmax(scores)
            probs[pair, tile] = weights
            mixed = nn(weights, values[rows, cols])
            context[rows, cols] = jnp.where(low, mixed[:80], mixed[80:]).astype(jnp.bfloat16)


def attend_cross(image, wide, keys, values, cell_ok, probs):
    low, first, second = lanes()

    @pl.loop(0, cell_ok.shape[0])
    def _(row):
        rows = pl.ds(pl.multiple_of(row * 40, 40), 40)
        which = image[row]
        allowed = jnp.broadcast_to(cell_ok[pl.ds(row, 1), :], (80, cell_ok.shape[1])) > 0
        for tile in range(6):
            cols = slice(tile * 128, (tile + 1) * 128)
            query = wide[rows, cols]
            both = jnp.concatenate([query * first, query * second], axis=0).astype(jnp.bfloat16)
            scores = jnp.where(allowed, nt(both, keys[which, :, cols]) * HEAD_DIM ** (-0.5), -1000000000.0)
            weights = softmax(scores)
            probs[row, tile] = weights
            mixed = nn(weights, values[which, :, cols])
            wide[rows, cols] = jnp.where(low, mixed[:40], mixed[40:])


def forward_kernel(
    image, tokens, near, pair_ok, cell_ok, self_weights, cross_weights, keyval, first_gain, first_shift, second_gain,
    second_shift,
    queries, keys, values, self_probs, self_context, first_unit, first_inverse, first_low, cross_queries, image_keys,
    image_values, cross_probs, cross_context, second_unit, second_inverse, second_value, second_low,
    total, first_value, wide,
):
    bf16 = jnp.bfloat16
    for target, which in ((queries, 0), (keys, 1), (values, 2)):
        target[...] = nt(tokens[...], part(self_weights, which)).astype(bf16)
    attend_self(queries, keys, values, pair_ok, self_probs, self_context)
    total[...] = nn(self_context[...], part(self_weights, 3)) + tokens[...].astype(jnp.float32)
    norm_forward(total, first_unit, first_inverse, first_value, first_low, first_gain, first_shift)
    cross_queries[...] = nt(first_low[...], part(cross_weights, 0)).astype(bf16)
    wide[...] = cross_queries[...].astype(jnp.float32)
    images, cells, depth = near.shape
    half = images // 2
    for target, which in ((image_keys, 0), (image_values, 1)):
        weight = part(keyval, which)
        for step in range(2):
            block = near[step * half : (step + 1) * half].reshape(half * cells, depth)
            target[step * half : (step + 1) * half] = nt(block, weight).astype(bf16).reshape(half, cells, -1)
    attend_cross(image, wide, image_keys, image_values, cell_ok, cross_probs)
    cross_context[...] = wide[...].astype(bf16)
    total[...] = nn(cross_context[...], part(cross_weights, 1)) + first_value[...]
    norm_forward(total, second_unit, second_inverse, second_value, second_low, second_gain, second_shift)


def feed_kernel(
    second_value, second_low, expand, shrink, bias, gain, shift, cotangent,
    joined, expand_grad, shrink_grad, bias_grad, gain_grad, shift_grad, second_up,
    active, slope, wide, unit, inverse, feed_low,
):
    bf16 = jnp.bfloat16
    second_up[...] = second_value[...]

    @pl.loop(0, 4)
    def _(m):
        wide[...] = nt(second_low[...], expand[m])

        @tiles(wide.shape[0], 40)
        def _(rows):
            inner = wide[rows, :] + bias[pl.ds(m, 1), :]
            share = 0.5 * (1.0 + lax.erf(inner * 0.5**0.5))
            wide[rows, :] = inner * share
            unit[rows, :] = share + inner * (jnp.exp(-0.5 * inner * inner) * 0.3989422804014327)

        active[m] = wide[...].astype(bf16)
        slope[m] = unit[...].astype(bf16)
        second_up[...] += nn(active[m], shrink[m])

    norm_forward(second_up, unit, inverse, None, joined, gain, shift)
    norm_reverse(cotangent, unit, inverse, gain, gain_grad, shift_grad, second_up, feed_low)

    @pl.loop(0, 4)
    def _(m):
        shrink_grad[m] = tn(active[m], feed_low[...]).astype(bf16)
        wide[...] = nt(feed_low[...], shrink[m])
        bias_grad[pl.ds(m, 1), :] = jnp.zeros((1, 768), jnp.float32)

        @tiles(wide.shape[0], 80)
        def _(rows):
            low = (wide[rows, :] * slope[m, rows, :].astype(jnp.float32)).astype(bf16)
            active[m, rows, :] = low
            bias_grad[pl.ds(m, 1), :] += jnp.sum(low.astype(jnp.float32), axis=0, keepdims=True)

        expand_grad[m] = tn(active[m], second_low[...]).astype(bf16)
        second_up[...] += nn(active[m], expand[m])


def cross_back_kernel(
    image, near, cross_weights, keyval, cross_queries, image_keys, image_values, cross_probs, cross_context, second_up,
    second_unit, second_inverse, second_gain, first_low,
    weights_grad, keyval_grad, patch_part, gain_grad, shift_grad, first_up,
    grad_low, wide, turn, key_sum, value_sum, query_low,
):
    bf16 = jnp.bfloat16
    low, first, second = lanes()
    norm_reverse(second_up, second_unit, second_inverse, second_gain, gain_grad, shift_grad, first_up, grad_low)
    store_part(weights_grad, 1, tn(cross_context[...], grad_low[...]))
    wide[...] = nt(grad_low[...], part(cross_weights, 1)).astype(bf16).astype(jnp.float32)
    turn[...] = cross_queries[...].astype(jnp.float32)
    key_sum[...] = jnp.zeros_like(key_sum)
    value_sum[...] = jnp.zeros_like(value_sum)

    @pl.loop(0, cross_probs.shape[0])
    def _(row):
        rows = pl.ds(pl.multiple_of(row * 40, 40), 40)
        which = image[row]
        for tile in range(6):
            cols = slice(tile * 128, (tile + 1) * 128)
            query, grad = turn[rows, cols], wide[rows, cols]
            queries = jnp.concatenate([query * first, query * second], axis=0).astype(bf16)
            grads = jnp.concatenate([grad * first, grad * second], axis=0).astype(bf16)
            weights = cross_probs[row, tile]
            probs = weights.astype(jnp.float32)
            upstream = nt(grads, image_values[which, :, cols])
            back = (probs * (upstream - jnp.sum(probs * upstream, axis=-1, keepdims=True))).astype(bf16)
            mixed = nn(back, image_keys[which, :, cols])
            turn[rows, cols] = jnp.where(low, mixed[:40], mixed[40:]) * HEAD_DIM ** (-0.5)
            key_sum[which, :, cols] += tn(back, queries) * HEAD_DIM ** (-0.5)
            value_sum[which, :, cols] += tn(weights, grads)

    query_low[...] = turn[...].astype(bf16)
    store_part(weights_grad, 0, tn(query_low[...], first_low[...]))
    first_up[...] += nn(query_low[...], part(cross_weights, 0))
    images, cells, depth = near.shape
    amount = images * cells
    for source, which in ((key_sum, 0), (value_sum, 1)):
        flat = source[...].astype(bf16).reshape(amount, -1)
        store_part(keyval_grad, which, tn(flat, near[...].reshape(amount, depth)))
    for step in range(2):
        here = slice(step * (images // 2), (step + 1) * (images // 2))
        block = nn(key_sum[here].astype(bf16).reshape(amount // 2, -1), part(keyval, 0))
        block += nn(value_sum[here].astype(bf16).reshape(amount // 2, -1), part(keyval, 1))
        block = block.astype(bf16)
        for m in range(4):
            patch_part[m, here] = block[:, m * 256 : (m + 1) * 256].reshape(images // 2, cells, 256)


def self_back_kernel(
    tokens, self_weights, queries, keys, values, self_probs, self_context, first_up, first_unit, first_inverse,
    first_gain,
    weights_grad, gain_grad, shift_grad, text_grad,
    grad_low, context_low, query_low, key_low, value_low,
):
    bf16 = jnp.bfloat16
    low, first, second = lanes()
    first_mask, second_mask = first.astype(bf16), second.astype(bf16)
    norm_reverse(first_up, first_unit, first_inverse, first_gain, gain_grad, shift_grad, text_grad, grad_low)
    store_part(weights_grad, 3, tn(self_context[...], grad_low[...]))
    context_low[...] = nt(grad_low[...], part(self_weights, 3)).astype(bf16)

    @pl.loop(0, self_probs.shape[0])
    def _(pair):
        rows = pl.ds(pl.multiple_of(pair * 80, 80), 80)
        for tile in range(6):
            cols = slice(tile * 128, (tile + 1) * 128)
            query, grad = queries[rows, cols], context_low[rows, cols]
            both = jnp.concatenate([query * first_mask, query * second_mask], axis=0)
            grads = jnp.concatenate([grad * first_mask, grad * second_mask], axis=0)
            weights = self_probs[pair, tile]
            probs = weights.astype(jnp.float32)
            upstream = nt(grads, values[rows, cols])
            back = (probs * (upstream - jnp.sum(probs * upstream, axis=-1, keepdims=True))).astype(bf16)
            mixed = nn(back, keys[rows, cols])
            query_low[rows, cols] = (jnp.where(low, mixed[:80], mixed[80:]) * HEAD_DIM ** (-0.5)).astype(bf16)
            key_low[rows, cols] = (tn(back, both) * HEAD_DIM ** (-0.5)).astype(bf16)
            value_low[rows, cols] = tn(weights, grads).astype(bf16)

    for source, which in ((query_low, 0), (key_low, 1), (value_low, 2)):
        store_part(weights_grad, which, tn(source[...], tokens[...]))
        text_grad[...] += nn(source[...], part(self_weights, which))


def place_kernel(starts, windows, result):
    cells = result.shape[1]
    result[...] = jnp.zeros_like(result)
    for m in range(windows.shape[0]):

        @pl.loop(0, windows.shape[1])
        def _(i):
            result[starts[m] + i] += windows[m, i, :cells, :].astype(jnp.float32)


def on_core(kernel, name, inputs, outputs, scratch, scalars=0):
    vmem, smem = pl.BlockSpec(memory_space=pltpu.VMEM), pl.BlockSpec(memory_space=pltpu.SMEM)
    return pl.pallas_call(
        kernel,
        out_shape=[jax.ShapeDtypeStruct(shape, kind) for shape, kind in outputs],
        in_specs=[smem] * scalars + [vmem] * (len(inputs) - scalars),
        out_specs=[vmem] * len(outputs),
        scratch_shapes=[pltpu.VMEM(shape, kind) for shape, kind in scratch],
        compiler_params=pltpu.CompilerParams(vmem_limit_bytes=62 << 20),
        name=name,
    )(*inputs)


def image_windows(parts, rows, group_images):
    group_rows = parts * rows
    first = [m * rows // ROWS_MAX for m in range(parts)]
    last = [group_images - 1 - max(0, -(-(group_rows - (m + 1) * rows - (ROWS_MAX - 1)) // ROWS_MAX)) for m in range(parts)]
    last = [min(stop, (m + 1) * rows - 1) for m, stop in enumerate(last)]
    window = max(stop - start + 1 for start, stop in zip(first, last))
    return [min(start, group_images - window) for start in first], window


def gather_shards(shards, bias, chunks, own):
    if own:
        return gather_weights(shards, bias, chunks)
    return [lax.all_gather(shard, "mp", axis=0) for shard in shards], lax.all_gather(bias, "mp", axis=0)


def reduce_shards(grads, patch, vectors, chunks, own):
    if own:
        return reduce_grads(grads, patch, vectors, chunks)
    sums = [
        lax.psum(lax.psum_scatter(grad.astype(jnp.float32), "mp", scatter_dimension=0, tiled=True)[0], "dp")
        for grad in grads
    ]
    windows = lax.all_to_all(patch, "mp", split_axis=0, concat_axis=0, tiled=True)
    return sums, windows, lax.psum(vectors, ("dp", "mp"))


def per_device(
    tokens, patches, image_rows, row_lengths, box_mask, self_project, self_output, first_gain, first_shift, cross_query,
    cross_keyval, cross_output, second_gain, second_shift, expand_weight, expand_bias, shrink_weight, third_gain,
    third_shift, cotangent, *, parts, own,
):
    bf16, f32 = jnp.bfloat16, jnp.float32
    rows, slots, width = tokens.shape
    group_images, cells, depth = patches.shape
    starts, window = image_windows(parts, rows, group_images)
    padded = -(-cells // 16) * 16
    plane = lax.axis_index("mp")
    start = jnp.asarray(starts, jnp.int32)[plane]
    amount, pairs, tiles_of = rows * slots, rows // 2, width // 128

    inner, hidden = self_output.shape[0], expand_bias.shape[0]
    shards = [
        jnp.concatenate([self_project[0].T, self_project[1].T, self_project[2].T, self_output], axis=0),
        jnp.concatenate([cross_query.T, cross_output], axis=0),
        jnp.concatenate([cross_keyval[0].T, cross_keyval[1].T], axis=0),
        expand_weight.T,
        shrink_weight,
    ]
    chunks = [(0, 0, 384), (0, 384, 384), (1, 0, 384), (2, 0, 384), (3, 0, 384), (3, 384, 384), (4, 0, 384), (4, 384, 384)]
    bias_rows = jnp.pad(expand_bias.reshape(hidden // 128, 128), ((0, -(hidden // 128) % 8), (0, 0)))
    (self_weights, cross_weights, keyval, expand, shrink), biases = gather_shards(shards, bias_rows, chunks, own)
    bias = biases[:, : hidden // 128].reshape(parts, hidden)

    counts = image_rows[0]
    ends = jnp.cumsum(counts)
    row_index = plane * rows + jnp.arange(rows, dtype=jnp.int32)
    owner = jnp.sum(row_index[:, None] >= ends[None, :], axis=1).astype(jnp.int32)
    caption = jnp.any(row_index[:, None] == (ends - counts)[None, :], axis=1)
    lengths = lax.dynamic_slice_in_dim(row_lengths, plane * rows, rows, 0)
    boxes = lax.dynamic_slice_in_dim(box_mask, plane * rows, rows, 0)
    cell_ok = jnp.pad((caption[:, None] | (boxes > 0)).astype(f32), ((0, 0), (0, padded - cells)))
    slot = jnp.arange(2 * slots, dtype=jnp.int32)
    key_ok = (slot % slots)[None, :] < jnp.repeat(lengths.reshape(pairs, 2), slots, axis=1)
    pair_ok = (key_ok[:, None, :] & ((slot // slots)[:, None] == (slot // slots)[None, :])[None]).astype(f32)
    near = lax.dynamic_slice_in_dim(patches, start, window, 0)
    near = jnp.pad(near, ((0, 0), (0, padded - cells), (0, 0)))
    image = owner - start

    text = tokens.reshape(amount, width)
    row = lambda vector: vector.reshape(1, width)
    flat, unit_row, vector = (amount, width), (amount, 128), ((1, width), f32)
    low_flat, full_flat = (flat, bf16), (flat, f32)
    probs_self, probs_cross = (pairs, tiles_of, 4 * slots, 2 * slots), (rows, tiles_of, 2 * slots, padded)
    image_part = ((window, padded, width), bf16)
    (
        queries, keys, values, self_probs, self_context, first_unit, first_inverse, first_low, cross_queries, image_keys,
        image_values, cross_probs, cross_context, second_unit, second_inverse, second_value, second_low,
    ) = on_core(
        forward_kernel,
        "forward",
        [image, text, near, pair_ok, cell_ok, self_weights, cross_weights, keyval]
        + [row(v) for v in (first_gain, first_shift, second_gain, second_shift)],
        [low_flat] * 3 + [(probs_self, bf16), low_flat, full_flat, (unit_row, f32), low_flat, low_flat]
        + [image_part, image_part, (probs_cross, bf16), low_flat, full_flat, (unit_row, f32), full_flat, low_flat],
        [full_flat] * 3,
        scalars=1,
    )
    joined, expand_grad, shrink_grad, bias_grad, third_gain_grad, third_shift_grad, second_up = on_core(
        feed_kernel,
        "feed",
        [second_value, second_low, expand, shrink, bias, row(third_gain), row(third_shift), cotangent.reshape(flat)],
        [low_flat, (expand.shape, bf16), (shrink.shape, bf16), (bias.shape, f32), vector, vector, full_flat],
        [((parts,) + flat, bf16)] * 2 + [full_flat, full_flat, (unit_row, f32), low_flat],
    )
    cross_weights_grad, keyval_grad, patch, second_gain_grad, second_shift_grad, first_up = on_core(
        cross_back_kernel,
        "cross_back",
        [image, near, cross_weights, keyval, cross_queries, image_keys, image_values, cross_probs, cross_context, second_up]
        + [second_unit, second_inverse, row(second_gain), first_low],
        [(cross_weights.shape, bf16), (keyval.shape, bf16), ((parts, window, padded, depth // parts), bf16)]
        + [vector, vector, full_flat],
        [low_flat, full_flat, full_flat, (image_part[0], f32), (image_part[0], f32), low_flat],
        scalars=1,
    )
    self_weights_grad, first_gain_grad, first_shift_grad, text_grad = on_core(
        self_back_kernel,
        "self_back",
        [text, self_weights, queries, keys, values, self_probs, self_context, first_up, first_unit, first_inverse]
        + [row(first_gain)],
        [(self_weights.shape, bf16), vector, vector, full_flat],
        [low_flat] * 5,
    )
    vectors = jnp.concatenate(
        [bias_grad.reshape(-1)]
        + [
            grad.reshape(-1)
            for grad in (
                first_gain_grad, first_shift_grad, second_gain_grad, second_shift_grad, third_gain_grad, third_shift_grad
            )
        ]
    )
    entries = vectors.shape[0]
    vectors = jnp.pad(vectors.reshape(entries // 128, 128), ((0, -(entries // 128) % 8), (0, 0)))
    grads = [self_weights_grad, cross_weights_grad, keyval_grad, expand_grad, shrink_grad]
    order = [(4, 0, 768), (3, 0, 768), (1, 0, 384), (2, 0, 384), (0, 0, 768)]
    sums, windows, vectors = reduce_shards(grads, patch, vectors, order, own)
    (patch_grad,) = on_core(
        place_kernel, "place", [jnp.asarray(starts, jnp.int32), windows], [((group_images, cells, depth // parts), f32)], [],
        scalars=1,
    )
    self_sum, cross_sum, keyval_sum, expand_sum, shrink_sum = (total.astype(f32) for total in sums)
    vectors = vectors.reshape(-1)
    bias_sum = lax.dynamic_slice_in_dim(vectors, plane * hidden, hidden, 0)
    norms = [vectors[parts * hidden + i * width : parts * hidden + (i + 1) * width] for i in range(6)]
    return (
        joined.reshape(tokens.shape),
        text_grad.reshape(tokens.shape),
        patch_grad,
        jnp.stack([self_sum[c * inner : (c + 1) * inner].T for c in range(3)]),
        self_sum[3 * inner :],
        norms[0],
        norms[1],
        cross_sum[:inner].T,
        jnp.stack([keyval_sum[:inner].T, keyval_sum[inner:].T]),
        cross_sum[inner:],
        norms[2],
        norms[3],
        expand_sum.T,
        bias_sum,
        shrink_sum,
        norms[4],
        norms[5],
    )


def solution(mesh):
    parts = mesh.shape["mp"]
    own = mesh.shape["dp"] == 8 and parts == 4
    return jax.shard_map(
        functools.partial(per_device, parts=parts, own=own),
        mesh=mesh,
        in_specs=(
            P(("dp", "mp"), None, None),
            P("dp", None, None),
            P("dp", None),
            P("dp"),
            P("dp", None),
            P(None, None, "mp"),
            P("mp", None),
            P(),
            P(),
            P(None, "mp"),
            P(None, None, "mp"),
            P("mp", None),
            P(),
            P(),
            P(None, "mp"),
            P("mp"),
            P("mp", None),
            P(),
            P(),
            P(("dp", "mp"), None, None),
        ),
        out_specs=(
            P(("dp", "mp"), None, None),
            P(("dp", "mp"), None, None),
            P("dp", None, "mp"),
            P(None, None, "mp"),
            P("mp", None),
            P(),
            P(),
            P(None, "mp"),
            P(None, None, "mp"),
            P("mp", None),
            P(),
            P(),
            P(None, "mp"),
            P("mp"),
            P("mp", None),
            P(),
            P(),
        ),
        check_vma=False,
    )
```

```python
import functools

import jax
import jax.numpy as jnp
from jax import lax
from jax.experimental import pallas as pl
from jax.experimental.pallas import tpu as pltpu
from jax.sharding import PartitionSpec as P

HEAD_DIM = 64
ROWS_MAX = 7
MESH = pl.DeviceIdType.MESH


def place():
    index = lax.axis_index("dp")
    plane = lax.axis_index("mp")
    y, x, c = index // 4, (index // 2) % 2, index % 2
    return index, plane, y, x, c


def partners(index, plane):
    core = (index + 1 - 2 * (index % 2), plane)
    across = (index + 2 - 4 * ((index // 2) % 2), plane)
    along = (index + 4 - 8 * (index // 4), plane)
    planes = [(index, lax.rem(plane + step, 4)) for step in (1, 2, 3)]
    return core, across, along, planes


def greet(peers):
    barrier = pltpu.get_barrier_semaphore()
    for peer in peers:
        pl.semaphore_signal(barrier, inc=1, device_id=peer, device_id_type=MESH)
    pl.semaphore_wait(barrier, len(peers))


class Sends:
    def __init__(self):
        self.stages, self.all = {}, []

    def start(self, name, k, items):
        copies = []
        for source, target, sends, recvs, peer in items:
            copy = pltpu.make_async_remote_copy(
                src_ref=source, dst_ref=target, send_sem=sends, recv_sem=recvs, device_id=peer, device_id_type=MESH
            )
            copy.start()
            copies.append(copy)
        self.stages[name, k] = copies
        self.all.extend(copies)

    def arrived(self, name, k):
        for copy in self.stages[name, k]:
            copy.wait_recv()

    def close(self):
        for copy in self.all:
            copy.wait_send()


class Gather:
    stages = 4

    def __init__(self, chunks, shards, wholes, sems, window, gap):
        self.chunks, self.shards, self.wholes, self.window = chunks, shards, wholes, window
        self.sems, self.gap = sems, gap
        self.index, self.plane, self.y, self.x, self.c = place()
        self.core, self.across, self.along, self.planes = partners(self.index, self.plane)
        self.others = [lax.rem(self.plane + step, 4) for step in (1, 2, 3)]
        self.sends = Sends()

    def sizes(self, k):
        which, base, rows = self.chunks[k]
        return which, base, rows // 8, self.wholes[which].shape[2] // 2

    def level(self, k):
        which, base, r, w = self.sizes(k)
        _, _, send, recv = self.sems[:4]
        self.own(which)
        items = []
        for h, first in enumerate((self.x * 2 + self.y, self.y * 2 + self.x)):
            here = (pl.ds(pl.multiple_of(base + (self.c * 4 + first) * r, 16), r), pl.ds(h * w, w))
            for j, peer in enumerate(self.planes):
                piece = self.wholes[which].at[(self.plane,) + here]
                items.append((piece, piece, send.at[k, h, j], recv.at[k, h, j], peer))
        self.sends.start("level", k, items)

    def near(self, k):
        which, base, r, w = self.sizes(k)
        send, recv = self.sems[4:6]
        self.sends.arrived("level", k)
        if k + self.window < len(self.chunks):
            self.level(k + self.window)
        items = []
        for h, first in enumerate((self.x * 2 + self.y, self.y * 2 + self.x)):
            row = pl.multiple_of(base + (self.c * 4 + first) * r, 16)
            for j, other in enumerate(self.others):
                piece = self.wholes[which].at[other, pl.ds(row, r), pl.ds(h * w, w)]
                items.append((piece, piece, send.at[k, h, j], recv.at[k, h, j], (self.along, self.across)[h]))
        self.sends.start("near", k, items)

    def far(self, k):
        which, base, r, w = self.sizes(k)
        send, recv = self.sems[6:8]
        self.sends.arrived("near", k)
        items = []
        for h, first in enumerate((self.x, self.y)):
            row = pl.multiple_of(base + (self.c * 4 + first * 2) * r, 16)
            for j, other in enumerate(self.others):
                piece = self.wholes[which].at[other, pl.ds(row, 2 * r), pl.ds(h * w, w)]
                items.append((piece, piece, send.at[k, h, j], recv.at[k, h, j], (self.across, self.along)[h]))
        self.sends.start("far", k, items)

    def cross(self, k):
        which, base, r, w = self.sizes(k)
        send, recv = self.sems[8:10]
        self.sends.arrived("far", k)
        row = pl.multiple_of(base + self.c * 4 * r, 16)
        items = []
        for j, other in enumerate(self.others):
            piece = self.wholes[which].at[other, pl.ds(row, 4 * r), :]
            items.append((piece, piece, send.at[k, j], recv.at[k, j], self.core))
        self.sends.start("core", k, items)

    def own(self, which):
        for copy in self.local.pop(which, ()):
            copy.wait()

    def begin(self):
        self.local = {}
        for which, pieces in enumerate(self.shards):
            row, self.local[which] = 0, []
            for i, piece in enumerate(pieces):
                target = self.wholes[which].at[self.plane, pl.ds(row, piece.shape[0]), :]
                copy = pltpu.make_async_copy(piece, target, self.sems[0].at[which, i])
                copy.start()
                self.local[which].append(copy)
                row += piece.shape[0]
        greet([self.core, self.across, self.along] + self.planes)
        for k in range(self.window):
            self.level(k)

    def step(self, t):
        if 0 <= t - 2 * self.gap < len(self.chunks):
            self.cross(t - 2 * self.gap)
        if 0 <= t - self.gap < len(self.chunks):
            self.far(t - self.gap)
        if 0 <= t < len(self.chunks):
            self.near(t)

    @property
    def steps(self):
        return len(self.chunks) + 2 * self.gap

    def ready(self, k):
        self.sends.arrived("core", k)

    @staticmethod
    def scratch(count, total):
        dma = pltpu.SemaphoreType.DMA
        return [dma((count, 2)), dma((count,))] + [dma((total, 2, 3))] * 6 + [dma((total, 3))] * 2


class Ticks:
    def __init__(self, gather, outs, sem):
        self.gather, self.outs, self.sem = gather, outs, sem
        self.now, self.done, self.final = 0, 0, []

    def __call__(self):
        gather, total = self.gather, len(self.gather.chunks)
        if self.now < gather.steps:
            gather.step(self.now)
        k = self.now - 3 * gather.gap
        if 0 <= k < total:
            gather.ready(k)
            self.done = k + 1
            which = gather.chunks[k][0]
            if k + 1 == total or gather.chunks[k + 1][0] != which:
                copy = pltpu.make_async_copy(gather.wholes[which], self.outs[which], self.sem.at[which])
                copy.start()
                self.final.append(copy)
        self.now += 1

    def wait(self, which):
        last = max(k for k, chunk in enumerate(self.gather.chunks) if chunk[0] == which)
        while self.done <= last:
            self()

    def close(self):
        while self.done < len(self.gather.chunks):
            self()
        self.gather.sends.close()
        for copy in self.final:
            copy.wait()


def forward_kernel(chunks, pieces, window, count, *refs):
    image, tokens, pair_ok, cell_ok, norms, patches = refs[:6]
    refs, shards, arrays = refs[6:], [], len(pieces)
    for amount in pieces:
        shards.append(refs[:amount])
        refs = refs[amount:]
    outs, biases, far, refs = refs[:arrays], refs[arrays], refs[arrays + 1 : arrays + 1 + count], refs[arrays + 1 + count :]
    wholes, refs = refs[:arrays], refs[arrays:]
    saved = [Slot(far[i], refs[2 * i], refs[2 * i + 1]) for i in range(count)]
    (wide, near, bias_send, bias_recv, near_sem), sems = refs[2 * count : 2 * count + 5], refs[2 * count + 5 :]
    gather = Gather(chunks, shards, wholes, sems, 3, 1)
    gather.begin()
    gather.sends.start(
        "bias", 0, [(norms, biases.at[gather.plane], bias_send.at[j], bias_recv.at[j], peer) for j, peer in enumerate(gather.planes)]
    )
    start = jnp.minimum(gather.plane * cell_ok.shape[0] // ROWS_MAX, patches.shape[0] - window)
    copy = pltpu.make_async_copy(patches.at[pl.ds(start, window)], near, near_sem)
    copy.start()
    biases[gather.plane] = norms[...]
    copy.wait()
    ticks = Ticks(gather, outs, sems[1])
    forward_steps(ticks, image, tokens, near, pair_ok, cell_ok, wholes[:3], norms, saved, wide)
    gather.sends.arrived("bias", 0)
    ticks.close()
    for slot in saved:
        slot.finish()


def gather_forward(image, inputs, patches, shards, window, outputs, chunks):
    dma, bf16, arrays, count = pltpu.SemaphoreType.DMA, jnp.bfloat16, len(shards), len(outputs)
    any_space, vmem = pl.BlockSpec(memory_space=pl.ANY), pl.BlockSpec(memory_space=pltpu.VMEM)
    tokens, norms = inputs[0], inputs[-1]
    shapes = [(4, sum(piece.shape[0] for piece in pieces), pieces[0].shape[1]) for pieces in shards]
    flat = [piece for pieces in shards for piece in pieces]
    results = pl.pallas_call(
        functools.partial(forward_kernel, chunks, [len(pieces) for pieces in shards], window, count),
        out_shape=[jax.ShapeDtypeStruct(shape, bf16) for shape in shapes]
        + [jax.ShapeDtypeStruct((4,) + norms.shape, norms.dtype)]
        + [jax.ShapeDtypeStruct(shape, kind) for shape, kind in outputs],
        in_specs=[pl.BlockSpec(memory_space=pltpu.SMEM)] + [vmem] * len(inputs) + [any_space] * (len(flat) + 1),
        out_specs=[any_space] * arrays + [vmem] + [any_space] * count,
        scratch_shapes=[pltpu.VMEM(shape, bf16) for shape in shapes]
        + [entry for shape, kind in outputs for entry in slot_scratch(shape, kind)]
        + [pltpu.VMEM(tokens.shape, jnp.float32), pltpu.VMEM((window,) + patches.shape[1:], bf16)]
        + [dma((3,)), dma((3,)), dma(())]
        + Gather.scratch(arrays, len(chunks)),
        compiler_params=pltpu.CompilerParams(collective_id=0, has_side_effects=True, vmem_limit_bytes=63 << 20),
        name="gather_forward",
    )(image, *inputs, patches, *flat)
    return results[:arrays], results[arrays], results[arrays + 1 :]


class Alone:
    def __call__(self):
        pass

    def wait(self, which):
        pass


def lone_forward_kernel(image, inputs, outputs, scratch):
    tokens, pair_ok, cell_ok, norms, near, *weights = (slot.ready() for slot in inputs)
    forward_steps(Alone(), image, tokens, near, pair_ok, cell_ok, weights, norms, outputs, scratch[0])


class Reduce:
    def __init__(self, chunks, grads, sums, buffers, sems):
        self.chunks, self.grads, self.sums, self.sems = chunks, grads, sums, sems
        total = len(chunks)
        self.mine, self.core_in, self.near_in, self.far_in, self.plane_in, self.done = (
            buffers[i * total : (i + 1) * total] for i in range(6)
        )
        self.index, self.plane, self.y, self.x, self.c = place()
        self.core, self.across, self.along, self.planes = partners(self.index, self.plane)
        self.others = [lax.rem(self.plane + step, 4) for step in (1, 2, 3)]
        self.sends = Sends()
        self.local, self.final = {}, []
        self.order = [self.begin, self.near, self.far, self.level, self.out_near, self.out_far, self.out_core, self.end]

    @staticmethod
    def scratch(sizes):
        low, dma, total = jnp.bfloat16, pltpu.SemaphoreType.DMA, len(sizes)
        shapes = [[(4, r // 2, w) for r, w in sizes]] * 2
        shapes += [[(2, 4, r // 4, w // 2) for r, w in sizes], [(2, 4, r // 8, w // 2) for r, w in sizes]]
        shapes += [[(2, 3, r // 8, w // 2) for r, w in sizes], [(r, w) for r, w in sizes]]
        buffers = [pltpu.VMEM(shape, low) for group in shapes for shape in group]
        sems = [dma((total,))] * 4 + [dma((total, 2))] * 8 + [dma((total, 2, 3))] * 2 + [dma((total,))] * 2
        return buffers, sems

    def sizes(self, k):
        which, base, rows = self.chunks[k]
        return which, base, rows // 8, self.grads[which].shape[2] // 2

    @staticmethod
    def add(total, total_row, total_col, part, part_col, rows, cols):
        @pl.loop(0, rows // 16)
        def _(i):
            for shard in range(4):
                here = (shard, pl.ds(pl.multiple_of(total_row + i * 16, 16), 16), pl.ds(total_col, cols))
                there = (shard, pl.ds(pl.multiple_of(i * 16, 16), 16), pl.ds(part_col, cols))
                total[here] = (total[here].astype(jnp.float32) + part[there].astype(jnp.float32)).astype(jnp.bfloat16)

    def places(self, r, w):
        return [((self.x * 2 + self.y) * r, 0), ((self.y * 2 + self.x) * r, w)]

    def begin(self, k):
        which, base, r, w = self.sizes(k)
        theirs = pl.multiple_of(base + (1 - self.c) * 4 * r, 16)
        ours = pl.multiple_of(base + self.c * 4 * r, 16)
        source = self.grads[which].at[:, pl.ds(theirs, 4 * r), :]
        self.sends.start("core", k, [(source, self.core_in[k], self.sems[0].at[k], self.sems[1].at[k], self.core)])
        self.local[k] = pltpu.make_async_copy(
            self.grads[which].at[:, pl.ds(ours, 4 * r), :], self.mine[k], self.sems[2].at[k]
        )
        self.local[k].start()

    def near(self, k):
        which, base, r, w = self.sizes(k)
        self.local[k].wait()
        self.sends.arrived("core", k)
        self.add(self.mine[k], 0, 0, self.core_in[k], 0, 4 * r, 2 * w)
        items = []
        for h, (bit, peer) in enumerate([(self.x, self.across), (self.y, self.along)]):
            row = pl.multiple_of((1 - bit) * 2 * r, 16)
            source = self.mine[k].at[:, pl.ds(row, 2 * r), pl.ds(h * w, w)]
            items.append((source, self.near_in[k].at[h], self.sems[4].at[k, h], self.sems[5].at[k, h], peer))
        self.sends.start("near", k, items)

    def far(self, k):
        which, base, r, w = self.sizes(k)
        self.sends.arrived("near", k)
        items = []
        for h, (bit, second, peer) in enumerate([(self.x, self.y, self.along), (self.y, self.x, self.across)]):
            row = bit * 2 * r
            self.add(self.mine[k], row, h * w, self.near_in[k].at[h], 0, 2 * r, w)
            row = pl.multiple_of(row + (1 - second) * r, 16)
            source = self.mine[k].at[:, pl.ds(row, r), pl.ds(h * w, w)]
            items.append((source, self.far_in[k].at[h], self.sems[6].at[k, h], self.sems[7].at[k, h], peer))
        self.sends.start("far", k, items)

    def level(self, k):
        which, base, r, w = self.sizes(k)
        self.sends.arrived("far", k)
        items = []
        for h, (row, col) in enumerate(self.places(r, w)):
            self.add(self.mine[k], row, col, self.far_in[k].at[h], 0, r, w)
            row = pl.multiple_of(row, 16)
            for j in range(3):
                source = self.mine[k].at[self.others[j], pl.ds(row, r), pl.ds(col, w)]
                items.append(
                    (source, self.plane_in[k].at[h, j], self.sems[12].at[k, h, j], self.sems[13].at[k, h, j], self.planes[j])
                )
        self.sends.start("level", k, items)

    def out_near(self, k):
        which, base, r, w = self.sizes(k)
        self.sends.arrived("level", k)
        items = []
        for h, (row, col) in enumerate(self.places(r, w)):

            @pl.loop(0, r // 16)
            def _(i):
                step = pl.ds(pl.multiple_of(i * 16, 16), 16)
                here = pl.ds(pl.multiple_of(row + i * 16, 16), 16)
                total = self.mine[k][self.plane, here, pl.ds(col, w)].astype(jnp.float32)
                for j in range(3):
                    total = total + self.plane_in[k][h, j, step, :].astype(jnp.float32)
                here = pl.ds(pl.multiple_of(self.c * 4 * r + row + i * 16, 16), 16)
                self.done[k][here, pl.ds(col, w)] = total.astype(jnp.bfloat16)

            piece = self.done[k].at[pl.ds(pl.multiple_of(self.c * 4 * r + row, 16), r), pl.ds(col, w)]
            peer = (self.along, self.across)[h]
            items.append((piece, piece, self.sems[8].at[k, h], self.sems[9].at[k, h], peer))
        self.sends.start("out_near", k, items)

    def out_far(self, k):
        which, base, r, w = self.sizes(k)
        self.sends.arrived("out_near", k)
        items = []
        for h, (bit, peer) in enumerate([(self.x, self.across), (self.y, self.along)]):
            row = pl.multiple_of((self.c * 4 + bit * 2) * r, 16)
            piece = self.done[k].at[pl.ds(row, 2 * r), pl.ds(h * w, w)]
            items.append((piece, piece, self.sems[10].at[k, h], self.sems[11].at[k, h], peer))
        self.sends.start("out_far", k, items)

    def out_core(self, k):
        which, base, r, w = self.sizes(k)
        self.sends.arrived("out_far", k)
        piece = self.done[k].at[pl.ds(pl.multiple_of(self.c * 4 * r, 16), 4 * r), :]
        self.sends.start("out_core", k, [(piece, piece, self.sems[14].at[k], self.sems[15].at[k], self.core)])

    def end(self, k):
        which, base, r, w = self.sizes(k)
        self.sends.arrived("out_core", k)
        copy = pltpu.make_async_copy(self.done[k], self.sums[which].at[pl.ds(base, 8 * r), :], self.sems[3].at[k])
        copy.start()
        self.final.append(copy)

    @property
    def steps(self):
        return len(self.chunks) + len(self.order) - 1

    def step(self, t):
        for s in reversed(range(len(self.order))):
            if 0 <= t - s < len(self.chunks):
                self.order[s](t - s)

    def close(self):
        self.sends.close()
        for copy in self.final:
            copy.wait()


def reduce_kernel(chunks, count, *refs):
    grads, patch, vectors = refs[:count], refs[count], refs[count + 1]
    sums, windows, vector_sum = refs[count + 2 : 2 * count + 2], refs[2 * count + 2], refs[2 * count + 3]
    rest = refs[2 * count + 4 :]
    total = 6 * len(chunks)
    buffers, sems = rest[:total], rest[total : total + 16]
    vector_in, patch_send, patch_recv, vector_send, vector_recv, patch_local = rest[total + 16 :]
    reduce = Reduce(chunks, grads, sums, buffers, sems)
    greet([reduce.core, reduce.across, reduce.along] + reduce.planes)
    reduce.sends.start(
        "patch",
        0,
        [
            (patch.at[other], windows.at[reduce.plane], patch_send.at[j], patch_recv.at[j], peer)
            for j, (other, peer) in enumerate(zip(reduce.others, reduce.planes))
        ],
    )
    copy = pltpu.make_async_copy(patch.at[reduce.plane], windows.at[reduce.plane], patch_local)
    copy.start()
    vector_sum[0] = vectors[...]
    for t in range(reduce.steps):
        if t < 3:
            peer = (reduce.core, reduce.across, reduce.along)[t]
            reduce.sends.start("vector", t, [(vector_sum.at[t], vector_in.at[t], vector_send.at[t], vector_recv.at[t], peer)])
        if t == 3:
            reduce.sends.start(
                "vector",
                t,
                [
                    (vector_sum.at[3], vector_in.at[3 + j], vector_send.at[3 + j], vector_recv.at[3 + j], peer)
                    for j, peer in enumerate(reduce.planes)
                ],
            )
        reduce.step(t)
        if t < 3:
            reduce.sends.arrived("vector", t)
            vector_sum[t + 1] = vector_sum[t] + vector_in[t]
        if t == 3:
            reduce.sends.arrived("vector", t)
            vector_sum[4] = vector_sum[3] + ((vector_in[3] + vector_in[4]) + vector_in[5])
    reduce.sends.arrived("patch", 0)
    reduce.close()
    copy.wait()


def reduce_grads(grads, patch, vectors, chunks):
    count, dma = len(grads), pltpu.SemaphoreType.DMA
    any_space, vmem = pl.BlockSpec(memory_space=pl.ANY), pl.BlockSpec(memory_space=pltpu.VMEM)
    buffers, sems = Reduce.scratch([(rows, grads[which].shape[2]) for which, _, rows in chunks])
    *sums, windows, vector_sum = pl.pallas_call(
        functools.partial(reduce_kernel, chunks, count),
        out_shape=[jax.ShapeDtypeStruct(g.shape[1:], g.dtype) for g in grads]
        + [jax.ShapeDtypeStruct(patch.shape, patch.dtype), jax.ShapeDtypeStruct((5,) + vectors.shape, vectors.dtype)],
        in_specs=[any_space] * (count + 1) + [vmem],
        out_specs=[any_space] * (count + 1) + [vmem],
        scratch_shapes=buffers
        + sems
        + [pltpu.VMEM((6,) + vectors.shape, vectors.dtype), dma((3,)), dma((3,)), dma((6,)), dma((6,)), dma(())],
        compiler_params=pltpu.CompilerParams(collective_id=1, has_side_effects=True, vmem_limit_bytes=62 << 20),
        name="reduce_grads",
    )(*grads, patch, vectors)
    return sums, windows, vector_sum[4]


class Slot:
    def __init__(self, far, near, sem, parts=0):
        self.far, self.near, self.sem, self.parts, self.waited = far, near, sem, parts, False

    def copy(self, out, m=None):
        far, near = (self.far, self.near) if m is None else (self.far.at[m], self.near.at[m])
        sem = self.sem.at[0 if m is None else m]
        return pltpu.make_async_copy(near, far, sem) if out else pltpu.make_async_copy(far, near, sem)

    def fetch(self):
        for m in range(self.parts) if self.parts else (None,):
            self.copy(False, m).start()

    def ready(self):
        if not self.waited:
            self.waited = True
            for m in range(self.parts) if self.parts else (None,):
                self.copy(False, m).wait()
        return self.near

    def flush(self, m=None):
        self.copy(True, m).start()

    def finish(self):
        for m in range(self.parts) if self.parts else (None,):
            self.copy(True, m).wait()


def slot_scratch(shape, kind, parts=0):
    return [pltpu.VMEM(shape, kind), pltpu.SemaphoreType.DMA((max(parts, 1),))]


def on_slots(kernel, name, image, inputs, outputs, scratch, parts_in=(), parts_out=()):
    count, total = len(inputs), len(inputs) + len(outputs)

    def body(image_ref, *refs):
        far, refs = refs[:total], refs[total:]
        slots = []
        for i in range(total):
            parts = far[i].shape[0] if (i in parts_in if i < count else i - count in parts_out) else 0
            slots.append(Slot(far[i], refs[2 * i], refs[2 * i + 1], parts))
        for slot in slots[:count]:
            slot.fetch()
        kernel(image_ref, slots[:count], slots[count:], refs[2 * total :])
        for slot in slots[count:]:
            slot.finish()

    spaces = []
    for i, array in enumerate(inputs):
        spaces += slot_scratch(array.shape, array.dtype, array.shape[0] if i in parts_in else 0)
    for i, (shape, kind) in enumerate(outputs):
        spaces += slot_scratch(shape, kind, shape[0] if i in parts_out else 0)
    any_space = pl.BlockSpec(memory_space=pl.ANY)
    return pl.pallas_call(
        body,
        out_shape=[jax.ShapeDtypeStruct(shape, kind) for shape, kind in outputs],
        in_specs=[pl.BlockSpec(memory_space=pltpu.SMEM)] + [any_space] * count,
        out_specs=[any_space] * len(outputs),
        scratch_shapes=spaces + [pltpu.VMEM(shape, kind) for shape, kind in scratch],
        compiler_params=pltpu.CompilerParams(vmem_limit_bytes=63 << 20),
        name=name,
    )(image, *inputs)


def nn(left, right):
    return lax.dot_general(left, right, (((1,), (0,)), ((), ())), preferred_element_type=jnp.float32)


def nt(left, right):
    return lax.dot_general(left, right, (((1,), (1,)), ((), ())), preferred_element_type=jnp.float32)


def tn(left, right):
    return lax.dot_general(left, right, (((0,), (0,)), ((), ())), preferred_element_type=jnp.float32)


def part(ref, which):
    inner = ref.shape[2] // 4 if ref.shape[2] == 768 else 192
    return jnp.concatenate([ref[m, which * 192 : (which + 1) * 192, :] for m in range(4)], axis=0)


def store_part(ref, which, value):
    low = value.astype(jnp.bfloat16)
    for m in range(4):
        ref[m, which * 192 : (which + 1) * 192, :] = low[m * 192 : (m + 1) * 192]


def tiles(amount, step):
    def wrap(body):
        @pl.loop(0, amount // step)
        def _(i):
            body(pl.ds(pl.multiple_of(i * step, step), step))

    return wrap


def lanes():
    place = lax.broadcasted_iota(jnp.int32, (1, 2 * HEAD_DIM), 1)
    low = place < HEAD_DIM
    return low, low.astype(jnp.float32), 1.0 - low.astype(jnp.float32)


def norm_forward(total, unit, inverse, value, value_low, gain, shift):
    @tiles(total.shape[0], 80)
    def _(rows):
        hidden = total[rows, :]
        center = hidden - jnp.mean(hidden, axis=-1, keepdims=True)
        factor = lax.rsqrt(jnp.mean(center * center, axis=-1, keepdims=True) + 1e-06)
        scaled = center * factor
        result = scaled * gain[...] + shift[...]
        if unit is not None:
            unit[rows, :] = scaled
            inverse[rows, :] = jnp.broadcast_to(factor, (80, 128))
        if value is not None:
            value[rows, :] = result
        value_low[rows, :] = result.astype(jnp.bfloat16)


def norm_reverse(upstream, unit, inverse, gain, gain_grad, shift_grad, grad, grad_low):
    gain_grad[...] = jnp.zeros_like(gain_grad)
    shift_grad[...] = jnp.zeros_like(shift_grad)

    @tiles(upstream.shape[0], 80)
    def _(rows):
        up = upstream[rows, :].astype(jnp.float32)
        scaled = unit[rows, :]
        factor = inverse[rows, :][:, :1]
        gain_grad[...] += jnp.sum(up * scaled, axis=0, keepdims=True)
        shift_grad[...] += jnp.sum(up, axis=0, keepdims=True)
        inner = up * gain[...]
        result = factor * (
            inner
            - jnp.mean(inner, axis=-1, keepdims=True)
            - scaled * jnp.mean(inner * scaled, axis=-1, keepdims=True)
        )
        grad[rows, :] = result
        grad_low[rows, :] = result.astype(jnp.bfloat16)


def softmax(scores):
    raised = jnp.exp(scores - jnp.max(scores, axis=-1, keepdims=True))
    return (raised * (1.0 / jnp.sum(raised, axis=-1, keepdims=True))).astype(jnp.bfloat16)


def columns(width):
    return [slice(start, start + 128) for start in range(0, width, 128)]


def stack(value, first, second):
    return jnp.concatenate([value * first, value * second], axis=0)


def merge(low, value):
    half = value.shape[0] // 2
    return jnp.where(low, value[:half], value[half:])


def attend_self(queries, keys, values, pair_ok, probs, context, begin, end):
    low, first, second = lanes()
    first, second = first.astype(jnp.bfloat16), second.astype(jnp.bfloat16)
    cols = columns(queries.shape[1])

    @pl.loop(begin, end)
    def _(pair):
        rows = pl.ds(pl.multiple_of(pair * 80, 80), 80)
        allowed = pair_ok[pair] > 0
        allowed = jnp.concatenate([allowed, allowed], axis=0)
        stacked = [stack(queries[rows, c], first, second) for c in cols]
        scores = [nt(both, keys[rows, c]) * HEAD_DIM ** (-0.5) for both, c in zip(stacked, cols)]
        weights = [softmax(jnp.where(allowed, score, -1000000000.0)) for score in scores]
        mixed = [merge(low, nn(weight, values[rows, c])) for weight, c in zip(weights, cols)]
        for tile, c in enumerate(cols):
            probs[pair, tile] = weights[tile]
            context[rows, c] = mixed[tile].astype(jnp.bfloat16)


def attend_cross(image, wide, keys, values, cell_ok, probs, begin, end):
    low, first, second = lanes()
    cols = columns(wide.shape[1])

    @pl.loop(begin, end)
    def _(row):
        rows = pl.ds(pl.multiple_of(row * 40, 40), 40)
        which = image[row]
        allowed = jnp.broadcast_to(cell_ok[pl.ds(row, 1), :], (80, cell_ok.shape[1])) > 0
        stacked = [stack(wide[rows, c], first, second).astype(jnp.bfloat16) for c in cols]
        scores = [nt(both, keys[which, :, c]) * HEAD_DIM ** (-0.5) for both, c in zip(stacked, cols)]
        weights = [softmax(jnp.where(allowed, score, -1000000000.0)) for score in scores]
        mixed = [merge(low, nn(weight, values[which, :, c])) for weight, c in zip(weights, cols)]
        for tile, c in enumerate(cols):
            probs[row, tile] = weights[tile]
            wide[rows, c] = mixed[tile]


def forward_steps(ticks, image, tokens, near, pair_ok, cell_ok, weights, norms, saved, wide):
    bf16 = jnp.bfloat16
    self_weights, cross_weights, keyval = weights
    (
        queries, keys, values, self_probs, self_context, first_unit, first_inverse, first_low, cross_queries, image_keys,
        image_values, cross_probs, cross_context, second_unit, second_inverse, second_value, second_low,
    ) = (slot.near for slot in saved)

    def flush(*places):
        for place in places:
            saved[place].flush()

    gains = [norms.at[pl.ds(i, 1), :] for i in range(4)]
    ticks.wait(0)
    for target, which in ((queries, 0), (keys, 1), (values, 2)):
        target[...] = nt(tokens[...], part(self_weights, which)).astype(bf16)
    flush(0, 1, 2)
    ticks()
    pairs = pair_ok.shape[0]
    attend_self(queries, keys, values, pair_ok, self_probs, self_context, 0, pairs)
    flush(3, 4)
    ticks()
    second_value[...] = nn(self_context[...], part(self_weights, 3)) + tokens[...].astype(jnp.float32)
    norm_forward(second_value, first_unit, first_inverse, None, first_low, gains[0], gains[1])
    flush(5, 6, 7)
    ticks.wait(1)
    cross_queries[...] = nt(first_low[...], part(cross_weights, 0)).astype(bf16)
    flush(8)
    wide[...] = cross_queries[...].astype(jnp.float32)
    images, cells, depth = near.shape
    half = images // 2
    ticks.wait(2)
    for target, which in ((image_keys, 0), (image_values, 1)):
        weight = part(keyval, which)
        for step in range(2):
            block = near[step * half : (step + 1) * half].reshape(half * cells, depth)
            target[step * half : (step + 1) * half] = nt(block, weight).astype(bf16).reshape(half, cells, -1)
        flush(9 + which)
    ticks()
    rows = cell_ok.shape[0]
    for part_of in range(2):
        begin, end = part_of * rows // 2, (part_of + 1) * rows // 2
        attend_cross(image, wide, image_keys, image_values, cell_ok, cross_probs, begin, end)
        ticks()
    flush(11)
    cross_context[...] = wide[...].astype(bf16)
    flush(12)
    second_value[...] = nn(cross_context[...], part(cross_weights, 1)) + (first_unit[...] * gains[0][...] + gains[1][...])
    norm_forward(second_value, second_unit, second_inverse, second_value, second_low, gains[2], gains[3])
    flush(13, 14, 15, 16)


def feed_kernel(image, inputs, outputs, scratch):
    second_value, second_low, norms, biases, expand, shrink, cotangent = inputs
    joined, expand_grad, shrink_grad, vectors, second_up = outputs
    active, slope, wide, unit, inverse, feed_low = scratch
    bf16 = jnp.bfloat16
    total = second_up.near
    total[...] = second_value.ready()[...]
    second_low, norms, biases = second_low.ready(), norms.ready(), biases.ready()
    gain, shift = norms.at[pl.ds(4, 1), :], norms.at[pl.ds(5, 1), :]
    hidden = expand.near.shape[0]

    @pl.loop(0, hidden)
    def _(m):
        expand.copy(False, m).wait()
        wide[...] = nn(second_low[...], expand.near[m])

        @tiles(wide.shape[0], 80)
        def _(rows):
            inner = wide[rows, :] + biases[m, pl.ds(6, 1), :]
            share = 0.5 * (1.0 + lax.erf(inner * 0.5**0.5))
            active[m, rows, :] = (inner * share).astype(bf16)
            slope[m, rows, :] = (share + inner * (jnp.exp(-0.5 * inner * inner) * 0.3989422804014327)).astype(bf16)

        shrink.copy(False, m).wait()
        total[...] += nn(active[m], shrink.near[m])

    norm_forward(total, unit, inverse, None, joined.near, gain, shift)
    joined.flush()
    sums = vectors.near
    sums[...] = jnp.zeros_like(sums)
    norm_reverse(
        cotangent.ready(), unit, inverse, gain, sums.at[pl.ds(8, 1), :], sums.at[pl.ds(9, 1), :], total, feed_low
    )

    @pl.loop(0, hidden)
    def _(m):
        shrink_grad.near[m] = tn(active[m], feed_low[...]).astype(bf16)
        shrink_grad.flush(m)
        wide[...] = nt(feed_low[...], shrink.near[m])

        @tiles(wide.shape[0], 80)
        def _(rows):
            low = (wide[rows, :] * slope[m, rows, :].astype(jnp.float32)).astype(bf16)
            active[m, rows, :] = low
            sums[pl.ds(m, 1), :] += jnp.sum(low.astype(jnp.float32), axis=0, keepdims=True)

        expand_grad.near[m] = tn(second_low[...], active[m]).astype(bf16)
        expand_grad.flush(m)
        total[...] += nt(active[m], expand.near[m])

    vectors.flush()
    second_up.flush()


def score_back(weights, upstream):
    probs = weights.astype(jnp.float32)
    return (probs * (upstream - jnp.sum(probs * upstream, axis=-1, keepdims=True))).astype(jnp.bfloat16)


def cross_back_kernel(image, inputs, outputs, scratch):
    (
        second_up, second_unit, second_inverse, norms, cross_weights, cross_context, cross_queries, image_values,
        image_keys, cross_probs, first_low, keyval, near,
    ) = inputs
    weights_grad, keyval_grad, patch, vectors, first_up = outputs
    grad_low, wide, turn, key_sum, value_sum, query_low = scratch
    bf16 = jnp.bfloat16
    low, first, second = lanes()
    sums = vectors.near
    sums[...] = jnp.zeros_like(sums)
    norm_reverse(
        second_up.ready(), second_unit.ready(), second_inverse.ready(), norms.ready().at[pl.ds(2, 1), :],
        sums.at[pl.ds(6, 1), :], sums.at[pl.ds(7, 1), :], first_up.near, grad_low,
    )
    vectors.flush()
    cross_weights = cross_weights.ready()
    wide[...] = nt(grad_low[...], part(cross_weights, 1)).astype(bf16).astype(jnp.float32)
    store_part(weights_grad.near, 1, tn(cross_context.ready()[...], grad_low[...]))
    turn[...] = cross_queries.ready()[...].astype(jnp.float32)
    key_sum[...] = jnp.zeros_like(key_sum)
    value_sum[...] = jnp.zeros_like(value_sum)
    cols = columns(wide.shape[1])
    image_values, image_keys, cross_probs = image_values.ready(), image_keys.ready(), cross_probs.ready()

    @pl.loop(0, cross_probs.shape[0])
    def _(row):
        rows = pl.ds(pl.multiple_of(row * 40, 40), 40)
        which = image[row]
        queries = [stack(turn[rows, c], first, second).astype(bf16) for c in cols]
        grads = [stack(wide[rows, c], first, second).astype(bf16) for c in cols]
        weights = [cross_probs[row, tile] for tile in range(len(cols))]
        upstream = [nt(grad, image_values[which, :, c]) for grad, c in zip(grads, cols)]
        back = [score_back(weight, up) for weight, up in zip(weights, upstream)]
        mixed = [merge(low, nn(grad, image_keys[which, :, c])) * HEAD_DIM ** (-0.5) for grad, c in zip(back, cols)]
        key_parts = [tn(grad, both) * HEAD_DIM ** (-0.5) for grad, both in zip(back, queries)]
        value_parts = [tn(weight, grad) for weight, grad in zip(weights, grads)]
        for tile, c in enumerate(cols):
            turn[rows, c] = mixed[tile]
        for tile, c in enumerate(cols):
            key_sum[which, :, c] += key_parts[tile]
        for tile, c in enumerate(cols):
            value_sum[which, :, c] += value_parts[tile]

    keyval, near = keyval.ready(), near.ready()
    images, cells, depth = near.shape
    amount = images * cells
    for step in range(2):
        here = slice(step * (images // 2), (step + 1) * (images // 2))
        block = nn(key_sum[here].astype(bf16).reshape(amount // 2, -1), part(keyval, 0))
        block += nn(value_sum[here].astype(bf16).reshape(amount // 2, -1), part(keyval, 1))
        block = block.astype(bf16)
        quarter = patch.near.shape[3]
        for m in range(patch.near.shape[0]):
            patch.near[m, here] = block[:, m * quarter : (m + 1) * quarter].reshape(images // 2, cells, quarter)
    patch.flush()
    for source, which in ((key_sum, 0), (value_sum, 1)):
        flat = source[...].astype(bf16).reshape(amount, -1)
        store_part(keyval_grad.near, which, tn(flat, near[...].reshape(amount, depth)))
    keyval_grad.flush()
    query_low[...] = turn[...].astype(bf16)
    first_up.near[...] += nn(query_low[...], part(cross_weights, 0))
    first_up.flush()
    store_part(weights_grad.near, 0, tn(query_low[...], first_low.ready()[...]))
    weights_grad.flush()


def self_back_kernel(image, inputs, outputs, scratch):
    (
        first_up, first_unit, first_inverse, norms, self_weights, self_context, queries, keys, values, self_probs, tokens,
    ) = inputs
    weights_grad, vectors, text_grad = outputs
    grad_low, context_low, query_low, key_low, value_low = scratch
    bf16 = jnp.bfloat16
    low, first, second = lanes()
    first_mask, second_mask = first.astype(bf16), second.astype(bf16)
    sums = vectors.near
    sums[...] = jnp.zeros_like(sums)
    norm_reverse(
        first_up.ready(), first_unit.ready(), first_inverse.ready(), norms.ready().at[pl.ds(0, 1), :],
        sums.at[pl.ds(4, 1), :], sums.at[pl.ds(5, 1), :], text_grad.near, grad_low,
    )
    vectors.flush()
    self_weights = self_weights.ready()
    context_low[...] = nt(grad_low[...], part(self_weights, 3)).astype(bf16)
    store_part(weights_grad.near, 3, tn(self_context.ready()[...], grad_low[...]))
    cols = columns(context_low.shape[1])
    queries, keys, values, self_probs = queries.ready(), keys.ready(), values.ready(), self_probs.ready()

    @pl.loop(0, self_probs.shape[0])
    def _(pair):
        rows = pl.ds(pl.multiple_of(pair * 80, 80), 80)
        stacked = [stack(queries[rows, c], first_mask, second_mask) for c in cols]
        grads = [stack(context_low[rows, c], first_mask, second_mask) for c in cols]
        weights = [self_probs[pair, tile] for tile in range(len(cols))]
        upstream = [nt(grad, values[rows, c]) for grad, c in zip(grads, cols)]
        back = [score_back(weight, up) for weight, up in zip(weights, upstream)]
        query_parts = [merge(low, nn(grad, keys[rows, c])) * HEAD_DIM ** (-0.5) for grad, c in zip(back, cols)]
        key_parts = [tn(grad, both) * HEAD_DIM ** (-0.5) for grad, both in zip(back, stacked)]
        value_parts = [tn(weight, grad) for weight, grad in zip(weights, grads)]
        for tile, c in enumerate(cols):
            query_low[rows, c] = query_parts[tile].astype(bf16)
            key_low[rows, c] = key_parts[tile].astype(bf16)
            value_low[rows, c] = value_parts[tile].astype(bf16)

    tokens = tokens.ready()
    for source, which in ((query_low, 0), (key_low, 1), (value_low, 2)):
        store_part(weights_grad.near, which, tn(source[...], tokens[...]))
        text_grad.near[...] += nn(source[...], part(self_weights, which))
    weights_grad.flush()
    text_grad.flush()


def place_kernel(starts, windows, result):
    cells = result.shape[1]
    result[...] = jnp.zeros_like(result)
    for m in range(windows.shape[0]):

        @pl.loop(0, windows.shape[1])
        def _(i):
            result[starts[m] + i] += windows[m, i, :cells, :].astype(jnp.float32)


def on_core(kernel, name, inputs, outputs, scratch, scalars=0):
    vmem, smem = pl.BlockSpec(memory_space=pltpu.VMEM), pl.BlockSpec(memory_space=pltpu.SMEM)
    return pl.pallas_call(
        kernel,
        out_shape=[jax.ShapeDtypeStruct(shape, kind) for shape, kind in outputs],
        in_specs=[smem] * scalars + [vmem] * (len(inputs) - scalars),
        out_specs=[vmem] * len(outputs),
        scratch_shapes=[pltpu.VMEM(shape, kind) for shape, kind in scratch],
        compiler_params=pltpu.CompilerParams(vmem_limit_bytes=62 << 20),
        name=name,
    )(*inputs)


def image_windows(parts, rows, group_images):
    group_rows = parts * rows
    first = [m * rows // ROWS_MAX for m in range(parts)]
    last = [group_images - 1 - max(0, -(-(group_rows - (m + 1) * rows - (ROWS_MAX - 1)) // ROWS_MAX)) for m in range(parts)]
    last = [min(stop, (m + 1) * rows - 1) for m, stop in enumerate(last)]
    window = max(stop - start + 1 for start, stop in zip(first, last))
    return [min(start, group_images - window) for start in first], window


def forward(image, inputs, patches, shards, start, window, outputs, chunks, own):
    if own:
        return gather_forward(image, inputs, patches, shards, window, outputs, chunks)
    weights = [lax.all_gather(jnp.concatenate(pieces, axis=0), "mp", axis=0) for pieces in shards]
    biases = lax.all_gather(inputs[-1], "mp", axis=0)
    near = lax.dynamic_slice_in_dim(patches, start, window, 0)
    scratch = [(inputs[0].shape, jnp.float32)]
    saved = on_slots(lone_forward_kernel, "forward", image, inputs + [near] + weights[:3], outputs, scratch)
    return weights, biases, saved


def reduce_shards(grads, patch, vectors, chunks, own):
    if own:
        return reduce_grads(grads, patch, vectors, chunks)
    sums = [
        lax.psum(lax.psum_scatter(grad.astype(jnp.float32), "mp", scatter_dimension=0, tiled=True)[0], "dp")
        for grad in grads
    ]
    windows = lax.all_to_all(patch, "mp", split_axis=0, concat_axis=0, tiled=True)
    return sums, windows, lax.psum(vectors, ("dp", "mp"))


def per_device(
    tokens, patches, image_rows, row_lengths, box_mask, self_project, self_output, first_gain, first_shift, cross_query,
    cross_keyval, cross_output, second_gain, second_shift, expand_weight, expand_bias, shrink_weight, third_gain,
    third_shift, cotangent, *, parts, own,
):
    bf16, f32 = jnp.bfloat16, jnp.float32
    rows, slots, width = tokens.shape
    group_images, cells, depth = patches.shape
    starts, window = image_windows(parts, rows, group_images)
    padded = -(-cells // 16) * 16
    plane = lax.axis_index("mp")
    start = jnp.asarray(starts, jnp.int32)[plane]
    amount, pairs, tiles_of = rows * slots, rows // 2, width // 128

    inner = self_output.shape[0]
    shards = [
        [self_project.transpose(0, 2, 1).reshape(3 * inner, width), self_output],
        [cross_query.T, cross_output],
        [cross_keyval.transpose(0, 2, 1).reshape(2 * inner, depth)],
        [expand_weight],
        [shrink_weight],
    ]
    chunks = [(0, 0, 384), (0, 384, 384), (1, 0, 384), (2, 0, 384), (3, 0, 384), (3, 384, 384), (4, 0, 384), (4, 384, 384)]
    norms = [first_gain, first_shift, second_gain, second_shift, third_gain, third_shift, expand_bias]
    norms = jnp.stack(norms + [jnp.zeros_like(expand_bias)])
    counts = image_rows[0]
    ends = jnp.cumsum(counts)
    row_index = plane * rows + jnp.arange(rows, dtype=jnp.int32)
    owner = jnp.sum(row_index[:, None] >= ends[None, :], axis=1).astype(jnp.int32)
    caption = jnp.any(row_index[:, None] == (ends - counts)[None, :], axis=1)
    lengths = lax.dynamic_slice_in_dim(row_lengths, plane * rows, rows, 0)
    boxes = lax.dynamic_slice_in_dim(box_mask, plane * rows, rows, 0)
    cell_ok = jnp.pad((caption[:, None] | (boxes > 0)).astype(f32), ((0, 0), (0, padded - cells)))
    slot = jnp.arange(2 * slots, dtype=jnp.int32)
    key_ok = (slot % slots)[None, :] < jnp.repeat(lengths.reshape(pairs, 2), slots, axis=1)
    pair_ok = (key_ok[:, None, :] & ((slot // slots)[:, None] == (slot // slots)[None, :])[None]).astype(f32)
    patches = jnp.pad(patches, ((0, 0), (0, padded - cells), (0, 0)))
    near = lax.dynamic_slice_in_dim(patches, start, window, 0)
    image = owner - start

    text = tokens.reshape(amount, width)
    flat, unit_row = (amount, width), ((amount, 128), f32)
    low_flat, full_flat = (flat, bf16), (flat, f32)
    probs_self, probs_cross = (pairs, tiles_of, 4 * slots, 2 * slots), (rows, tiles_of, 2 * slots, padded)
    image_part, vector = ((window, padded, width), bf16), ((16, width), f32)
    weights, biases, saved = forward(
        image,
        [text, pair_ok, cell_ok, norms],
        patches,
        shards,
        start,
        window,
        [low_flat] * 3 + [(probs_self, bf16), low_flat, full_flat, unit_row, low_flat, low_flat]
        + [image_part, image_part, (probs_cross, bf16), low_flat, full_flat, unit_row, full_flat, low_flat],
        chunks,
        own,
    )
    self_weights, cross_weights, keyval, expand, shrink = weights
    (
        queries, keys, values, self_probs, self_context, first_unit, first_inverse, first_low, cross_queries, image_keys,
        image_values, cross_probs, cross_context, second_unit, second_inverse, second_value, second_low,
    ) = saved
    joined, expand_grad, shrink_grad, feed_vectors, second_up = on_slots(
        feed_kernel,
        "feed",
        image,
        [second_value, second_low, norms, biases, expand, shrink, cotangent.reshape(flat)],
        [low_flat, (expand.shape, bf16), (shrink.shape, bf16), vector, full_flat],
        [((parts,) + flat, bf16)] * 2 + [full_flat, full_flat, unit_row, low_flat],
        parts_in=(4, 5),
        parts_out=(1, 2),
    )
    cross_weights_grad, keyval_grad, patch, cross_vectors, first_up = on_slots(
        cross_back_kernel,
        "cross_back",
        image,
        [second_up, second_unit, second_inverse, norms, cross_weights, cross_context, cross_queries, image_values]
        + [image_keys, cross_probs, first_low, keyval, near],
        [(cross_weights.shape, bf16), (keyval.shape, bf16), ((parts, window, padded, depth // parts), bf16)]
        + [vector, full_flat],
        [low_flat, full_flat, full_flat, (image_part[0], f32), (image_part[0], f32), low_flat],
    )
    self_weights_grad, self_vectors, text_grad = on_slots(
        self_back_kernel,
        "self_back",
        image,
        [first_up, first_unit, first_inverse, norms, self_weights, self_context, queries, keys, values, self_probs, text],
        [(self_weights.shape, bf16), vector, full_flat],
        [low_flat] * 5,
    )
    vectors = feed_vectors + cross_vectors + self_vectors
    grads = [self_weights_grad, cross_weights_grad, keyval_grad, expand_grad, shrink_grad]
    order = [(4, 0, 768), (3, 0, 768), (1, 0, 384), (2, 0, 384), (0, 0, 768)]
    sums, windows, vectors = reduce_shards(grads, patch, vectors, order, own)
    (patch_grad,) = on_core(
        place_kernel, "place", [jnp.asarray(starts, jnp.int32), windows], [((group_images, cells, depth // parts), f32)], [],
        scalars=1,
    )
    self_sum, cross_sum, keyval_sum, expand_sum, shrink_sum = (total.astype(f32) for total in sums)
    bias_sum = lax.dynamic_index_in_dim(vectors, plane, 0, keepdims=False)
    norms = [vectors[parts + i] for i in range(6)]
    return (
        joined.reshape(tokens.shape),
        text_grad.reshape(tokens.shape),
        patch_grad,
        self_sum[: 3 * inner].reshape(3, inner, width).transpose(0, 2, 1),
        self_sum[3 * inner :],
        norms[0],
        norms[1],
        cross_sum[:inner].T,
        keyval_sum.reshape(2, inner, depth).transpose(0, 2, 1),
        cross_sum[inner:],
        norms[2],
        norms[3],
        expand_sum,
        bias_sum,
        shrink_sum,
        norms[4],
        norms[5],
    )


def solution(mesh):
    parts = mesh.shape["mp"]
    own = mesh.shape["dp"] == 8 and parts == 4
    return jax.shard_map(
        functools.partial(per_device, parts=parts, own=own),
        mesh=mesh,
        in_specs=(
            P(("dp", "mp"), None, None),
            P("dp", None, None),
            P("dp", None),
            P("dp"),
            P("dp", None),
            P(None, None, "mp"),
            P("mp", None),
            P(),
            P(),
            P(None, "mp"),
            P(None, None, "mp"),
            P("mp", None),
            P(),
            P(),
            P(None, "mp"),
            P("mp"),
            P("mp", None),
            P(),
            P(),
            P(("dp", "mp"), None, None),
        ),
        out_specs=(
            P(("dp", "mp"), None, None),
            P(("dp", "mp"), None, None),
            P("dp", None, "mp"),
            P(None, None, "mp"),
            P("mp", None),
            P(),
            P(),
            P(None, "mp"),
            P(None, None, "mp"),
            P("mp", None),
            P(),
            P(),
            P(None, "mp"),
            P("mp"),
            P("mp", None),
            P(),
            P(),
        ),
        check_vma=False,
    )
```

```python
import functools

import jax
import jax.numpy as jnp
from jax import lax
from jax.experimental import pallas as pl
from jax.experimental.pallas import tpu as pltpu
from jax.sharding import PartitionSpec as P

HEAD_DIM = 64
ROWS_MAX = 7
MESH = pl.DeviceIdType.MESH


def place():
    index = lax.axis_index("dp")
    plane = lax.axis_index("mp")
    y, x, c = index // 4, (index // 2) % 2, index % 2
    return index, plane, y, x, c


def partners(index, plane):
    core = (index + 1 - 2 * (index % 2), plane)
    across = (index + 2 - 4 * ((index // 2) % 2), plane)
    along = (index + 4 - 8 * (index // 4), plane)
    planes = [(index, lax.rem(plane + step, 4)) for step in (1, 2, 3)]
    return core, across, along, planes


def greet(peers):
    barrier = pltpu.get_barrier_semaphore()
    for peer in peers:
        pl.semaphore_signal(barrier, inc=1, device_id=peer, device_id_type=MESH)
    pl.semaphore_wait(barrier, len(peers))


class Sends:
    def __init__(self):
        self.stages, self.all = {}, []

    def start(self, name, k, items):
        copies = []
        for source, target, sends, recvs, peer in items:
            copy = pltpu.make_async_remote_copy(
                src_ref=source, dst_ref=target, send_sem=sends, recv_sem=recvs, device_id=peer, device_id_type=MESH
            )
            copy.start()
            copies.append(copy)
        self.stages[name, k] = copies
        self.all.extend(copies)

    def arrived(self, name, k):
        for copy in self.stages[name, k]:
            copy.wait_recv()

    def close(self):
        for copy in self.all:
            copy.wait_send()


class Gather:
    stages = 4

    def __init__(self, chunks, shards, wholes, sems, window, gap):
        self.chunks, self.shards, self.wholes, self.window = chunks, shards, wholes, window
        self.sems, self.gap = sems, gap
        self.index, self.plane, self.y, self.x, self.c = place()
        self.core, self.across, self.along, self.planes = partners(self.index, self.plane)
        self.others = [lax.rem(self.plane + step, 4) for step in (1, 2, 3)]
        self.sends = Sends()

    def sizes(self, k):
        which, base, rows = self.chunks[k]
        return which, base, rows // 8, self.wholes[which].shape[2] // 2

    def level(self, k):
        which, base, r, w = self.sizes(k)
        _, _, send, recv = self.sems[:4]
        self.own(which)
        items = []
        for h, first in enumerate((self.x * 2 + self.y, self.y * 2 + self.x)):
            here = (pl.ds(pl.multiple_of(base + (self.c * 4 + first) * r, 16), r), pl.ds(h * w, w))
            for j, peer in enumerate(self.planes):
                piece = self.wholes[which].at[(self.plane,) + here]
                items.append((piece, piece, send.at[k, h, j], recv.at[k, h, j], peer))
        self.sends.start("level", k, items)

    def near(self, k):
        which, base, r, w = self.sizes(k)
        send, recv = self.sems[4:6]
        self.sends.arrived("level", k)
        if k + self.window < len(self.chunks):
            self.level(k + self.window)
        items = []
        for h, first in enumerate((self.x * 2 + self.y, self.y * 2 + self.x)):
            row = pl.multiple_of(base + (self.c * 4 + first) * r, 16)
            for j, other in enumerate(self.others):
                piece = self.wholes[which].at[other, pl.ds(row, r), pl.ds(h * w, w)]
                items.append((piece, piece, send.at[k, h, j], recv.at[k, h, j], (self.along, self.across)[h]))
        self.sends.start("near", k, items)

    def far(self, k):
        which, base, r, w = self.sizes(k)
        send, recv = self.sems[6:8]
        self.sends.arrived("near", k)
        items = []
        for h, first in enumerate((self.x, self.y)):
            row = pl.multiple_of(base + (self.c * 4 + first * 2) * r, 16)
            for j, other in enumerate(self.others):
                piece = self.wholes[which].at[other, pl.ds(row, 2 * r), pl.ds(h * w, w)]
                items.append((piece, piece, send.at[k, h, j], recv.at[k, h, j], (self.across, self.along)[h]))
        self.sends.start("far", k, items)

    def cross(self, k):
        which, base, r, w = self.sizes(k)
        send, recv = self.sems[8:10]
        self.sends.arrived("far", k)
        row = pl.multiple_of(base + self.c * 4 * r, 16)
        items = []
        for j, other in enumerate(self.others):
            piece = self.wholes[which].at[other, pl.ds(row, 4 * r), :]
            items.append((piece, piece, send.at[k, j], recv.at[k, j], self.core))
        self.sends.start("core", k, items)

    def own(self, which):
        for copy in self.local.pop(which, ()):
            copy.wait()

    def begin(self):
        self.local = {}
        for which, pieces in enumerate(self.shards):
            row, self.local[which] = 0, []
            for i, piece in enumerate(pieces):
                target = self.wholes[which].at[self.plane, pl.ds(row, piece.shape[0]), :]
                copy = pltpu.make_async_copy(piece, target, self.sems[0].at[which, i])
                copy.start()
                self.local[which].append(copy)
                row += piece.shape[0]
        greet([self.core, self.across, self.along] + self.planes)
        for k in range(self.window):
            self.level(k)

    def step(self, t):
        if 0 <= t - 2 * self.gap < len(self.chunks):
            self.cross(t - 2 * self.gap)
        if 0 <= t - self.gap < len(self.chunks):
            self.far(t - self.gap)
        if 0 <= t < len(self.chunks):
            self.near(t)

    @property
    def steps(self):
        return len(self.chunks) + 2 * self.gap

    def ready(self, k):
        self.sends.arrived("core", k)

    @staticmethod
    def scratch(count, total):
        dma = pltpu.SemaphoreType.DMA
        return [dma((count, 2)), dma((count,))] + [dma((total, 2, 3))] * 6 + [dma((total, 3))] * 2


class Ticks:
    def __init__(self, gather, outs, sem):
        self.gather, self.outs, self.sem = gather, outs, sem
        self.now, self.done, self.final = 0, 0, []

    def __call__(self):
        gather, total = self.gather, len(self.gather.chunks)
        if self.now < gather.steps:
            gather.step(self.now)
        k = self.now - 3 * gather.gap
        if 0 <= k < total:
            gather.ready(k)
            self.done = k + 1
            which = gather.chunks[k][0]
            if k + 1 == total or gather.chunks[k + 1][0] != which:
                copy = pltpu.make_async_copy(gather.wholes[which], self.outs[which], self.sem.at[which])
                copy.start()
                self.final.append(copy)
        self.now += 1

    def wait(self, which):
        last = max(k for k, chunk in enumerate(self.gather.chunks) if chunk[0] == which)
        while self.done <= last:
            self()

    def close(self):
        while self.done < len(self.gather.chunks):
            self()
        self.gather.sends.close()
        for copy in self.final:
            copy.wait()


def forward_kernel(chunks, pieces, count, *refs):
    counts, lengths, tokens, boxes = refs[:4]
    vectors, cells_far, refs = refs[4:11], refs[11], refs[12:]
    shards, arrays = [], len(pieces)
    for amount in pieces:
        shards.append(refs[:amount])
        refs = refs[amount:]
    image, outs, biases, refs = refs[0], refs[1 : arrays + 1], refs[arrays + 1], refs[arrays + 2 :]
    far, refs = refs[: count + 1], refs[count + 1 :]
    wholes, refs = refs[:arrays], refs[arrays:]
    saved = [Slot(far[i], refs[2 * i], refs[2 * i + 1]) for i in range(count + 1)]
    *saved, near = saved
    refs = refs[2 * count + 2 :]
    (wide, cells_all, cell_ok, norms, caption, bias_send, bias_recv, cells_sem), sems = refs[:8], refs[8:]
    gather = Gather(chunks, shards, wholes, sems, 3, 1)
    copy = pltpu.make_async_copy(cells_far, cells_all, cells_sem)
    copy.start()
    gather.begin()
    copy.wait()
    prepare(counts, lengths, boxes, vectors, cells_all, image, caption, cell_ok, norms, near.near, gather.plane)
    near.flush()
    gather.sends.start(
        "bias", 0, [(norms, biases.at[gather.plane], bias_send.at[j], bias_recv.at[j], peer) for j, peer in enumerate(gather.planes)]
    )
    biases[gather.plane] = norms[...]
    ticks = Ticks(gather, outs, sems[1])
    rows = cell_ok.shape[0]
    forward_steps(
        ticks, image, caption, lambda r: lengths[gather.plane * rows + r], tokens, near.near, cell_ok, wholes[:3], norms, saved,
        wide,
    )
    gather.sends.arrived("bias", 0)
    ticks.close()
    for slot in saved + [near]:
        slot.finish()


def gather_forward(scalars, inputs, cells_all, shards, outputs, near, chunks):
    dma, bf16, f32, arrays, count = pltpu.SemaphoreType.DMA, jnp.bfloat16, jnp.float32, len(shards), len(outputs)
    any_space, vmem = pl.BlockSpec(memory_space=pl.ANY), pl.BlockSpec(memory_space=pltpu.VMEM)
    smem = pl.BlockSpec(memory_space=pltpu.SMEM)
    tokens = inputs[0]
    width = tokens.shape[1]
    rows, padded = tokens.shape[0] // 40, near[0][1]
    shapes = [(4, sum(piece.shape[0] for piece in pieces), pieces[0].shape[1]) for pieces in shards]
    flat = [piece for pieces in shards for piece in pieces]
    outputs = outputs + [near]
    results = pl.pallas_call(
        functools.partial(forward_kernel, chunks, [len(pieces) for pieces in shards], count),
        out_shape=[jax.ShapeDtypeStruct((rows,), jnp.int32)]
        + [jax.ShapeDtypeStruct(shape, bf16) for shape in shapes]
        + [jax.ShapeDtypeStruct((4, 8, width), f32)]
        + [jax.ShapeDtypeStruct(shape, kind) for shape, kind in outputs],
        in_specs=[smem] * len(scalars) + [vmem] * len(inputs) + [any_space] * (len(flat) + 1),
        out_specs=[smem] + [any_space] * arrays + [vmem] + [any_space] * (count + 1),
        scratch_shapes=[pltpu.VMEM(shape, bf16) for shape in shapes]
        + [entry for shape, kind in outputs for entry in slot_scratch(shape, kind)]
        + [pltpu.VMEM(tokens.shape, f32), pltpu.VMEM(cells_all.shape, bf16), pltpu.VMEM((rows, padded), f32)]
        + [pltpu.VMEM((8, width), f32), pltpu.SMEM((rows,), jnp.int32)]
        + [dma((3,)), dma((3,)), dma(())]
        + Gather.scratch(arrays, len(chunks)),
        compiler_params=pltpu.CompilerParams(collective_id=0, has_side_effects=True, vmem_limit_bytes=63 << 20),
        name="gather_forward",
    )(*scalars, *inputs, cells_all, *flat)
    return results[0], results[1 : arrays + 1], results[arrays + 1], results[arrays + 2 : -1], results[-1]


class Alone:
    def __call__(self):
        pass

    def wait(self, which):
        pass


def lone_forward_kernel(scalars, inputs, outputs, scratch):
    tokens, boxes, *vectors, cells_all, self_weights, cross_weights, keyval = (slot.ready() for slot in inputs)
    *saved, near = outputs
    counts, lengths, image = scalars
    wide, cell_ok, norms, caption = scratch
    rows, plane = cell_ok.shape[0], lax.axis_index("mp")
    prepare(counts, lengths, boxes, vectors, cells_all, image, caption, cell_ok, norms, near.near, plane)
    near.flush()
    forward_steps(
        Alone(), image, caption, lambda r: lengths[plane * rows + r], tokens, near.near, cell_ok,
        (self_weights, cross_weights, keyval), norms, saved, wide,
    )


class Reduce:
    def __init__(self, chunks, grads, sums, buffers, sems, local):
        self.chunks, self.grads, self.sums, self.sems, self.local = chunks, grads, sums, sems, local
        self.mine, self.core_in, self.near_in, self.far_in, self.plane_in = [], [], [], [], []
        buffers = list(buffers)
        self.index, self.plane, self.y, self.x, self.c = place()
        for which, base, rows in chunks:
            if which in local:
                self.mine.append((local[which], base + self.c * (rows // 2)))
            else:
                self.mine.append((buffers.pop(0), 0))
            self.core_in.append(buffers.pop(0))
            self.near_in.append(buffers.pop(0))
            self.far_in.append(buffers.pop(0))
            self.plane_in.append(buffers.pop(0))
        self.core, self.across, self.along, self.planes = partners(self.index, self.plane)
        self.others = [lax.rem(self.plane + step, 4) for step in (1, 2, 3)]
        self.sends = Sends()
        self.fetched, self.final = {}, []
        self.order = [self.begin, self.near, self.far, self.level, self.out_near, self.out_far, self.out_core, self.end]

    @staticmethod
    def scratch(chunks, widths, local):
        low, dma, total = jnp.bfloat16, pltpu.SemaphoreType.DMA, len(chunks)
        shapes = []
        for which, _, r in chunks:
            w = widths[which]
            shapes += [] if which in local else [(4, r // 2, w)]
            shapes += [(4, r // 2, w), (2, 4, r // 4, w // 2), (2, 4, r // 8, w // 2), (2, 3, r // 8, w // 2)]
        sems = [dma((total,))] * 4 + [dma((total, 2))] * 8 + [dma((total, 2, 3))] * 2 + [dma((total,))] * 2
        return [pltpu.VMEM(shape, low) for shape in shapes], sems

    def sizes(self, k):
        which, base, rows = self.chunks[k]
        return which, base, rows // 8, self.grads[which].shape[2] // 2

    @staticmethod
    def add(total, total_row, total_col, part, part_col, rows, cols):
        @pl.loop(0, rows // 16)
        def _(i):
            here = (pl.ds(pl.multiple_of(total_row + i * 16, 16), 16), pl.ds(total_col, cols))
            there = (pl.ds(pl.multiple_of(i * 16, 16), 16), pl.ds(part_col, cols))
            ours = [total[(shard,) + here].astype(jnp.float32) for shard in range(4)]
            theirs = [part[(shard,) + there].astype(jnp.float32) for shard in range(4)]
            sums = [(left + right).astype(jnp.bfloat16) for left, right in zip(ours, theirs)]
            for shard in range(4):
                total[(shard,) + here] = sums[shard]

    def places(self, r, w):
        return [((self.x * 2 + self.y) * r, 0), ((self.y * 2 + self.x) * r, w)]

    def begin(self, k):
        which, base, r, w = self.sizes(k)
        theirs = pl.multiple_of(base + (1 - self.c) * 4 * r, 16)
        ours = pl.multiple_of(base + self.c * 4 * r, 16)
        source = self.grads[which].at[:, pl.ds(theirs, 4 * r), :]
        self.sends.start("core", k, [(source, self.core_in[k], self.sems[0].at[k], self.sems[1].at[k], self.core)])
        if which not in self.local:
            source = self.grads[which].at[:, pl.ds(ours, 4 * r), :]
            self.fetched[k] = pltpu.make_async_copy(source, self.mine[k][0], self.sems[2].at[k])
            self.fetched[k].start()

    def near(self, k):
        which, base, r, w = self.sizes(k)
        mine, offset = self.mine[k]
        if k in self.fetched:
            self.fetched[k].wait()
        self.sends.arrived("core", k)
        items = []
        for h, (bit, peer) in enumerate([(self.x, self.across), (self.y, self.along)]):
            self.add(mine, offset, h * w, self.core_in[k], h * w, 4 * r, w)
            row = pl.multiple_of(offset + (1 - bit) * 2 * r, 16)
            source = mine.at[:, pl.ds(row, 2 * r), pl.ds(h * w, w)]
            items.append((source, self.near_in[k].at[h], self.sems[4].at[k, h], self.sems[5].at[k, h], peer))
        self.sends.start("near", k, items)

    def far(self, k):
        which, base, r, w = self.sizes(k)
        mine, offset = self.mine[k]
        self.sends.arrived("near", k)
        items = []
        for h, (bit, second, peer) in enumerate([(self.x, self.y, self.along), (self.y, self.x, self.across)]):
            row = offset + bit * 2 * r
            self.add(mine, row, h * w, self.near_in[k].at[h], 0, 2 * r, w)
            row = pl.multiple_of(row + (1 - second) * r, 16)
            source = mine.at[:, pl.ds(row, r), pl.ds(h * w, w)]
            items.append((source, self.far_in[k].at[h], self.sems[6].at[k, h], self.sems[7].at[k, h], peer))
        self.sends.start("far", k, items)

    def level(self, k):
        which, base, r, w = self.sizes(k)
        mine, offset = self.mine[k]
        self.sends.arrived("far", k)
        items = []
        for h, (row, col) in enumerate(self.places(r, w)):
            self.add(mine, offset + row, col, self.far_in[k].at[h], 0, r, w)
            row = pl.multiple_of(offset + row, 16)
            for j in range(3):
                source = mine.at[self.others[j], pl.ds(row, r), pl.ds(col, w)]
                items.append(
                    (source, self.plane_in[k].at[h, j], self.sems[12].at[k, h, j], self.sems[13].at[k, h, j], self.planes[j])
                )
        self.sends.start("level", k, items)

    def out_near(self, k):
        which, base, r, w = self.sizes(k)
        mine, offset = self.mine[k]
        self.sends.arrived("level", k)
        items = []
        for h, (row, col) in enumerate(self.places(r, w)):

            @pl.loop(0, r // 16)
            def _(i):
                step = pl.ds(pl.multiple_of(i * 16, 16), 16)
                here = pl.ds(pl.multiple_of(offset + row + i * 16, 16), 16)
                total = mine[self.plane, here, pl.ds(col, w)].astype(jnp.float32)
                for j in range(3):
                    total = total + self.plane_in[k][h, j, step, :].astype(jnp.float32)
                here = pl.ds(pl.multiple_of(row + i * 16, 16), 16)
                self.core_in[k][0, here, pl.ds(col, w)] = total.astype(jnp.bfloat16)

            piece = self.core_in[k].at[0, pl.ds(pl.multiple_of(row, 16), r), pl.ds(col, w)]
            peer = (self.along, self.across)[h]
            items.append((piece, piece, self.sems[8].at[k, h], self.sems[9].at[k, h], peer))
        self.sends.start("out_near", k, items)

    def out_far(self, k):
        which, base, r, w = self.sizes(k)
        self.sends.arrived("out_near", k)
        items = []
        for h, (bit, peer) in enumerate([(self.x, self.across), (self.y, self.along)]):
            piece = self.core_in[k].at[0, pl.ds(pl.multiple_of(bit * 2 * r, 16), 2 * r), pl.ds(h * w, w)]
            items.append((piece, piece, self.sems[10].at[k, h], self.sems[11].at[k, h], peer))
        self.sends.start("out_far", k, items)

    def out_core(self, k):
        which, base, r, w = self.sizes(k)
        self.sends.arrived("out_far", k)
        target = self.sums[which].at[pl.ds(pl.multiple_of(base + self.c * 4 * r, 16), 4 * r), :]
        source = self.core_in[k].at[0]
        self.sends.start("out_core", k, [(source, target, self.sems[14].at[k], self.sems[15].at[k], self.core)])
        copy = pltpu.make_async_copy(source, target, self.sems[3].at[k])
        copy.start()
        self.final.append(copy)

    def end(self, k):
        self.sends.arrived("out_core", k)

    @property
    def steps(self):
        return len(self.chunks) + len(self.order) - 1

    def step(self, t):
        for s in reversed(range(len(self.order))):
            if 0 <= t - s < len(self.chunks):
                self.order[s](t - s)

    def close(self):
        self.sends.close()
        for copy in self.final:
            copy.wait()


class ReduceTicks:
    def __init__(self, reduce, vector_sum, vector_in, send, recv):
        self.reduce, self.vector_sum, self.vector_in, self.send, self.recv = reduce, vector_sum, vector_in, send, recv
        self.now = 0

    def __call__(self):
        if self.now < self.reduce.steps:
            self.reduce.step(self.now)
        self.now += 1

    def sum_vectors(self):
        reduce, total, arrived = self.reduce, self.vector_sum, self.vector_in
        for t, peer in enumerate((reduce.core, reduce.across, reduce.along)):
            reduce.sends.start("vector", t, [(total.at[t], arrived.at[t], self.send.at[t], self.recv.at[t], peer)])
            self()
            reduce.sends.arrived("vector", t)
            total[t + 1] = total[t] + arrived[t]
        items = [
            (total.at[3], arrived.at[3 + j], self.send.at[3 + j], self.recv.at[3 + j], peer)
            for j, peer in enumerate(reduce.planes)
        ]
        reduce.sends.start("vector", 3, items)
        self()
        reduce.sends.arrived("vector", 3)
        ordered = [arrived[3 + j] for j in range(3)]
        plane, own = reduce.plane, total[3]
        slots = []
        for m in range(4):
            value = own
            for j in range(3):
                value = jnp.where(reduce.others[j] == m, ordered[j], value)
            slots.append(value)
        total[4] = (slots[0] + slots[1]) + (slots[2] + slots[3])


class Patches:
    def __init__(self, patch, windows, merged, buffers, sems, index, plane):
        self.patch, self.windows, self.merged = patch, windows, merged
        self.relay, self.own, self.total = buffers
        self.sends, self.recvs, self.relay_recv, self.merged_recv, self.local, self.fetch = sems
        self.index, self.plane = index, plane
        self.outer = (plane == 0) | (plane == 3)
        self.first = plane < 2
        self.next = jnp.where(plane == 0, 1, 2)
        self.far = 3 - self.next
        self.edge = jnp.where(plane == 1, 0, 3)
        self.across = 3 - plane
        images = patch.shape[1]
        self.shift = self.total.shape[0] - images

    def copy(self, slot, source, target, recv, to):
        return pltpu.make_async_remote_copy(
            src_ref=source, dst_ref=target, send_sem=self.sends.at[slot], recv_sem=recv, device_id=(self.index, to),
            device_id_type=MESH,
        )

    def direct(self, slot, to):
        return self.copy(slot, self.patch.at[to], self.windows.at[self.plane], self.recvs.at[self.plane], to)

    def to_relay(self):
        return self.copy(1, self.patch.at[self.across], self.relay, self.relay_recv.at[0], self.next)

    def to_edge(self):
        return self.copy(1, self.total, self.merged, self.merged_recv.at[0], 3 - self.edge)

    def keep(self):
        return pltpu.make_async_copy(self.patch.at[self.plane], self.windows.at[self.plane], self.local.at[0])

    def take(self):
        return pltpu.make_async_copy(self.patch.at[3 - self.edge], self.own, self.fetch.at[0])

    def begin(self):
        self.keep().start()

        @pl.when(self.outer)
        def _():
            self.to_relay().start()
            self.direct(0, self.far).start()

        @pl.when(jnp.logical_not(self.outer))
        def _():
            self.take().start()
            self.direct(0, self.across).start()

    def middle(self):
        images, shift = self.own.shape[0], self.shift

        @pl.when(self.outer)
        def _():
            self.direct(2, self.next).start()

        @pl.when(jnp.logical_not(self.outer))
        def _():
            self.direct(2, self.edge).start()
            self.take().wait()
            self.to_relay().wait_recv()

            @pl.when(self.first)
            def _():
                self.add(self.relay, self.own)

            @pl.when(jnp.logical_not(self.first))
            def _():
                self.add(self.own, self.relay)

            self.to_edge().start()

    def add(self, early, late):
        images, shift = early.shape[0], self.shift
        for i in range(images + shift):
            if i < shift:
                self.total[i] = early[i]
            elif i < images:
                both = early[i].astype(jnp.float32) + late[i - shift].astype(jnp.float32)
                self.total[i] = both.astype(jnp.bfloat16)
            else:
                self.total[i] = late[i - shift]

    def end(self):
        self.keep().wait()

        @pl.when(self.outer)
        def _():
            self.copy(0, self.patch.at[0], self.windows.at[self.next], self.recvs.at[self.next], self.next).wait_recv()
            self.copy(1, self.total, self.merged, self.merged_recv.at[0], self.far).wait_recv()
            self.to_relay().wait_send()
            self.direct(0, self.far).wait_send()
            self.direct(2, self.next).wait_send()

        @pl.when(jnp.logical_not(self.outer))
        def _():
            for source in (self.across, 0, 3):
                self.copy(0, self.patch.at[0], self.windows.at[source], self.recvs.at[source], self.across).wait_recv()
            self.direct(0, self.across).wait_send()
            self.to_edge().wait_send()
            self.direct(2, self.edge).wait_send()


def back_kernel(chunks, count, slots, *refs):
    grads, patch, early, refs = refs[:count], refs[count], refs[count + 1 : count + 3], refs[count + 3 :]
    inputs, refs = refs[:slots], refs[slots:]
    sums, refs = refs[: count + 1], refs[count + 1 :]
    (windows, merged, vector_sum, text_far), refs = refs[:4], refs[4:]
    inputs = [Slot(inputs[i], refs[2 * i], refs[2 * i + 1]) for i in range(slots)]
    refs = refs[2 * slots :]
    self_grad, text_sem, refs = refs[0], refs[1], refs[2:]
    scratch, refs = refs[:5], refs[5:]
    (vector_in, vector_send, vector_recv), patch_refs, refs = refs[:3], refs[3:12], refs[12:]
    sems, buffers = refs[:16], refs[16:]
    for slot in inputs:
        slot.fetch()
    reduce = Reduce(chunks, [self_grad, *grads], sums, buffers, sems, {0: self_grad})
    greet([reduce.core, reduce.across, reduce.along] + reduce.planes)
    ticks = ReduceTicks(reduce, vector_sum, vector_in, vector_send, vector_recv)
    ticks()
    patches = Patches(patch, windows, merged, patch_refs[:3], patch_refs[3:], reduce.index, reduce.plane)
    patches.begin()
    vector_sum[0] = early[0][...] + early[1][...]
    text_grad = inputs[0].near
    self_back_steps(ticks, inputs, self_grad, vector_sum.at[0], text_grad, scratch)
    text_copy = pltpu.make_async_copy(text_grad, text_far, text_sem.at[0])
    text_copy.start()
    ticks()
    patches.middle()
    ticks.sum_vectors()
    while ticks.now < reduce.steps:
        ticks()
    patches.end()
    reduce.close()
    text_copy.wait()


def reduce_back(grads, patch, early, inputs, shift, chunks):
    count, dma, f32, bf16 = len(grads), pltpu.SemaphoreType.DMA, jnp.float32, jnp.bfloat16
    any_space, vmem = pl.BlockSpec(memory_space=pl.ANY), pl.BlockSpec(memory_space=pltpu.VMEM)
    weights, flat = inputs[4].shape, inputs[0].shape
    together = (patch.shape[1] + shift,) + patch.shape[2:]
    widths = [weights[2]] + [grad.shape[2] for grad in grads]
    buffers, sems = Reduce.scratch(chunks, widths, {0})
    *sums, windows, merged, vector_sum, text_grad = pl.pallas_call(
        functools.partial(back_kernel, chunks, count, len(inputs)),
        out_shape=[jax.ShapeDtypeStruct(shape[1:], bf16) for shape in [weights] + [grad.shape for grad in grads]]
        + [jax.ShapeDtypeStruct(patch.shape, bf16), jax.ShapeDtypeStruct(together, bf16)]
        + [jax.ShapeDtypeStruct((5,) + early[0].shape, f32)]
        + [jax.ShapeDtypeStruct(flat, f32)],
        in_specs=[any_space] * (count + 1) + [vmem] * 2 + [any_space] * len(inputs),
        out_specs=[any_space] * (count + 3) + [vmem, any_space],
        scratch_shapes=[entry for array in inputs for entry in slot_scratch(array.shape, array.dtype)]
        + [pltpu.VMEM(weights, bf16), dma((1,))]
        + [pltpu.VMEM(flat, bf16)] * 5
        + [pltpu.VMEM((6,) + early[0].shape, f32), dma((6,)), dma((6,))]
        + [pltpu.VMEM(patch.shape[1:], bf16), pltpu.VMEM(patch.shape[1:], bf16), pltpu.VMEM(together, bf16)]
        + [dma((3,)), dma((4,)), dma((1,)), dma((1,)), dma((1,)), dma((1,))]
        + sems
        + buffers,
        compiler_params=pltpu.CompilerParams(collective_id=1, has_side_effects=True, vmem_limit_bytes=63 << 20),
        name="reduce_back",
    )(*grads, patch, *early, *inputs)
    return sums, windows, merged, vector_sum[4], text_grad


class Slot:
    def __init__(self, far, near, sem, parts=0):
        self.far, self.near, self.sem, self.parts, self.waited = far, near, sem, parts, False

    def copy(self, out, m=None):
        far, near = (self.far, self.near) if m is None else (self.far.at[m], self.near.at[m])
        sem = self.sem.at[0 if m is None else m]
        return pltpu.make_async_copy(near, far, sem) if out else pltpu.make_async_copy(far, near, sem)

    def fetch(self):
        for m in range(self.parts) if self.parts else (None,):
            self.copy(False, m).start()

    def ready(self):
        if not self.waited:
            self.waited = True
            for m in range(self.parts) if self.parts else (None,):
                self.copy(False, m).wait()
        return self.near

    def flush(self, m=None):
        self.copy(True, m).start()

    def finish(self):
        for m in range(self.parts) if self.parts else (None,):
            self.copy(True, m).wait()


def slot_scratch(shape, kind, parts=0):
    return [pltpu.VMEM(shape, kind), pltpu.SemaphoreType.DMA((max(parts, 1),))]


def on_slots(kernel, name, scalars, inputs, outputs, scratch, parts_in=(), parts_out=(), counted=0):
    count, total, given = len(inputs), len(inputs) + len(outputs), len(scalars)

    def body(*refs):
        scalar_refs, refs = refs[:given], refs[given:]
        far_in, refs = refs[:count], refs[count:]
        if counted:
            scalar_refs, refs = scalar_refs + refs[:1], refs[1:]
        far, refs = far_in + refs[: total - count], refs[total - count :]
        slots = []
        for i in range(total):
            parts = far[i].shape[0] if (i in parts_in if i < count else i - count in parts_out) else 0
            slots.append(Slot(far[i], refs[2 * i], refs[2 * i + 1], parts))
        for slot in slots[:count]:
            slot.fetch()
        kernel(scalar_refs, slots[:count], slots[count:], refs[2 * total :])
        for slot in slots[count:]:
            slot.finish()

    spaces = []
    for i, array in enumerate(inputs):
        spaces += slot_scratch(array.shape, array.dtype, array.shape[0] if i in parts_in else 0)
    for i, (shape, kind) in enumerate(outputs):
        spaces += slot_scratch(shape, kind, shape[0] if i in parts_out else 0)
    any_space, smem = pl.BlockSpec(memory_space=pl.ANY), pl.BlockSpec(memory_space=pltpu.SMEM)
    first = [jax.ShapeDtypeStruct((counted,), jnp.int32)] if counted else []
    return pl.pallas_call(
        body,
        out_shape=first + [jax.ShapeDtypeStruct(shape, kind) for shape, kind in outputs],
        in_specs=[smem] * given + [any_space] * count,
        out_specs=[smem] * len(first) + [any_space] * len(outputs),
        scratch_shapes=spaces + [entry if hasattr(entry, "memory_space") else pltpu.VMEM(*entry) for entry in scratch],
        compiler_params=pltpu.CompilerParams(vmem_limit_bytes=63 << 20),
        name=name,
    )(*scalars, *inputs)


def nn(left, right):
    return lax.dot_general(left, right, (((1,), (0,)), ((), ())), preferred_element_type=jnp.float32)


def nt(left, right):
    return lax.dot_general(left, right, (((1,), (1,)), ((), ())), preferred_element_type=jnp.float32)


def tn(left, right):
    return lax.dot_general(left, right, (((0,), (0,)), ((), ())), preferred_element_type=jnp.float32)


def part(ref, which):
    inner = ref.shape[2] // 4 if ref.shape[2] == 768 else 192
    return jnp.concatenate([ref[m, which * 192 : (which + 1) * 192, :] for m in range(4)], axis=0)


def store_part(ref, which, value):
    low = value.astype(jnp.bfloat16)
    for m in range(4):
        ref[m, which * 192 : (which + 1) * 192, :] = low[m * 192 : (m + 1) * 192]


def tiles(amount, step):
    def wrap(body):
        @pl.loop(0, amount // step)
        def _(i):
            body(pl.ds(pl.multiple_of(i * step, step), step))

    return wrap


def lanes():
    place = lax.broadcasted_iota(jnp.int32, (1, 2 * HEAD_DIM), 1)
    low = place < HEAD_DIM
    return low, low.astype(jnp.float32), 1.0 - low.astype(jnp.float32)


def norm_forward(total, unit, inverse, value, value_low, gain, shift):
    @tiles(total.shape[0], 80)
    def _(rows):
        hidden = total[rows, :]
        center = hidden - jnp.mean(hidden, axis=-1, keepdims=True)
        factor = lax.rsqrt(jnp.mean(center * center, axis=-1, keepdims=True) + 1e-06)
        scaled = center * factor
        result = scaled * gain[...] + shift[...]
        if unit is not None:
            unit[rows, :] = scaled
            inverse[rows, :] = jnp.broadcast_to(factor, (80, 128))
        if value is not None:
            value[rows, :] = result
        value_low[rows, :] = result.astype(jnp.bfloat16)


def norm_reverse(upstream, unit, inverse, gain, gain_grad, shift_grad, grad, grad_low):
    gain_grad[...] = jnp.zeros_like(gain_grad)
    shift_grad[...] = jnp.zeros_like(shift_grad)

    @tiles(upstream.shape[0], 80)
    def _(rows):
        up = upstream[rows, :].astype(jnp.float32)
        scaled = unit[rows, :]
        factor = inverse[rows, :][:, :1]
        gain_grad[...] += jnp.sum(up * scaled, axis=0, keepdims=True)
        shift_grad[...] += jnp.sum(up, axis=0, keepdims=True)
        inner = up * gain[...]
        result = factor * (
            inner
            - jnp.mean(inner, axis=-1, keepdims=True)
            - scaled * jnp.mean(inner * scaled, axis=-1, keepdims=True)
        )
        grad[rows, :] = result
        grad_low[rows, :] = result.astype(jnp.bfloat16)


def softmax(scores):
    raised = jnp.exp(scores - jnp.max(scores, axis=-1, keepdims=True))
    return (raised * (1.0 / jnp.sum(raised, axis=-1, keepdims=True))).astype(jnp.bfloat16)


def columns(width):
    return [slice(start, start + 128) for start in range(0, width, 128)]


def stack(value, first, second):
    return jnp.concatenate([value * first, value * second], axis=0)


def merge(low, value):
    half = value.shape[0] // 2
    return jnp.where(low, value[:half], value[half:])


def attend_self(queries, keys, values, lengths, probs, context):
    low, first, second = lanes()
    first, second = first.astype(jnp.bfloat16), second.astype(jnp.bfloat16)
    cols = columns(queries.shape[1])
    query = lax.broadcasted_iota(jnp.int32, (160, 80), 0)
    key = lax.broadcasted_iota(jnp.int32, (160, 80), 1)
    query = jnp.where(query >= 80, query - 80, query)
    same = (query < 40) == (key < 40)

    @pl.loop(0, queries.shape[0] // 80)
    def _(pair):
        rows = pl.ds(pl.multiple_of(pair * 80, 80), 80)
        allowed = same & (key < jnp.where(key < 40, lengths(2 * pair), lengths(2 * pair + 1) + 40))
        stacked = [stack(queries[rows, c], first, second) for c in cols]
        scores = [nt(both, keys[rows, c]) * HEAD_DIM ** (-0.5) for both, c in zip(stacked, cols)]
        weights = [softmax(jnp.where(allowed, score, -1000000000.0)) for score in scores]
        mixed = [merge(low, nn(weight, values[rows, c])) for weight, c in zip(weights, cols)]
        for tile, c in enumerate(cols):
            probs[pair, tile] = weights[tile]
            context[rows, c] = mixed[tile].astype(jnp.bfloat16)


def attend_cross(image, caption, wide, keys, values, cell_ok, probs, begin, end):
    low, first, second = lanes()
    cols = columns(wide.shape[1])

    @pl.loop(begin, end)
    def _(row):
        rows = pl.ds(pl.multiple_of(row * 40, 40), 40)
        which = image[row]
        cells = cell_ok[pl.ds(row, 1), :] + caption[row].astype(jnp.float32)
        allowed = jnp.broadcast_to(cells, (80, cell_ok.shape[1])) > 0
        stacked = [stack(wide[rows, c], first, second).astype(jnp.bfloat16) for c in cols]
        scores = [nt(both, keys[which, :, c]) * HEAD_DIM ** (-0.5) for both, c in zip(stacked, cols)]
        weights = [softmax(jnp.where(allowed, score, -1000000000.0)) for score in scores]
        mixed = [merge(low, nn(weight, values[which, :, c])) for weight, c in zip(weights, cols)]
        for tile, c in enumerate(cols):
            probs[row, tile] = weights[tile]
            wide[rows, c] = mixed[tile]


def prepare(counts, lengths, boxes, vectors, cells_all, image, caption, cell_ok, norms, near, plane):
    rows, padded = cell_ok.shape
    cells, images, _ = cells_all.shape
    window = near.shape[0]
    start = jnp.minimum(plane * rows // ROWS_MAX, images - window)

    @pl.loop(0, rows)
    def _(r):
        row = plane * rows + r
        end, here, before = jnp.int32(0), jnp.int32(0), jnp.int32(0)
        for i in range(images):
            end = end + counts[0, i]
            here = here + (end <= row).astype(jnp.int32)
            before = before + (end <= row - 1).astype(jnp.int32)
        image[r] = jnp.minimum(jnp.maximum(here - start, 0), window - 1)
        caption[r] = jnp.where(row == 0, jnp.int32(1), here - before)

    cell_ok[...] = jnp.full(cell_ok.shape, -2.0, jnp.float32)
    cell_ok[:, :cells] = (boxes[pl.ds(pl.multiple_of(plane * rows, 8), rows), :] > 0).astype(jnp.float32)
    norms[...] = jnp.zeros_like(norms)
    for i, vector in enumerate(vectors):
        norms[pl.ds(i, 1), :] = vector[...].reshape(1, norms.shape[1])
    step = 16
    for first in range(0, padded, step):
        amount = min(step, cells - first)
        to = lax.broadcasted_iota(jnp.int32, (window * step, amount * images), 0)
        source = lax.broadcasted_iota(jnp.int32, (window * step, amount * images), 1)
        pick = (source // images == to % step) & (source % images == to // step + start)
        block = cells_all[first : first + amount].reshape(amount * images, cells_all.shape[2])
        block = nn(pick.astype(jnp.bfloat16), block).astype(jnp.bfloat16)
        near[:, first : first + step, :] = block.reshape(window, step, cells_all.shape[2])


def forward_steps(ticks, image, caption, lengths, tokens, near, cell_ok, weights, norms, saved, wide):
    bf16 = jnp.bfloat16
    self_weights, cross_weights, keyval = weights
    (
        queries, keys, values, self_probs, self_context, first_unit, first_inverse, first_low, cross_queries, image_keys,
        image_values, cross_probs, cross_context, second_unit, second_inverse, second_value, second_low,
    ) = (slot.near for slot in saved)

    def flush(*places):
        for place in places:
            saved[place].flush()

    gains = [norms.at[pl.ds(i, 1), :] for i in range(4)]
    ticks.wait(0)
    for target, which in ((queries, 0), (keys, 1), (values, 2)):
        target[...] = nt(tokens[...], part(self_weights, which)).astype(bf16)
    flush(0, 1, 2)
    ticks()
    attend_self(queries, keys, values, lengths, self_probs, self_context)
    flush(3, 4)
    ticks()
    second_value[...] = nn(self_context[...], part(self_weights, 3)) + tokens[...].astype(jnp.float32)
    norm_forward(second_value, first_unit, first_inverse, None, first_low, gains[0], gains[1])
    flush(5, 6, 7)
    ticks.wait(1)
    cross_queries[...] = nt(first_low[...], part(cross_weights, 0)).astype(bf16)
    flush(8)
    wide[...] = cross_queries[...].astype(jnp.float32)
    images, cells, depth = near.shape
    half = images // 2
    ticks.wait(2)
    for target, which in ((image_keys, 0), (image_values, 1)):
        weight = part(keyval, which)
        for step in range(2):
            block = near[step * half : (step + 1) * half].reshape(half * cells, depth)
            target[step * half : (step + 1) * half] = nt(block, weight).astype(bf16).reshape(half, cells, -1)
        flush(9 + which)
    ticks()
    rows = cell_ok.shape[0]
    for part_of in range(2):
        begin, end = part_of * rows // 2, (part_of + 1) * rows // 2
        attend_cross(image, caption, wide, image_keys, image_values, cell_ok, cross_probs, begin, end)
        ticks()
    flush(11)
    cross_context[...] = wide[...].astype(bf16)
    flush(12)
    second_value[...] = nn(cross_context[...], part(cross_weights, 1)) + (first_unit[...] * gains[0][...] + gains[1][...])
    norm_forward(second_value, second_unit, second_inverse, second_value, second_low, gains[2], gains[3])
    flush(13, 14, 15, 16)


def feed_kernel(scalars, inputs, outputs, scratch):
    second_value, second_low, norms, expand, shrink, cotangent = inputs
    joined, expand_grad, shrink_grad, vectors, second_up = outputs
    active, slope, unit, inverse, feed_low = scratch
    bf16 = jnp.bfloat16
    total = second_up.near
    total[...] = second_value.ready()[...]
    second_low, norms = second_low.ready(), norms.ready()
    gain, shift = norms.at[0, pl.ds(4, 1), :], norms.at[0, pl.ds(5, 1), :]
    hidden, amount = expand.near.shape[0], total.shape[0]
    halves = [slice(0, amount // 2), slice(amount // 2, amount)]

    @pl.loop(0, hidden)
    def _(m):
        expand.copy(False, m).wait()
        shrink.copy(False, m).wait()
        inners = [nn(second_low[rows, :], expand.near[m]) + norms[m, pl.ds(6, 1), :] for rows in halves]
        shares = [0.5 * (1.0 + lax.erf(inner * 0.5**0.5)) for inner in inners]
        acts = [(inner * share).astype(bf16) for inner, share in zip(inners, shares)]
        slopes = [
            (share + inner * (jnp.exp(-0.5 * inner * inner) * 0.3989422804014327)).astype(bf16)
            for inner, share in zip(inners, shares)
        ]
        for rows, act, inclination in zip(halves, acts, slopes):
            active[m, rows, :] = act
            slope[m, rows, :] = inclination
            total[rows, :] += nn(act, shrink.near[m])

    norm_forward(total, unit, inverse, None, joined.near, gain, shift)
    joined.flush()
    sums = vectors.near
    sums[...] = jnp.zeros_like(sums)
    norm_reverse(
        cotangent.ready(), unit, inverse, gain, sums.at[pl.ds(8, 1), :], sums.at[pl.ds(9, 1), :], total, feed_low
    )

    @pl.loop(0, hidden)
    def _(m):
        shrink_grad.near[m] = tn(active[m], feed_low[...]).astype(bf16)
        shrink_grad.flush(m)
        lows = [
            (nt(feed_low[rows, :], shrink.near[m]) * slope[m, rows, :].astype(jnp.float32)).astype(bf16) for rows in halves
        ]
        parts = [jnp.sum(low.astype(jnp.float32), axis=0, keepdims=True) for low in lows]
        sums[pl.ds(m, 1), :] = parts[0] + parts[1]
        for rows, low in zip(halves, lows):
            active[m, rows, :] = low
        expand_grad.near[m] = tn(second_low[...], active[m]).astype(bf16)
        expand_grad.flush(m)
        total[...] += nt(active[m], expand.near[m])

    vectors.flush()
    second_up.flush()


def score_back(weights, upstream):
    probs = weights.astype(jnp.float32)
    return (probs * (upstream - jnp.sum(probs * upstream, axis=-1, keepdims=True))).astype(jnp.bfloat16)


def cross_back_kernel(scalars, inputs, outputs, scratch):
    (image,) = scalars
    (
        second_up, second_unit, second_inverse, norms, cross_weights, cross_context, cross_queries, image_values,
        image_keys, cross_probs, first_low, keyval, near,
    ) = inputs
    weights_grad, keyval_grad, patch, vectors, first_up = outputs
    grad_low, wide, turn, key_sum, value_sum, query_low = scratch
    bf16 = jnp.bfloat16
    low, first, second = lanes()
    sums = vectors.near
    sums[...] = jnp.zeros_like(sums)
    norm_reverse(
        second_up.ready(), second_unit.ready(), second_inverse.ready(), norms.ready().at[0, pl.ds(2, 1), :],
        sums.at[pl.ds(6, 1), :], sums.at[pl.ds(7, 1), :], first_up.near, grad_low,
    )
    vectors.flush()
    cross_weights = cross_weights.ready()
    wide[...] = nt(grad_low[...], part(cross_weights, 1)).astype(bf16).astype(jnp.float32)
    store_part(weights_grad.near, 1, tn(cross_context.ready()[...], grad_low[...]))
    turn[...] = cross_queries.ready()[...].astype(jnp.float32)
    key_sum[...] = jnp.zeros_like(key_sum)
    value_sum[...] = jnp.zeros_like(value_sum)
    cols = columns(wide.shape[1])
    image_values, image_keys, cross_probs = image_values.ready(), image_keys.ready(), cross_probs.ready()

    @pl.loop(0, cross_probs.shape[0])
    def _(row):
        rows = pl.ds(pl.multiple_of(row * 40, 40), 40)
        which = image[row]
        queries = [stack(turn[rows, c], first, second).astype(bf16) for c in cols]
        grads = [stack(wide[rows, c], first, second).astype(bf16) for c in cols]
        weights = [cross_probs[row, tile] for tile in range(len(cols))]
        upstream = [nt(grad, image_values[which, :, c]) for grad, c in zip(grads, cols)]
        back = [score_back(weight, up) for weight, up in zip(weights, upstream)]
        mixed = [merge(low, nn(grad, image_keys[which, :, c])) * HEAD_DIM ** (-0.5) for grad, c in zip(back, cols)]
        key_parts = [tn(grad, both) * HEAD_DIM ** (-0.5) for grad, both in zip(back, queries)]
        value_parts = [tn(weight, grad) for weight, grad in zip(weights, grads)]
        for tile, c in enumerate(cols):
            turn[rows, c] = mixed[tile]
        for tile, c in enumerate(cols):
            key_sum[which, :, c] += key_parts[tile]
        for tile, c in enumerate(cols):
            value_sum[which, :, c] += value_parts[tile]

    keyval, near = keyval.ready(), near.ready()
    images, cells, depth = near.shape
    amount = images * cells
    for step in range(2):
        here = slice(step * (images // 2), (step + 1) * (images // 2))
        block = nn(key_sum[here].astype(bf16).reshape(amount // 2, -1), part(keyval, 0))
        block += nn(value_sum[here].astype(bf16).reshape(amount // 2, -1), part(keyval, 1))
        block = block.astype(bf16)
        quarter = patch.near.shape[3]
        for m in range(patch.near.shape[0]):
            patch.near[m, here] = block[:, m * quarter : (m + 1) * quarter].reshape(images // 2, cells, quarter)
    patch.flush()
    for source, which in ((key_sum, 0), (value_sum, 1)):
        flat = source[...].astype(bf16).reshape(amount, -1)
        store_part(keyval_grad.near, which, tn(flat, near[...].reshape(amount, depth)))
    keyval_grad.flush()
    query_low[...] = turn[...].astype(bf16)
    first_up.near[...] += nn(query_low[...], part(cross_weights, 0))
    first_up.flush()
    store_part(weights_grad.near, 0, tn(query_low[...], first_low.ready()[...]))
    weights_grad.flush()


def self_back_steps(ticks, inputs, weights_grad, sums, text_grad, scratch):
    (
        first_up, first_unit, first_inverse, norms, self_weights, self_context, queries, keys, values, self_probs, tokens,
    ) = inputs
    grad_low, context_low, query_low, key_low, value_low = scratch
    bf16 = jnp.bfloat16
    low, first, second = lanes()
    first_mask, second_mask = first.astype(bf16), second.astype(bf16)
    norm_reverse(
        first_up.ready(), first_unit.ready(), first_inverse.ready(), norms.ready().at[0, pl.ds(0, 1), :],
        sums.at[pl.ds(4, 1), :], sums.at[pl.ds(5, 1), :], text_grad, grad_low,
    )
    self_weights = self_weights.ready()
    context_low[...] = nt(grad_low[...], part(self_weights, 3)).astype(bf16)
    store_part(weights_grad, 3, tn(self_context.ready()[...], grad_low[...]))
    cols = columns(context_low.shape[1])
    queries, keys, values, self_probs = queries.ready(), keys.ready(), values.ready(), self_probs.ready()
    ticks()

    @pl.loop(0, self_probs.shape[0])
    def _(pair):
        rows = pl.ds(pl.multiple_of(pair * 80, 80), 80)
        stacked = [stack(queries[rows, c], first_mask, second_mask) for c in cols]
        grads = [stack(context_low[rows, c], first_mask, second_mask) for c in cols]
        weights = [self_probs[pair, tile] for tile in range(len(cols))]
        upstream = [nt(grad, values[rows, c]) for grad, c in zip(grads, cols)]
        back = [score_back(weight, up) for weight, up in zip(weights, upstream)]
        query_parts = [merge(low, nn(grad, keys[rows, c])) * HEAD_DIM ** (-0.5) for grad, c in zip(back, cols)]
        key_parts = [tn(grad, both) * HEAD_DIM ** (-0.5) for grad, both in zip(back, stacked)]
        value_parts = [tn(weight, grad) for weight, grad in zip(weights, grads)]
        for tile, c in enumerate(cols):
            query_low[rows, c] = query_parts[tile].astype(bf16)
            key_low[rows, c] = key_parts[tile].astype(bf16)
            value_low[rows, c] = value_parts[tile].astype(bf16)

    ticks()
    tokens = tokens.ready()
    for source, which in ((query_low, 0), (key_low, 1), (value_low, 2)):
        store_part(weights_grad, which, tn(source[...], tokens[...]))
        text_grad[...] += nn(source[...], part(self_weights, which))


def lone_self_back_kernel(scalars, inputs, outputs, scratch):
    weights_grad, vectors, text_grad = outputs
    vectors.near[...] = jnp.zeros_like(vectors.near)
    self_back_steps(Alone(), inputs, weights_grad.near, vectors.near, text_grad.near, scratch)
    for slot in outputs:
        slot.flush()


def finish_kernel(alone, scalars, inputs, outputs, scratch):
    self_sum, cross_sum, keyval_sum, expand_sum, shrink_sum, vectors, windows, merged = inputs
    project, self_out, query, cross_out, keyval, expand, shrink, patch_grad, *norms, bias = outputs
    inner = self_out.near.shape[0]

    def give(output, value):
        output.near[...] = value.astype(jnp.float32)
        output.flush()

    give(shrink, shrink_sum.ready()[...])
    give(expand, expand_sum.ready()[...])
    give(project, self_sum.ready()[: 3 * inner, :])
    give(self_out, self_sum.near[3 * inner :, :])
    give(query, cross_sum.ready()[:inner, :])
    give(cross_out, cross_sum.near[inner:, :])
    give(keyval, keyval_sum.ready()[...])
    sums = vectors.ready()
    for i, output in enumerate(norms):
        give(output, sums[4 + i : 5 + i, :].reshape(sums.shape[1]))
    plane = lax.axis_index("mp")
    give(bias, sums[pl.ds(plane, 1), :].reshape(sums.shape[1]))
    windows, merged = windows.ready(), merged.ready()
    cells, images, quarter = patch_grad.near.shape
    amount, step, rows = windows.shape[1], 16, scalars[0].shape[0]

    def first_image(m):
        return jnp.minimum(m * rows // ROWS_MAX, images - amount)

    def place(sources):
        for first in range(0, cells, step):
            size = min(step, cells - first)
            total = jnp.zeros((size * images, quarter), jnp.float32)
            for window, start in sources:
                count = window.shape[0]
                to = lax.broadcasted_iota(jnp.int32, (size * images, count * step), 0)
                source = lax.broadcasted_iota(jnp.int32, (size * images, count * step), 1)
                pick = (to // images == source % step) & (to % images == source // step + start)
                block = window[:, first : first + step, :].reshape(count * step, quarter)
                total = total + nn(pick.astype(jnp.bfloat16), block)
            patch_grad.near[first : first + size] = total.reshape(size, images, quarter)

    if alone:
        place([(windows.at[m], first_image(m)) for m in range(4)])
    else:
        outer = (plane == 0) | (plane == 3)

        @pl.when(outer)
        def _():
            beside = jnp.where(plane == 0, 1, 2)
            place(
                [(windows.at[m], first_image(m)) for m in (plane, beside)]
                + [(merged, jnp.where(plane == 0, first_image(2), first_image(0)))]
            )

        @pl.when(jnp.logical_not(outer))
        def _():
            place([(windows.at[m], first_image(m)) for m in range(4)])

    patch_grad.flush()


def image_windows(parts, rows, group_images):
    group_rows = parts * rows
    first = [m * rows // ROWS_MAX for m in range(parts)]
    last = [group_images - 1 - max(0, -(-(group_rows - (m + 1) * rows - (ROWS_MAX - 1)) // ROWS_MAX)) for m in range(parts)]
    last = [min(stop, (m + 1) * rows - 1) for m, stop in enumerate(last)]
    window = max(stop - start + 1 for start, stop in zip(first, last))
    return [min(start, group_images - window) for start in first], window


def forward(scalars, inputs, cells_all, shards, outputs, near, chunks, own):
    if own:
        return gather_forward(scalars, inputs, cells_all, shards, outputs, near, chunks)
    weights = [lax.all_gather(jnp.concatenate(pieces, axis=0), "mp", axis=0) for pieces in shards]
    vectors = jnp.stack(inputs[2:] + [jnp.zeros_like(inputs[2])])
    biases = lax.all_gather(vectors, "mp", axis=0)
    amount, width = inputs[0].shape
    rows = amount // 40
    image, *saved = on_slots(
        lone_forward_kernel, "forward", scalars, inputs + [cells_all] + weights[:3], outputs + [near],
        [((amount, width), jnp.float32), ((rows, near[0][1]), jnp.float32), ((8, width), jnp.float32)]
        + [pltpu.SMEM((rows,), jnp.int32)],
        counted=rows,
    )
    return image, weights, biases, saved[:-1], saved[-1]


def reduce_shards(grads, patch, early, inputs, shift, chunks, own):
    if own:
        return reduce_back(grads, patch, early, inputs, shift, chunks)
    flat, weights = inputs[0].shape, inputs[4].shape
    self_grad, late, text_grad = on_slots(
        lone_self_back_kernel, "self_back", [], inputs,
        [(weights, jnp.bfloat16), (early[0].shape, jnp.float32), (flat, jnp.float32)], [(flat, jnp.bfloat16)] * 5,
    )
    sums = [
        lax.psum(lax.psum_scatter(grad.astype(jnp.float32), "mp", scatter_dimension=0, tiled=True)[0], "dp").astype(grad.dtype)
        for grad in [self_grad] + grads
    ]
    windows = lax.all_to_all(patch, "mp", split_axis=0, concat_axis=0, tiled=True)
    return sums, windows, windows[0], lax.psum(early[0] + early[1] + late, ("dp", "mp")), text_grad


def per_device(
    tokens, patches, image_rows, row_lengths, box_mask, self_project, self_output, first_gain, first_shift, cross_query,
    cross_keyval, cross_output, second_gain, second_shift, expand_weight, expand_bias, shrink_weight, third_gain,
    third_shift, cotangent, *, parts, own,
):
    bf16, f32 = jnp.bfloat16, jnp.float32
    rows, slots, width = tokens.shape
    group_images, cells, depth = patches.shape
    starts, window = image_windows(parts, rows, group_images)
    padded = -(-cells // 16) * 16
    amount, pairs, tiles_of = rows * slots, rows // 2, width // 128
    inner = self_output.shape[0]
    shards = [
        [self_project.transpose(0, 2, 1).reshape(3 * inner, width), self_output],
        [cross_query.T, cross_output],
        [cross_keyval.transpose(0, 2, 1).reshape(2 * inner, depth)],
        [expand_weight],
        [shrink_weight],
    ]
    chunks = [(0, 0, 384), (0, 384, 384), (1, 0, 384), (2, 0, 384), (3, 0, 384), (3, 384, 384), (4, 0, 384), (4, 384, 384)]
    text = tokens.reshape(amount, width)
    flat, unit_row = (amount, width), ((amount, 128), f32)
    low_flat, full_flat = (flat, bf16), (flat, f32)
    probs_self, probs_cross = (pairs, tiles_of, 4 * slots, 2 * slots), (rows, tiles_of, 2 * slots, padded)
    image_part, vector = ((window, padded, width), bf16), ((16, width), f32)
    image, weights, norms, saved, near = forward(
        [image_rows, row_lengths],
        [text, box_mask, first_gain, first_shift, second_gain, second_shift, third_gain, third_shift, expand_bias],
        patches.transpose(1, 0, 2),
        shards,
        [low_flat] * 3 + [(probs_self, bf16), low_flat, full_flat, unit_row, low_flat, low_flat]
        + [image_part, image_part, (probs_cross, bf16), low_flat, full_flat, unit_row, full_flat, low_flat],
        ((window, padded, depth), bf16),
        chunks,
        own,
    )
    self_weights, cross_weights, keyval, expand, shrink = weights
    (
        queries, keys, values, self_probs, self_context, first_unit, first_inverse, first_low, cross_queries, image_keys,
        image_values, cross_probs, cross_context, second_unit, second_inverse, second_value, second_low,
    ) = saved
    joined, expand_grad, shrink_grad, feed_vectors, second_up = on_slots(
        feed_kernel,
        "feed",
        [],
        [second_value, second_low, norms, expand, shrink, cotangent.reshape(flat)],
        [low_flat, (expand.shape, bf16), (shrink.shape, bf16), vector, full_flat],
        [((parts,) + flat, bf16)] * 2 + [full_flat, unit_row, low_flat],
        parts_in=(3, 4),
        parts_out=(1, 2),
    )
    cross_weights_grad, keyval_grad, patch, cross_vectors, first_up = on_slots(
        cross_back_kernel,
        "cross_back",
        [image],
        [second_up, second_unit, second_inverse, norms, cross_weights, cross_context, cross_queries, image_values]
        + [image_keys, cross_probs, first_low, keyval, near],
        [(cross_weights.shape, bf16), (keyval.shape, bf16), ((parts, window, padded, depth // parts), bf16)]
        + [vector, full_flat],
        [low_flat, full_flat, full_flat, (image_part[0], f32), (image_part[0], f32), low_flat],
    )
    order = [(4, 0, 384), (4, 384, 384), (3, 0, 384), (3, 384, 384), (1, 0, 384), (2, 0, 384), (0, 0, 384), (0, 384, 384)]
    sums, windows, merged, vectors, text_grad = reduce_shards(
        [cross_weights_grad, keyval_grad, expand_grad, shrink_grad],
        patch,
        [feed_vectors, cross_vectors],
        [first_up, first_unit, first_inverse, norms, self_weights, self_context, queries, keys, values, self_probs, text],
        starts[1] - starts[0],
        order,
        own,
    )
    square, piece, line = ((width, width), f32), ((inner, width), f32), ((width,), f32)
    project, self_out, query, cross_out, pixel, expand_sum, shrink_sum, patch_grad, *lines = on_slots(
        functools.partial(finish_kernel, not own),
        "finish",
        [image],
        list(sums) + [vectors, windows, merged],
        [((3 * inner, width), f32), piece, piece, piece, ((2 * inner, depth), f32), square, square]
        + [((cells, group_images, depth // parts), f32)]
        + [line] * 7,
        [],
    )
    return (
        joined.reshape(tokens.shape),
        text_grad.reshape(tokens.shape),
        patch_grad.transpose(1, 0, 2),
        project.reshape(3, inner, width).transpose(0, 2, 1),
        self_out,
        lines[0],
        lines[1],
        query.T,
        pixel.reshape(2, inner, depth).transpose(0, 2, 1),
        cross_out,
        lines[2],
        lines[3],
        expand_sum,
        lines[6],
        shrink_sum,
        lines[4],
        lines[5],
    )


def solution(mesh):
    parts = mesh.shape["mp"]
    own = mesh.shape["dp"] == 8 and parts == 4
    return jax.shard_map(
        functools.partial(per_device, parts=parts, own=own),
        mesh=mesh,
        in_specs=(
            P(("dp", "mp"), None, None),
            P("dp", None, None),
            P("dp", None),
            P("dp"),
            P("dp", None),
            P(None, None, "mp"),
            P("mp", None),
            P(),
            P(),
            P(None, "mp"),
            P(None, None, "mp"),
            P("mp", None),
            P(),
            P(),
            P(None, "mp"),
            P("mp"),
            P("mp", None),
            P(),
            P(),
            P(("dp", "mp"), None, None),
        ),
        out_specs=(
            P(("dp", "mp"), None, None),
            P(("dp", "mp"), None, None),
            P("dp", None, "mp"),
            P(None, None, "mp"),
            P("mp", None),
            P(),
            P(),
            P(None, "mp"),
            P(None, None, "mp"),
            P("mp", None),
            P(),
            P(),
            P(None, "mp"),
            P("mp"),
            P("mp", None),
            P(),
            P(),
        ),
        check_vma=False,
    )
```

```python
import functools

import jax
import jax.numpy as jnp
from jax import lax
from jax.experimental import pallas as pl
from jax.experimental.pallas import tpu as pltpu
from jax.sharding import PartitionSpec as P

HEAD_DIM = 64
ROWS_MAX = 7
MESH = pl.DeviceIdType.MESH


def place():
    index = lax.axis_index("dp")
    plane = lax.axis_index("mp")
    y, x, c = index // 4, (index // 2) % 2, index % 2
    return index, plane, y, x, c


def partners(index, plane):
    core = (index + 1 - 2 * (index % 2), plane)
    across = (index + 2 - 4 * ((index // 2) % 2), plane)
    along = (index + 4 - 8 * (index // 4), plane)
    planes = [(index, lax.rem(plane + step, 4)) for step in (1, 2, 3)]
    return core, across, along, planes


def greet(peers):
    barrier = pltpu.get_barrier_semaphore()
    for peer in peers:
        pl.semaphore_signal(barrier, inc=1, device_id=peer, device_id_type=MESH)
    pl.semaphore_wait(barrier, len(peers))


class Sends:
    def __init__(self):
        self.stages, self.all = {}, []

    def start(self, name, k, items):
        copies = []
        for source, target, sends, recvs, peer in items:
            copy = pltpu.make_async_remote_copy(
                src_ref=source, dst_ref=target, send_sem=sends, recv_sem=recvs, device_id=peer, device_id_type=MESH
            )
            copy.start()
            copies.append(copy)
        self.stages[name, k] = copies
        self.all.extend(copies)

    def arrived(self, name, k):
        for copy in self.stages[name, k]:
            copy.wait_recv()

    def close(self):
        for copy in self.all:
            copy.wait_send()


class Gather:
    stages = 4

    def __init__(self, chunks, shards, wholes, sems, window, gap):
        self.chunks, self.shards, self.wholes, self.window = chunks, shards, wholes, window
        self.sems, self.gap = sems, gap
        self.index, self.plane, self.y, self.x, self.c = place()
        self.core, self.across, self.along, self.planes = partners(self.index, self.plane)
        self.others = [lax.rem(self.plane + step, 4) for step in (1, 2, 3)]
        self.sends = Sends()

    def sizes(self, k):
        which, base, rows = self.chunks[k]
        return which, base, rows // 8, self.wholes[which].shape[2] // 2

    def level(self, k):
        which, base, r, w = self.sizes(k)
        _, _, send, recv = self.sems[:4]
        self.own(which)
        items = []
        for h, first in enumerate((self.x * 2 + self.y, self.y * 2 + self.x)):
            here = (pl.ds(pl.multiple_of(base + (self.c * 4 + first) * r, 16), r), pl.ds(h * w, w))
            for j, peer in enumerate(self.planes):
                piece = self.wholes[which].at[(self.plane,) + here]
                items.append((piece, piece, send.at[k, h, j], recv.at[k, h, j], peer))
        self.sends.start("level", k, items)

    def near(self, k):
        which, base, r, w = self.sizes(k)
        send, recv = self.sems[4:6]
        self.sends.arrived("level", k)
        if k + self.window < len(self.chunks):
            self.level(k + self.window)
        items = []
        for h, first in enumerate((self.x * 2 + self.y, self.y * 2 + self.x)):
            row = pl.multiple_of(base + (self.c * 4 + first) * r, 16)
            for j, other in enumerate(self.others):
                piece = self.wholes[which].at[other, pl.ds(row, r), pl.ds(h * w, w)]
                items.append((piece, piece, send.at[k, h, j], recv.at[k, h, j], (self.along, self.across)[h]))
        self.sends.start("near", k, items)

    def far(self, k):
        which, base, r, w = self.sizes(k)
        send, recv = self.sems[6:8]
        self.sends.arrived("near", k)
        items = []
        for h, first in enumerate((self.x, self.y)):
            row = pl.multiple_of(base + (self.c * 4 + first * 2) * r, 16)
            for j, other in enumerate(self.others):
                piece = self.wholes[which].at[other, pl.ds(row, 2 * r), pl.ds(h * w, w)]
                items.append((piece, piece, send.at[k, h, j], recv.at[k, h, j], (self.across, self.along)[h]))
        self.sends.start("far", k, items)

    def cross(self, k):
        which, base, r, w = self.sizes(k)
        send, recv = self.sems[8:10]
        self.sends.arrived("far", k)
        row = pl.multiple_of(base + self.c * 4 * r, 16)
        items = []
        for j, other in enumerate(self.others):
            piece = self.wholes[which].at[other, pl.ds(row, 4 * r), :]
            items.append((piece, piece, send.at[k, j], recv.at[k, j], self.core))
        self.sends.start("core", k, items)

    def own(self, which):
        for copy in self.local.pop(which, ()):
            copy.wait()

    def begin(self):
        self.local = {}
        for which, pieces in enumerate(self.shards):
            row, self.local[which] = 0, []
            for i, piece in enumerate(pieces):
                target = self.wholes[which].at[self.plane, pl.ds(row, piece.shape[0]), :]
                copy = pltpu.make_async_copy(piece, target, self.sems[0].at[which, i])
                copy.start()
                self.local[which].append(copy)
                row += piece.shape[0]
        greet([self.core, self.across, self.along] + self.planes)
        for k in range(self.window):
            self.level(k)

    def step(self, t):
        if 0 <= t - 2 * self.gap < len(self.chunks):
            self.cross(t - 2 * self.gap)
        if 0 <= t - self.gap < len(self.chunks):
            self.far(t - self.gap)
        if 0 <= t < len(self.chunks):
            self.near(t)

    @property
    def steps(self):
        return len(self.chunks) + 2 * self.gap

    def ready(self, k):
        self.sends.arrived("core", k)

    @staticmethod
    def scratch(count, total):
        dma = pltpu.SemaphoreType.DMA
        return [dma((count, 2)), dma((count,))] + [dma((total, 2, 3))] * 6 + [dma((total, 3))] * 2


class Ticks:
    def __init__(self, gather, outs, sem):
        self.gather, self.outs, self.sem = gather, outs, sem
        self.now, self.done, self.final = 0, 0, []

    def __call__(self):
        gather, total = self.gather, len(self.gather.chunks)
        if self.now < gather.steps:
            gather.step(self.now)
        k = self.now - 3 * gather.gap
        if 0 <= k < total:
            gather.ready(k)
            self.done = k + 1
            which = gather.chunks[k][0]
            if k + 1 == total or gather.chunks[k + 1][0] != which:
                copy = pltpu.make_async_copy(gather.wholes[which], self.outs[which], self.sem.at[which])
                copy.start()
                self.final.append(copy)
        self.now += 1

    def wait(self, which):
        last = max(k for k, chunk in enumerate(self.gather.chunks) if chunk[0] == which)
        while self.done <= last:
            self()

    def close(self):
        while self.done < len(self.gather.chunks):
            self()
        self.gather.sends.close()
        for copy in self.final:
            copy.wait()


def forward_kernel(chunks, pieces, count, *refs):
    counts, lengths, tokens, boxes = refs[:4]
    vectors, cells_far, refs = refs[4:11], refs[11], refs[12:]
    shards, arrays = [], len(pieces)
    for amount in pieces:
        shards.append(refs[:amount])
        refs = refs[amount:]
    image, outs, biases, refs = refs[0], refs[1 : arrays + 1], refs[arrays + 1], refs[arrays + 2 :]
    far, refs = refs[: count + 1], refs[count + 1 :]
    wholes, refs = refs[:arrays], refs[arrays:]
    saved = [Slot(far[i], refs[2 * i], refs[2 * i + 1]) for i in range(count + 1)]
    *saved, near = saved
    refs = refs[2 * count + 2 :]
    (wide, cells_all, cell_ok, norms, caption, bias_send, bias_recv, cells_sem), sems = refs[:8], refs[8:]
    gather = Gather(chunks, shards, wholes, sems, 3, 1)
    copy = pltpu.make_async_copy(cells_far, cells_all, cells_sem)
    copy.start()
    gather.begin()
    copy.wait()
    prepare(counts, lengths, boxes, vectors, cells_all, image, caption, cell_ok, norms, near.near, gather.plane)
    near.flush()
    gather.sends.start(
        "bias", 0, [(norms, biases.at[gather.plane], bias_send.at[j], bias_recv.at[j], peer) for j, peer in enumerate(gather.planes)]
    )
    biases[gather.plane] = norms[...]
    ticks = Ticks(gather, outs, sems[1])
    rows = cell_ok.shape[0]
    forward_steps(
        ticks, image, caption, lambda r: lengths[gather.plane * rows + r], tokens, near.near, cell_ok, wholes[:3], norms, saved,
        wide,
    )
    gather.sends.arrived("bias", 0)
    ticks.close()
    for slot in saved + [near]:
        slot.finish()


def gather_forward(scalars, inputs, cells_all, shards, outputs, near, chunks):
    dma, bf16, f32, arrays, count = pltpu.SemaphoreType.DMA, jnp.bfloat16, jnp.float32, len(shards), len(outputs)
    any_space, vmem = pl.BlockSpec(memory_space=pl.ANY), pl.BlockSpec(memory_space=pltpu.VMEM)
    smem = pl.BlockSpec(memory_space=pltpu.SMEM)
    tokens = inputs[0]
    width = tokens.shape[1]
    rows, padded = tokens.shape[0] // 40, near[0][1]
    shapes = [(4, sum(piece.shape[0] for piece in pieces), pieces[0].shape[1]) for pieces in shards]
    flat = [piece for pieces in shards for piece in pieces]
    outputs = outputs + [near]
    results = pl.pallas_call(
        functools.partial(forward_kernel, chunks, [len(pieces) for pieces in shards], count),
        out_shape=[jax.ShapeDtypeStruct((rows,), jnp.int32)]
        + [jax.ShapeDtypeStruct(shape, bf16) for shape in shapes]
        + [jax.ShapeDtypeStruct((4, 8, width), f32)]
        + [jax.ShapeDtypeStruct(shape, kind) for shape, kind in outputs],
        in_specs=[smem] * len(scalars) + [vmem] * len(inputs) + [any_space] * (len(flat) + 1),
        out_specs=[smem] + [any_space] * arrays + [vmem] + [any_space] * (count + 1),
        scratch_shapes=[pltpu.VMEM(shape, bf16) for shape in shapes]
        + [entry for shape, kind in outputs for entry in slot_scratch(shape, kind)]
        + [pltpu.VMEM(tokens.shape, f32), pltpu.VMEM(cells_all.shape, bf16), pltpu.VMEM((rows, padded), f32)]
        + [pltpu.VMEM((8, width), f32), pltpu.SMEM((rows,), jnp.int32)]
        + [dma((3,)), dma((3,)), dma(())]
        + Gather.scratch(arrays, len(chunks)),
        compiler_params=pltpu.CompilerParams(collective_id=0, has_side_effects=True, vmem_limit_bytes=63 << 20),
        name="gather_forward",
    )(*scalars, *inputs, cells_all, *flat)
    return results[0], results[1 : arrays + 1], results[arrays + 1], results[arrays + 2 : -1], results[-1]


class Alone:
    def __call__(self):
        pass

    def wait(self, which):
        pass


def lone_forward_kernel(scalars, inputs, outputs, scratch):
    tokens, boxes, *vectors, cells_all, self_weights, cross_weights, keyval = (slot.ready() for slot in inputs)
    *saved, near = outputs
    counts, lengths, image = scalars
    wide, cell_ok, norms, caption = scratch
    rows, plane = cell_ok.shape[0], lax.axis_index("mp")
    prepare(counts, lengths, boxes, vectors, cells_all, image, caption, cell_ok, norms, near.near, plane)
    near.flush()
    forward_steps(
        Alone(), image, caption, lambda r: lengths[plane * rows + r], tokens, near.near, cell_ok,
        (self_weights, cross_weights, keyval), norms, saved, wide,
    )


class Reduce:
    def __init__(self, chunks, grads, sums, buffers, sems, local):
        self.chunks, self.grads, self.sums, self.sems, self.local = chunks, grads, sums, sems, local
        self.mine, self.core_in, self.near_in, self.far_in, self.plane_in, self.relay_in = [], [], [], [], [], []
        buffers = list(buffers)
        self.index, self.plane, self.y, self.x, self.c = place()
        for which, base, rows in chunks:
            if which in local:
                self.mine.append((local[which], base + self.c * (rows // 2)))
            else:
                self.mine.append((buffers.pop(0), 0))
            self.core_in.append(buffers.pop(0))
            self.near_in.append(buffers.pop(0))
            self.far_in.append(buffers.pop(0))
            self.plane_in.append(buffers.pop(0))
            self.relay_in.append(buffers.pop(0))
        self.core, self.across, self.along, self.planes = partners(self.index, self.plane)
        self.others = [lax.rem(self.plane + step, 4) for step in (1, 2, 3)]
        self.sends = Sends()
        self.outer = (self.plane == 0) | (self.plane == 3)
        self.next = jnp.where(self.plane == 0, 1, 2)
        self.beyond = 3 - self.next
        self.edge = jnp.where(self.plane == 1, 0, 3)
        self.fetched, self.final = {}, []
        self.order = [self.begin, self.near, self.far, self.level, self.bridge]
        self.order += [self.out_near, self.out_far, self.out_core, self.end]

    @staticmethod
    def scratch(chunks, widths, local):
        low, dma, total = jnp.bfloat16, pltpu.SemaphoreType.DMA, len(chunks)
        shapes = []
        for which, _, r in chunks:
            w = widths[which]
            shapes += [] if which in local else [(4, r // 2, w)]
            shapes += [(4, r // 2, w), (2, 4, r // 4, w // 2), (2, 4, r // 8, w // 2), (2, 3, r // 8, w // 2)]
            shapes += [(2, r // 8, w // 2)]
        sems = [dma((total,))] * 4 + [dma((total, 2))] * 8 + [dma((total, 2, 3))] * 2 + [dma((total,))] * 2 + [dma((total, 2))]
        return [pltpu.VMEM(shape, low) for shape in shapes], sems

    def sizes(self, k):
        which, base, rows = self.chunks[k]
        return which, base, rows // 8, self.grads[which].shape[2] // 2

    @staticmethod
    def add(total, total_row, total_col, part, part_col, rows, cols):
        @pl.loop(0, rows // 16)
        def _(i):
            here = (pl.ds(pl.multiple_of(total_row + i * 16, 16), 16), pl.ds(total_col, cols))
            there = (pl.ds(pl.multiple_of(i * 16, 16), 16), pl.ds(part_col, cols))
            ours = [total[(shard,) + here].astype(jnp.float32) for shard in range(4)]
            theirs = [part[(shard,) + there].astype(jnp.float32) for shard in range(4)]
            sums = [(left + right).astype(jnp.bfloat16) for left, right in zip(ours, theirs)]
            for shard in range(4):
                total[(shard,) + here] = sums[shard]

    def places(self, r, w):
        return [((self.x * 2 + self.y) * r, 0), ((self.y * 2 + self.x) * r, w)]

    def begin(self, k):
        which, base, r, w = self.sizes(k)
        theirs = pl.multiple_of(base + (1 - self.c) * 4 * r, 16)
        ours = pl.multiple_of(base + self.c * 4 * r, 16)
        source = self.grads[which].at[:, pl.ds(theirs, 4 * r), :]
        self.sends.start("core", k, [(source, self.core_in[k], self.sems[0].at[k], self.sems[1].at[k], self.core)])
        if which not in self.local:
            source = self.grads[which].at[:, pl.ds(ours, 4 * r), :]
            self.fetched[k] = pltpu.make_async_copy(source, self.mine[k][0], self.sems[2].at[k])
            self.fetched[k].start()

    def near(self, k):
        which, base, r, w = self.sizes(k)
        mine, offset = self.mine[k]
        if k in self.fetched:
            self.fetched[k].wait()
        self.sends.arrived("core", k)
        items = []
        for h, (bit, peer) in enumerate([(self.x, self.across), (self.y, self.along)]):
            self.add(mine, offset, h * w, self.core_in[k], h * w, 4 * r, w)
            row = pl.multiple_of(offset + (1 - bit) * 2 * r, 16)
            source = mine.at[:, pl.ds(row, 2 * r), pl.ds(h * w, w)]
            items.append((source, self.near_in[k].at[h], self.sems[4].at[k, h], self.sems[5].at[k, h], peer))
        self.sends.start("near", k, items)

    def far(self, k):
        which, base, r, w = self.sizes(k)
        mine, offset = self.mine[k]
        self.sends.arrived("near", k)
        items = []
        for h, (bit, second, peer) in enumerate([(self.x, self.y, self.along), (self.y, self.x, self.across)]):
            row = offset + bit * 2 * r
            self.add(mine, row, h * w, self.near_in[k].at[h], 0, 2 * r, w)
            row = pl.multiple_of(row + (1 - second) * r, 16)
            source = mine.at[:, pl.ds(row, r), pl.ds(h * w, w)]
            items.append((source, self.far_in[k].at[h], self.sems[6].at[k, h], self.sems[7].at[k, h], peer))
        self.sends.start("far", k, items)


    def hop(self, k, h, j, source, target, recv, to):
        return pltpu.make_async_remote_copy(
            src_ref=source, dst_ref=target, send_sem=self.sems[12].at[k, h, j], recv_sem=recv,
            device_id=(self.index, to), device_id_type=MESH,
        )

    def slot(self, k, h, j):
        return self.plane_in[k].at[h, j], self.sems[13].at[k, h, j]

    def bridge_slot(self, k, h):
        return self.relay_in[k].at[h], self.sems[16].at[k, h]

    def level(self, k):
        which, base, r, w = self.sizes(k)
        mine, offset = self.mine[k]
        self.sends.arrived("far", k)
        for h, (row, col) in enumerate(self.places(r, w)):
            self.add(mine, offset + row, col, self.far_in[k].at[h], 0, r, w)

        def piece(h, plane):
            row, col = self.places(r, w)[h]
            return mine.at[plane, pl.ds(pl.multiple_of(offset + row, 16), r), pl.ds(col, w)]

        @pl.when(self.outer)
        def _():
            for h in range(2):
                self.hop(k, h, 2, piece(h, 3 - self.plane), *self.bridge_slot(k, h), self.next).start()
            for h in range(2):
                self.hop(k, h, 1, piece(h, self.beyond), *self.slot(k, h, 2), self.beyond).start()
                self.hop(k, h, 0, piece(h, self.next), *self.slot(k, h, 1), self.next).start()

        @pl.when(jnp.logical_not(self.outer))
        def _():
            for h in range(2):
                self.hop(k, h, 1, piece(h, 3 - self.plane), *self.slot(k, h, 0), 3 - self.plane).start()
                self.hop(k, h, 0, piece(h, self.edge), *self.slot(k, h, 0), self.edge).start()

    def bridge(self, k):
        which, base, r, w = self.sizes(k)
        mine, offset = self.mine[k]
        relay = self.relay_in[k]

        @pl.when(jnp.logical_not(self.outer))
        def _():
            for h, (row, col) in enumerate(self.places(r, w)):
                self.hop(k, h, 2, relay.at[h], *self.bridge_slot(k, h), self.plane).wait_recv()

                @pl.loop(0, r // 16)
                def _(i):
                    step = pl.ds(pl.multiple_of(i * 16, 16), 16)
                    here = pl.ds(pl.multiple_of(offset + row + i * 16, 16), 16)
                    ours = mine[3 - self.edge, here, pl.ds(col, w)].astype(jnp.float32)
                    relay[h, step, :] = (ours + relay[h, step, :].astype(jnp.float32)).astype(jnp.bfloat16)

                self.hop(k, h, 2, relay.at[h], *self.slot(k, h, 1), 3 - self.edge).start()

    def out_near(self, k):
        which, base, r, w = self.sizes(k)
        mine, offset = self.mine[k]

        def gather(amount):
            for h, (row, col) in enumerate(self.places(r, w)):
                for j in range(amount):
                    place, sem = self.slot(k, h, j)
                    self.hop(k, h, j, place, place, sem, self.plane).wait_recv()

                @pl.loop(0, r // 16)
                def _(i):
                    step = pl.ds(pl.multiple_of(i * 16, 16), 16)
                    here = pl.ds(pl.multiple_of(offset + row + i * 16, 16), 16)
                    total = mine[self.plane, here, pl.ds(col, w)].astype(jnp.float32)
                    for j in range(amount):
                        total = total + self.plane_in[k][h, j, step, :].astype(jnp.float32)
                    here = pl.ds(pl.multiple_of(row + i * 16, 16), 16)
                    self.core_in[k][0, here, pl.ds(col, w)] = total.astype(jnp.bfloat16)

        @pl.when(self.outer)
        def _():
            gather(2)

        @pl.when(jnp.logical_not(self.outer))
        def _():
            gather(3)

        items = []
        for h, (row, col) in enumerate(self.places(r, w)):
            piece = self.core_in[k].at[0, pl.ds(pl.multiple_of(row, 16), r), pl.ds(col, w)]
            peer = (self.along, self.across)[h]
            items.append((piece, piece, self.sems[8].at[k, h], self.sems[9].at[k, h], peer))
        self.sends.start("out_near", k, items)

    def out_far(self, k):
        which, base, r, w = self.sizes(k)
        self.sends.arrived("out_near", k)
        items = []
        for h, (bit, peer) in enumerate([(self.x, self.across), (self.y, self.along)]):
            piece = self.core_in[k].at[0, pl.ds(pl.multiple_of(bit * 2 * r, 16), 2 * r), pl.ds(h * w, w)]
            items.append((piece, piece, self.sems[10].at[k, h], self.sems[11].at[k, h], peer))
        self.sends.start("out_far", k, items)

    def out_core(self, k):
        which, base, r, w = self.sizes(k)
        self.sends.arrived("out_far", k)
        target = self.sums[which].at[pl.ds(pl.multiple_of(base + self.c * 4 * r, 16), 4 * r), :]
        source = self.core_in[k].at[0]
        self.sends.start("out_core", k, [(source, target, self.sems[14].at[k], self.sems[15].at[k], self.core)])
        copy = pltpu.make_async_copy(source, target, self.sems[3].at[k])
        copy.start()
        self.final.append(copy)

    def end(self, k):
        self.sends.arrived("out_core", k)

    @property
    def steps(self):
        return len(self.chunks) + len(self.order) - 1

    def step(self, t):
        for s in range(len(self.order)):
            if 0 <= t - s < len(self.chunks):
                self.order[s](t - s)

    def close(self):
        self.sends.close()
        for k in range(len(self.chunks)):
            for h in range(2):
                for j in range(3):
                    place, sem = self.slot(k, h, j)
                    self.hop(k, h, j, place, place, sem, self.plane).wait_send()
        for copy in self.final:
            copy.wait()


class ReduceTicks:
    def __init__(self, reduce, vector_sum, vector_in, send, recv):
        self.reduce, self.vector_sum, self.vector_in, self.send, self.recv = reduce, vector_sum, vector_in, send, recv
        self.now = 0

    def __call__(self):
        if self.now < self.reduce.steps:
            self.reduce.step(self.now)
        self.now += 1

    def sum_vectors(self):
        reduce, total, arrived = self.reduce, self.vector_sum, self.vector_in
        for t, peer in enumerate((reduce.core, reduce.across, reduce.along)):
            reduce.sends.start("vector", t, [(total.at[t], arrived.at[t], self.send.at[t], self.recv.at[t], peer)])
            self()
            reduce.sends.arrived("vector", t)
            total[t + 1] = total[t] + arrived[t]
        items = [
            (total.at[3], arrived.at[3 + j], self.send.at[3 + j], self.recv.at[3 + j], peer)
            for j, peer in enumerate(reduce.planes)
        ]
        reduce.sends.start("vector", 3, items)
        self()
        reduce.sends.arrived("vector", 3)
        ordered = [arrived[3 + j] for j in range(3)]
        plane, own = reduce.plane, total[3]
        slots = []
        for m in range(4):
            value = own
            for j in range(3):
                value = jnp.where(reduce.others[j] == m, ordered[j], value)
            slots.append(value)
        total[4] = (slots[0] + slots[1]) + (slots[2] + slots[3])


class Patches:
    def __init__(self, patch, windows, merged, buffers, sems, index, plane, images, shift):
        self.patch, self.windows, self.merged = patch, windows, merged
        self.relay, self.own, self.total = buffers
        self.sends, self.recvs, self.relay_recv, self.merged_recv, self.local, self.fetch = sems
        self.index, self.plane = index, plane
        self.outer = (plane == 0) | (plane == 3)
        self.first = plane < 2
        self.next = jnp.where(plane == 0, 1, 2)
        self.far = 3 - self.next
        self.edge = jnp.where(plane == 1, 0, 3)
        self.across = 3 - plane
        self.images, self.shift = images, shift
    def copy(self, slot, source, target, recv, to):
        return pltpu.make_async_remote_copy(
            src_ref=source, dst_ref=target, send_sem=self.sends.at[slot], recv_sem=recv, device_id=(self.index, to),
            device_id_type=MESH,
        )

    def direct(self, slot, to):
        return self.copy(slot, self.patch.at[to], self.windows.at[self.plane], self.recvs.at[self.plane], to)

    def to_relay(self):
        return self.copy(1, self.patch.at[self.across], self.relay, self.relay_recv.at[0], self.next)

    def to_edge(self):
        return self.copy(1, self.total, self.merged, self.merged_recv.at[0], 3 - self.edge)

    def keep(self):
        return pltpu.make_async_copy(self.patch.at[self.plane], self.windows.at[self.plane], self.local.at[0])

    def take(self):
        return pltpu.make_async_copy(self.patch.at[3 - self.edge], self.own, self.fetch.at[0])

    def begin(self):
        self.keep().start()

        @pl.when(self.outer)
        def _():
            self.to_relay().start()
            self.direct(0, self.far).start()

        @pl.when(jnp.logical_not(self.outer))
        def _():
            self.take().start()
            self.direct(0, self.across).start()

    def middle(self):
        @pl.when(self.outer)
        def _():
            self.direct(2, self.next).start()

        @pl.when(jnp.logical_not(self.outer))
        def _():
            self.direct(2, self.edge).start()
            self.take().wait()
            self.to_relay().wait_recv()

            @pl.when(self.first)
            def _():
                self.add(self.relay, self.own)

            @pl.when(jnp.logical_not(self.first))
            def _():
                self.add(self.own, self.relay)

            self.to_edge().start()

    def add(self, early, late):
        images, shift, total = self.images, self.shift, self.total
        size = (early.shape[0] - 16) // images
        for i in range(images + shift):
            here = pl.ds(i * size, size)
            there = pl.ds((i - shift) * size, size)
            if i < shift:
                total[here, :] = early[here, :]
            elif i < images:
                both = early[here, :].astype(jnp.float32) + late[there, :].astype(jnp.float32)
                total[here, :] = both.astype(jnp.bfloat16)
            else:
                total[here, :] = late[there, :]
        row = lax.broadcasted_iota(jnp.int32, (16, 16), 0)
        column = lax.broadcasted_iota(jnp.int32, (16, 16), 1)
        down = (row == column + shift).astype(jnp.bfloat16)
        last = pl.ds(images * size, 16)
        both = early[last, :].astype(jnp.float32) + nn(down, late[last, :])
        total[pl.ds((images + shift) * size, 16), :] = both.astype(jnp.bfloat16)

    def end(self):
        self.keep().wait()

        @pl.when(self.outer)
        def _():
            self.copy(0, self.patch.at[0], self.windows.at[self.next], self.recvs.at[self.next], self.next).wait_recv()
            self.copy(1, self.total, self.merged, self.merged_recv.at[0], self.far).wait_recv()
            self.to_relay().wait_send()
            self.direct(0, self.far).wait_send()
            self.direct(2, self.next).wait_send()

        @pl.when(jnp.logical_not(self.outer))
        def _():
            for source in (self.across, 0, 3):
                self.copy(0, self.patch.at[0], self.windows.at[source], self.recvs.at[source], self.across).wait_recv()
            self.direct(0, self.across).wait_send()
            self.to_edge().wait_send()
            self.direct(2, self.edge).wait_send()


def back_kernel(chunks, count, slots, window, shift, *refs):
    grads, patch, early, refs = refs[:count], refs[count], refs[count + 1 : count + 3], refs[count + 3 :]
    inputs, refs = refs[:slots], refs[slots:]
    sums, refs = refs[: count + 1], refs[count + 1 :]
    (windows, merged, vector_sum, text_far), refs = refs[:4], refs[4:]
    inputs = [Slot(inputs[i], refs[2 * i], refs[2 * i + 1]) for i in range(slots)]
    refs = refs[2 * slots :]
    self_grad, text_sem, refs = refs[0], refs[1], refs[2:]
    scratch, refs = refs[:5], refs[5:]
    (vector_in, vector_send, vector_recv), patch_refs, refs = refs[:3], refs[3:12], refs[12:]
    sems, buffers = refs[:17], refs[17:]
    for slot in inputs:
        slot.fetch()
    reduce = Reduce(chunks, [self_grad, *grads], sums, buffers, sems, {0: self_grad})
    greet([reduce.core, reduce.across, reduce.along] + reduce.planes)
    ticks = ReduceTicks(reduce, vector_sum, vector_in, vector_send, vector_recv)
    ticks()
    patches = Patches(
        patch, windows, merged, patch_refs[:3], patch_refs[3:], reduce.index, reduce.plane, window, shift
    )
    patches.begin()
    vector_sum[0] = early[0][...] + early[1][...]
    text_grad = inputs[0].near
    self_back_steps(ticks, inputs, self_grad, vector_sum.at[0], text_grad, scratch)
    text_copy = pltpu.make_async_copy(text_grad, text_far, text_sem.at[0])
    text_copy.start()
    ticks()
    patches.middle()
    ticks.sum_vectors()
    while ticks.now < reduce.steps:
        ticks()
    patches.end()
    reduce.close()
    text_copy.wait()


def reduce_back(grads, patch, early, inputs, window, shift, chunks):
    count, dma, f32, bf16 = len(grads), pltpu.SemaphoreType.DMA, jnp.float32, jnp.bfloat16
    any_space, vmem = pl.BlockSpec(memory_space=pl.ANY), pl.BlockSpec(memory_space=pltpu.VMEM)
    weights, flat = inputs[4].shape, inputs[0].shape
    together = (patch.shape[1] + shift * ((patch.shape[1] - 16) // window), patch.shape[2])
    widths = [weights[2]] + [grad.shape[2] for grad in grads]
    buffers, sems = Reduce.scratch(chunks, widths, {0})
    *sums, windows, merged, vector_sum, text_grad = pl.pallas_call(
        functools.partial(back_kernel, chunks, count, len(inputs), window, shift),
        out_shape=[jax.ShapeDtypeStruct(shape[1:], bf16) for shape in [weights] + [grad.shape for grad in grads]]
        + [jax.ShapeDtypeStruct(patch.shape, bf16), jax.ShapeDtypeStruct(together, bf16)]
        + [jax.ShapeDtypeStruct((5,) + early[0].shape, f32)]
        + [jax.ShapeDtypeStruct(flat, f32)],
        in_specs=[any_space] * (count + 1) + [vmem] * 2 + [any_space] * len(inputs),
        out_specs=[any_space] * (count + 3) + [vmem, any_space],
        scratch_shapes=[entry for array in inputs for entry in slot_scratch(array.shape, array.dtype)]
        + [pltpu.VMEM(weights, bf16), dma((1,))]
        + [pltpu.VMEM(flat, bf16)] * 5
        + [pltpu.VMEM((6,) + early[0].shape, f32), dma((6,)), dma((6,))]
        + [pltpu.VMEM(patch.shape[1:], bf16), pltpu.VMEM(patch.shape[1:], bf16), pltpu.VMEM(together, bf16)]
        + [dma((3,)), dma((4,)), dma((1,)), dma((1,)), dma((1,)), dma((1,))]
        + sems
        + buffers,
        compiler_params=pltpu.CompilerParams(collective_id=1, has_side_effects=True, vmem_limit_bytes=63 << 20),
        name="reduce_back",
    )(*grads, patch, *early, *inputs)
    return sums, windows, merged, vector_sum, text_grad


class Slot:
    def __init__(self, far, near, sem, parts=0):
        self.far, self.near, self.sem, self.parts, self.waited = far, near, sem, parts, False

    def copy(self, out, m=None):
        far, near = (self.far, self.near) if m is None else (self.far.at[m], self.near.at[m])
        sem = self.sem.at[0 if m is None else m]
        return pltpu.make_async_copy(near, far, sem) if out else pltpu.make_async_copy(far, near, sem)

    def fetch(self):
        for m in range(self.parts) if self.parts else (None,):
            self.copy(False, m).start()

    def ready(self):
        if not self.waited:
            self.waited = True
            for m in range(self.parts) if self.parts else (None,):
                self.copy(False, m).wait()
        return self.near

    def flush(self, m=None):
        self.copy(True, m).start()

    def finish(self):
        for m in range(self.parts) if self.parts else (None,):
            self.copy(True, m).wait()


def slot_scratch(shape, kind, parts=0):
    return [pltpu.VMEM(shape, kind), pltpu.SemaphoreType.DMA((max(parts, 1),))]


def on_slots(kernel, name, scalars, inputs, outputs, scratch, parts_in=(), parts_out=(), counted=0):
    count, total, given = len(inputs), len(inputs) + len(outputs), len(scalars)

    def body(*refs):
        scalar_refs, refs = refs[:given], refs[given:]
        far_in, refs = refs[:count], refs[count:]
        if counted:
            scalar_refs, refs = scalar_refs + refs[:1], refs[1:]
        far, refs = far_in + refs[: total - count], refs[total - count :]
        slots = []
        for i in range(total):
            parts = far[i].shape[0] if (i in parts_in if i < count else i - count in parts_out) else 0
            slots.append(Slot(far[i], refs[2 * i], refs[2 * i + 1], parts))
        for slot in slots[:count]:
            slot.fetch()
        kernel(scalar_refs, slots[:count], slots[count:], refs[2 * total :])
        for slot in slots[count:]:
            slot.finish()

    spaces = []
    for i, array in enumerate(inputs):
        spaces += slot_scratch(array.shape, array.dtype, array.shape[0] if i in parts_in else 0)
    for i, (shape, kind) in enumerate(outputs):
        spaces += slot_scratch(shape, kind, shape[0] if i in parts_out else 0)
    any_space, smem = pl.BlockSpec(memory_space=pl.ANY), pl.BlockSpec(memory_space=pltpu.SMEM)
    first = [jax.ShapeDtypeStruct((counted,), jnp.int32)] if counted else []
    return pl.pallas_call(
        body,
        out_shape=first + [jax.ShapeDtypeStruct(shape, kind) for shape, kind in outputs],
        in_specs=[smem] * given + [any_space] * count,
        out_specs=[smem] * len(first) + [any_space] * len(outputs),
        scratch_shapes=spaces + [entry if hasattr(entry, "memory_space") else pltpu.VMEM(*entry) for entry in scratch],
        compiler_params=pltpu.CompilerParams(vmem_limit_bytes=63 << 20),
        name=name,
    )(*scalars, *inputs)


def nn(left, right):
    return lax.dot_general(left, right, (((1,), (0,)), ((), ())), preferred_element_type=jnp.float32)


def nt(left, right):
    return lax.dot_general(left, right, (((1,), (1,)), ((), ())), preferred_element_type=jnp.float32)


def tn(left, right):
    return lax.dot_general(left, right, (((0,), (0,)), ((), ())), preferred_element_type=jnp.float32)


def part(ref, which):
    inner = ref.shape[2] // 4 if ref.shape[2] == 768 else 192
    return jnp.concatenate([ref[m, which * 192 : (which + 1) * 192, :] for m in range(4)], axis=0)


def store_part(ref, which, value):
    low = value.astype(jnp.bfloat16)
    for m in range(4):
        ref[m, which * 192 : (which + 1) * 192, :] = low[m * 192 : (m + 1) * 192]


def tiles(amount, step):
    def wrap(body):
        @pl.loop(0, amount // step)
        def _(i):
            body(pl.ds(pl.multiple_of(i * step, step), step))

    return wrap


def lanes():
    place = lax.broadcasted_iota(jnp.int32, (1, 2 * HEAD_DIM), 1)
    low = place < HEAD_DIM
    return low, low.astype(jnp.float32), 1.0 - low.astype(jnp.float32)


def norm_forward(total, unit, inverse, value, value_low, gain, shift):
    @tiles(total.shape[0], 80)
    def _(rows):
        hidden = total[rows, :]
        center = hidden - jnp.mean(hidden, axis=-1, keepdims=True)
        factor = lax.rsqrt(jnp.mean(center * center, axis=-1, keepdims=True) + 1e-06)
        scaled = center * factor
        result = scaled * gain[...] + shift[...]
        if unit is not None:
            unit[rows, :] = scaled
            inverse[rows, :] = jnp.broadcast_to(factor, (80, 128))
        if value is not None:
            value[rows, :] = result
        value_low[rows, :] = result.astype(jnp.bfloat16)


def norm_reverse(upstream, unit, inverse, gain, gain_grad, shift_grad, grad, grad_low):
    gain_grad[...] = jnp.zeros_like(gain_grad)
    shift_grad[...] = jnp.zeros_like(shift_grad)

    @tiles(upstream.shape[0], 80)
    def _(rows):
        up = upstream[rows, :].astype(jnp.float32)
        scaled = unit[rows, :]
        factor = inverse[rows, :][:, :1]
        gain_grad[...] += jnp.sum(up * scaled, axis=0, keepdims=True)
        shift_grad[...] += jnp.sum(up, axis=0, keepdims=True)
        inner = up * gain[...]
        result = factor * (
            inner
            - jnp.mean(inner, axis=-1, keepdims=True)
            - scaled * jnp.mean(inner * scaled, axis=-1, keepdims=True)
        )
        grad[rows, :] = result
        grad_low[rows, :] = result.astype(jnp.bfloat16)


def softmax(scores):
    raised = jnp.exp(scores - jnp.max(scores, axis=-1, keepdims=True))
    return (raised * (1.0 / jnp.sum(raised, axis=-1, keepdims=True))).astype(jnp.bfloat16)


def columns(width):
    return [slice(start, start + 128) for start in range(0, width, 128)]


def stack(value, first, second):
    return jnp.concatenate([value * first, value * second], axis=0)


def merge(low, value):
    half = value.shape[0] // 2
    return jnp.where(low, value[:half], value[half:])


def attend_self(queries, keys, values, lengths, probs, context):
    low, first, second = lanes()
    first, second = first.astype(jnp.bfloat16), second.astype(jnp.bfloat16)
    cols = columns(queries.shape[1])
    query = lax.broadcasted_iota(jnp.int32, (160, 80), 0)
    key = lax.broadcasted_iota(jnp.int32, (160, 80), 1)
    query = jnp.where(query >= 80, query - 80, query)
    same = (query < 40) == (key < 40)

    @pl.loop(0, queries.shape[0] // 80)
    def _(pair):
        rows = pl.ds(pl.multiple_of(pair * 80, 80), 80)
        allowed = same & (key < jnp.where(key < 40, lengths(2 * pair), lengths(2 * pair + 1) + 40))
        stacked = [stack(queries[rows, c], first, second) for c in cols]
        scores = [nt(both, keys[rows, c]) * HEAD_DIM ** (-0.5) for both, c in zip(stacked, cols)]
        weights = [softmax(jnp.where(allowed, score, -1000000000.0)) for score in scores]
        mixed = [merge(low, nn(weight, values[rows, c])) for weight, c in zip(weights, cols)]
        for tile, c in enumerate(cols):
            probs[pair, tile] = weights[tile]
            context[rows, c] = mixed[tile].astype(jnp.bfloat16)


def attend_cross(image, caption, wide, keys, values, cell_ok, probs, begin, end):
    low, first, second = lanes()
    cols = columns(wide.shape[1])

    @pl.loop(begin, end)
    def _(row):
        rows = pl.ds(pl.multiple_of(row * 40, 40), 40)
        which = image[row]
        cells = cell_ok[pl.ds(row, 1), :] + caption[row].astype(jnp.float32)
        allowed = jnp.broadcast_to(cells, (80, cell_ok.shape[1])) > 0
        stacked = [stack(wide[rows, c], first, second).astype(jnp.bfloat16) for c in cols]
        scores = [nt(both, keys[which, :, c]) * HEAD_DIM ** (-0.5) for both, c in zip(stacked, cols)]
        weights = [softmax(jnp.where(allowed, score, -1000000000.0)) for score in scores]
        mixed = [merge(low, nn(weight, values[which, :, c])) for weight, c in zip(weights, cols)]
        for tile, c in enumerate(cols):
            probs[row, tile] = weights[tile]
            wide[rows, c] = mixed[tile]


def prepare(counts, lengths, boxes, vectors, cells_all, image, caption, cell_ok, norms, near, plane):
    rows, padded = cell_ok.shape
    cells, images, _ = cells_all.shape
    window = near.shape[0]
    start = jnp.minimum(plane * rows // ROWS_MAX, images - window)

    @pl.loop(0, rows)
    def _(r):
        row = plane * rows + r
        end, here, before = jnp.int32(0), jnp.int32(0), jnp.int32(0)
        for i in range(images):
            end = end + counts[0, i]
            here = here + (end <= row).astype(jnp.int32)
            before = before + (end <= row - 1).astype(jnp.int32)
        image[r] = jnp.minimum(jnp.maximum(here - start, 0), window - 1)
        caption[r] = jnp.where(row == 0, jnp.int32(1), here - before)

    cell_ok[...] = jnp.full(cell_ok.shape, -2.0, jnp.float32)
    cell_ok[:, :cells] = (boxes[pl.ds(pl.multiple_of(plane * rows, 8), rows), :] > 0).astype(jnp.float32)
    norms[...] = jnp.zeros_like(norms)
    for i, vector in enumerate(vectors):
        norms[pl.ds(i, 1), :] = vector[...].reshape(1, norms.shape[1])
    step = 16
    for first in range(0, padded, step):
        amount = min(step, cells - first)
        to = lax.broadcasted_iota(jnp.int32, (window * step, amount * images), 0)
        source = lax.broadcasted_iota(jnp.int32, (window * step, amount * images), 1)
        pick = (source // images == to % step) & (source % images == to // step + start)
        block = cells_all[first : first + amount].reshape(amount * images, cells_all.shape[2])
        block = nn(pick.astype(jnp.bfloat16), block).astype(jnp.bfloat16)
        near[:, first : first + step, :] = block.reshape(window, step, cells_all.shape[2])


def forward_steps(ticks, image, caption, lengths, tokens, near, cell_ok, weights, norms, saved, wide):
    bf16 = jnp.bfloat16
    self_weights, cross_weights, keyval = weights
    (
        queries, keys, values, self_probs, self_context, first_unit, first_inverse, first_low, cross_queries, image_keys,
        image_values, cross_probs, cross_context, second_unit, second_inverse, second_value, second_low,
    ) = (slot.near for slot in saved)

    def flush(*places):
        for place in places:
            saved[place].flush()

    gains = [norms.at[pl.ds(i, 1), :] for i in range(4)]
    ticks.wait(0)
    for target, which in ((queries, 0), (keys, 1), (values, 2)):
        target[...] = nt(tokens[...], part(self_weights, which)).astype(bf16)
    flush(0, 1, 2)
    ticks()
    attend_self(queries, keys, values, lengths, self_probs, self_context)
    flush(3, 4)
    ticks()
    second_value[...] = nn(self_context[...], part(self_weights, 3)) + tokens[...].astype(jnp.float32)
    norm_forward(second_value, first_unit, first_inverse, None, first_low, gains[0], gains[1])
    flush(5, 6, 7)
    ticks.wait(1)
    cross_queries[...] = nt(first_low[...], part(cross_weights, 0)).astype(bf16)
    flush(8)
    wide[...] = cross_queries[...].astype(jnp.float32)
    images, cells, depth = near.shape
    half = images // 2
    ticks.wait(2)
    for target, which in ((image_keys, 0), (image_values, 1)):
        weight = part(keyval, which)
        for step in range(2):
            block = near[step * half : (step + 1) * half].reshape(half * cells, depth)
            target[step * half : (step + 1) * half] = nt(block, weight).astype(bf16).reshape(half, cells, -1)
        flush(9 + which)
    ticks()
    rows = cell_ok.shape[0]
    for part_of in range(2):
        begin, end = part_of * rows // 2, (part_of + 1) * rows // 2
        attend_cross(image, caption, wide, image_keys, image_values, cell_ok, cross_probs, begin, end)
        ticks()
    flush(11)
    cross_context[...] = wide[...].astype(bf16)
    flush(12)
    second_value[...] = nn(cross_context[...], part(cross_weights, 1)) + (first_unit[...] * gains[0][...] + gains[1][...])
    norm_forward(second_value, second_unit, second_inverse, second_value, second_low, gains[2], gains[3])
    flush(13, 14, 15, 16)


def feed_kernel(scalars, inputs, outputs, scratch):
    second_value, second_low, norms, expand, shrink, cotangent = inputs
    joined, expand_grad, shrink_grad, vectors, second_up = outputs
    active, slope, unit, inverse, feed_low = scratch
    bf16 = jnp.bfloat16
    total = second_up.near
    total[...] = second_value.ready()[...]
    second_low, norms = second_low.ready(), norms.ready()
    gain, shift = norms.at[0, pl.ds(4, 1), :], norms.at[0, pl.ds(5, 1), :]
    hidden, amount = expand.near.shape[0], total.shape[0]
    halves = [slice(0, amount // 2), slice(amount // 2, amount)]

    @pl.loop(0, hidden)
    def _(m):
        expand.copy(False, m).wait()
        shrink.copy(False, m).wait()
        inners = [nn(second_low[rows, :], expand.near[m]) + norms[m, pl.ds(6, 1), :] for rows in halves]
        shares = [0.5 * (1.0 + lax.erf(inner * 0.5**0.5)) for inner in inners]
        acts = [(inner * share).astype(bf16) for inner, share in zip(inners, shares)]
        slopes = [
            (share + inner * (jnp.exp(-0.5 * inner * inner) * 0.3989422804014327)).astype(bf16)
            for inner, share in zip(inners, shares)
        ]
        for rows, act, inclination in zip(halves, acts, slopes):
            active[m, rows, :] = act
            slope[m, rows, :] = inclination
            total[rows, :] += nn(act, shrink.near[m])

    norm_forward(total, unit, inverse, None, joined.near, gain, shift)
    joined.flush()
    sums = vectors.near
    sums[...] = jnp.zeros_like(sums)
    norm_reverse(
        cotangent.ready(), unit, inverse, gain, sums.at[pl.ds(8, 1), :], sums.at[pl.ds(9, 1), :], total, feed_low
    )

    @pl.loop(0, hidden)
    def _(m):
        shrink_grad.near[m] = tn(active[m], feed_low[...]).astype(bf16)
        shrink_grad.flush(m)
        lows = [
            (nt(feed_low[rows, :], shrink.near[m]) * slope[m, rows, :].astype(jnp.float32)).astype(bf16) for rows in halves
        ]
        parts = [jnp.sum(low.astype(jnp.float32), axis=0, keepdims=True) for low in lows]
        sums[pl.ds(m, 1), :] = parts[0] + parts[1]
        for rows, low in zip(halves, lows):
            active[m, rows, :] = low
        expand_grad.near[m] = tn(second_low[...], active[m]).astype(bf16)
        expand_grad.flush(m)
        total[...] += nt(active[m], expand.near[m])

    vectors.flush()
    second_up.flush()


def score_back(weights, upstream):
    probs = weights.astype(jnp.float32)
    return (probs * (upstream - jnp.sum(probs * upstream, axis=-1, keepdims=True))).astype(jnp.bfloat16)


def cross_back_kernel(scalars, inputs, outputs, scratch):
    (image,) = scalars
    (
        second_up, second_unit, second_inverse, norms, cross_weights, cross_context, cross_queries, image_values,
        image_keys, cross_probs, first_low, keyval, near,
    ) = inputs
    weights_grad, keyval_grad, patch, vectors, first_up = outputs
    grad_low, wide, turn, key_sum, value_sum, query_low = scratch
    bf16 = jnp.bfloat16
    low, first, second = lanes()
    sums = vectors.near
    sums[...] = jnp.zeros_like(sums)
    norm_reverse(
        second_up.ready(), second_unit.ready(), second_inverse.ready(), norms.ready().at[0, pl.ds(2, 1), :],
        sums.at[pl.ds(6, 1), :], sums.at[pl.ds(7, 1), :], first_up.near, grad_low,
    )
    vectors.flush()
    cross_weights = cross_weights.ready()
    wide[...] = nt(grad_low[...], part(cross_weights, 1)).astype(bf16).astype(jnp.float32)
    store_part(weights_grad.near, 1, tn(cross_context.ready()[...], grad_low[...]))
    turn[...] = cross_queries.ready()[...].astype(jnp.float32)
    key_sum[...] = jnp.zeros_like(key_sum)
    value_sum[...] = jnp.zeros_like(value_sum)
    cols = columns(wide.shape[1])
    image_values, image_keys, cross_probs = image_values.ready(), image_keys.ready(), cross_probs.ready()

    @pl.loop(0, cross_probs.shape[0])
    def _(row):
        rows = pl.ds(pl.multiple_of(row * 40, 40), 40)
        which = image[row]
        queries = [stack(turn[rows, c], first, second).astype(bf16) for c in cols]
        grads = [stack(wide[rows, c], first, second).astype(bf16) for c in cols]
        weights = [cross_probs[row, tile] for tile in range(len(cols))]
        upstream = [nt(grad, image_values[which, :, c]) for grad, c in zip(grads, cols)]
        back = [score_back(weight, up) for weight, up in zip(weights, upstream)]
        mixed = [merge(low, nn(grad, image_keys[which, :, c])) * HEAD_DIM ** (-0.5) for grad, c in zip(back, cols)]
        key_parts = [tn(grad, both) * HEAD_DIM ** (-0.5) for grad, both in zip(back, queries)]
        value_parts = [tn(weight, grad) for weight, grad in zip(weights, grads)]
        for tile, c in enumerate(cols):
            turn[rows, c] = mixed[tile]
        for tile, c in enumerate(cols):
            key_sum[which, :, c] += key_parts[tile]
        for tile, c in enumerate(cols):
            value_sum[which, :, c] += value_parts[tile]

    keyval, near = keyval.ready(), near.ready()
    images, cells, depth = near.shape
    amount = images * cells
    quarter, size, half = patch.near.shape[2], (patch.near.shape[1] - 16) // images, images // 2
    last = jnp.zeros((16, depth), jnp.float32)
    for step in range(2):
        here = slice(step * half, (step + 1) * half)
        block = nn(key_sum[here].astype(bf16).reshape(amount // 2, -1), part(keyval, 0))
        block += nn(value_sum[here].astype(bf16).reshape(amount // 2, -1), part(keyval, 1))
        block = block.astype(bf16)
        row = lax.broadcasted_iota(jnp.int32, (16, amount // 2), 0)
        source = lax.broadcasted_iota(jnp.int32, (16, amount // 2), 1)
        last += nn((source == (row - step * half) * cells + size).astype(bf16), block)
        for m in range(patch.near.shape[0]):
            for i in range(half):
                rows = pl.ds((step * half + i) * size, size)
                patch.near[m, rows, :] = block[i * cells : i * cells + size, m * quarter : (m + 1) * quarter]
    for m in range(patch.near.shape[0]):
        patch.near[m, pl.ds(images * size, 16), :] = last[:, m * quarter : (m + 1) * quarter].astype(bf16)
    patch.flush()
    for source, which in ((key_sum, 0), (value_sum, 1)):
        flat = source[...].astype(bf16).reshape(amount, -1)
        store_part(keyval_grad.near, which, tn(flat, near[...].reshape(amount, depth)))
    keyval_grad.flush()
    query_low[...] = turn[...].astype(bf16)
    first_up.near[...] += nn(query_low[...], part(cross_weights, 0))
    first_up.flush()
    store_part(weights_grad.near, 0, tn(query_low[...], first_low.ready()[...]))
    weights_grad.flush()


def self_back_steps(ticks, inputs, weights_grad, sums, text_grad, scratch):
    (
        first_up, first_unit, first_inverse, norms, self_weights, self_context, queries, keys, values, self_probs, tokens,
    ) = inputs
    grad_low, context_low, query_low, key_low, value_low = scratch
    bf16 = jnp.bfloat16
    low, first, second = lanes()
    first_mask, second_mask = first.astype(bf16), second.astype(bf16)
    norm_reverse(
        first_up.ready(), first_unit.ready(), first_inverse.ready(), norms.ready().at[0, pl.ds(0, 1), :],
        sums.at[pl.ds(4, 1), :], sums.at[pl.ds(5, 1), :], text_grad, grad_low,
    )
    self_weights = self_weights.ready()
    context_low[...] = nt(grad_low[...], part(self_weights, 3)).astype(bf16)
    store_part(weights_grad, 3, tn(self_context.ready()[...], grad_low[...]))
    cols = columns(context_low.shape[1])
    queries, keys, values, self_probs = queries.ready(), keys.ready(), values.ready(), self_probs.ready()
    ticks()

    @pl.loop(0, self_probs.shape[0])
    def _(pair):
        rows = pl.ds(pl.multiple_of(pair * 80, 80), 80)
        stacked = [stack(queries[rows, c], first_mask, second_mask) for c in cols]
        grads = [stack(context_low[rows, c], first_mask, second_mask) for c in cols]
        weights = [self_probs[pair, tile] for tile in range(len(cols))]
        upstream = [nt(grad, values[rows, c]) for grad, c in zip(grads, cols)]
        back = [score_back(weight, up) for weight, up in zip(weights, upstream)]
        query_parts = [merge(low, nn(grad, keys[rows, c])) * HEAD_DIM ** (-0.5) for grad, c in zip(back, cols)]
        key_parts = [tn(grad, both) * HEAD_DIM ** (-0.5) for grad, both in zip(back, stacked)]
        value_parts = [tn(weight, grad) for weight, grad in zip(weights, grads)]
        for tile, c in enumerate(cols):
            query_low[rows, c] = query_parts[tile].astype(bf16)
            key_low[rows, c] = key_parts[tile].astype(bf16)
            value_low[rows, c] = value_parts[tile].astype(bf16)

    ticks()
    tokens = tokens.ready()
    for source, which in ((query_low, 0), (key_low, 1), (value_low, 2)):
        store_part(weights_grad, which, tn(source[...], tokens[...]))
        text_grad[...] += nn(source[...], part(self_weights, which))


def lone_self_back_kernel(scalars, inputs, outputs, scratch):
    weights_grad, vectors, text_grad = outputs
    vectors.near[...] = jnp.zeros_like(vectors.near)
    self_back_steps(Alone(), inputs, weights_grad.near, vectors.near, text_grad.near, scratch)
    for slot in outputs:
        slot.flush()


def finish_kernel(alone, scalars, inputs, outputs, scratch):
    self_sum, cross_sum, keyval_sum, expand_sum, shrink_sum, vectors, windows, merged, text = inputs
    text_grad, project, self_out, query, cross_out, keyval, expand, shrink, patch_grad, *norms, bias = outputs
    inner = self_out.near.shape[0]

    def give(output, value):
        output.near[...] = value.astype(jnp.float32)
        output.flush()

    give(text_grad, text.ready()[...])
    give(shrink, shrink_sum.ready()[...])
    give(expand, expand_sum.ready()[...])
    give(project, self_sum.ready()[: 3 * inner, :])
    give(self_out, self_sum.near[3 * inner :, :])
    give(query, cross_sum.ready()[:inner, :])
    give(cross_out, cross_sum.near[inner:, :])
    give(keyval, keyval_sum.ready()[...])
    sums = vectors.ready().at[vectors.near.shape[0] - 1]
    for i, output in enumerate(norms):
        give(output, sums[4 + i : 5 + i, :].reshape(sums.shape[1]))
    plane = lax.axis_index("mp")
    give(bias, sums[pl.ds(plane, 1), :].reshape(sums.shape[1]))
    windows, merged = windows.ready(), merged.ready()
    cells, images, quarter = patch_grad.near.shape
    size, step, rows = cells - 1, 16, scalars[0].shape[0]
    amount = (windows.shape[1] - step) // size

    def first_image(m):
        return jnp.minimum(m * rows // ROWS_MAX, images - amount)

    def place(sources):
        for first in range(0, size, step):
            total = jnp.zeros((step * images, quarter), jnp.float32)
            for window, start in sources:
                count = (window.shape[0] - step) // size
                to = lax.broadcasted_iota(jnp.int32, (step * images, count * step), 0)
                source = lax.broadcasted_iota(jnp.int32, (step * images, count * step), 1)
                pick = (to // images == source % step) & (to % images == source // step + start)
                block = [window[pl.ds(i * size + first, step), :] for i in range(count)]
                total = total + nn(pick.astype(jnp.bfloat16), jnp.concatenate(block, axis=0))
            patch_grad.near[first : first + step] = total.reshape(step, images, quarter)
        total = jnp.zeros((images, quarter), jnp.float32)
        for window, start in sources:
            count = (window.shape[0] - step) // size
            to = lax.broadcasted_iota(jnp.int32, (images, step), 0)
            source = lax.broadcasted_iota(jnp.int32, (images, step), 1)
            pick = (to == source + start) & (source < count)
            total = total + nn(pick.astype(jnp.bfloat16), window[pl.ds(count * size, step), :])
        patch_grad.near[size] = total

    if alone:
        place([(windows.at[m], first_image(m)) for m in range(4)])
    else:
        outer = (plane == 0) | (plane == 3)

        @pl.when(outer)
        def _():
            beside = jnp.where(plane == 0, 1, 2)
            place(
                [(windows.at[m], first_image(m)) for m in (plane, beside)]
                + [(merged, jnp.where(plane == 0, first_image(2), first_image(0)))]
            )

        @pl.when(jnp.logical_not(outer))
        def _():
            place([(windows.at[m], first_image(m)) for m in range(4)])

    patch_grad.flush()


def image_windows(parts, rows, group_images):
    group_rows = parts * rows
    first = [m * rows // ROWS_MAX for m in range(parts)]
    last = [group_images - 1 - max(0, -(-(group_rows - (m + 1) * rows - (ROWS_MAX - 1)) // ROWS_MAX)) for m in range(parts)]
    last = [min(stop, (m + 1) * rows - 1) for m, stop in enumerate(last)]
    window = max(stop - start + 1 for start, stop in zip(first, last))
    return [min(start, group_images - window) for start in first], window


def forward(scalars, inputs, cells_all, shards, outputs, near, chunks, own):
    if own:
        return gather_forward(scalars, inputs, cells_all, shards, outputs, near, chunks)
    weights = [lax.all_gather(jnp.concatenate(pieces, axis=0), "mp", axis=0) for pieces in shards]
    vectors = jnp.stack(inputs[2:] + [jnp.zeros_like(inputs[2])])
    biases = lax.all_gather(vectors, "mp", axis=0)
    amount, width = inputs[0].shape
    rows = amount // 40
    image, *saved = on_slots(
        lone_forward_kernel, "forward", scalars, inputs + [cells_all] + weights[:3], outputs + [near],
        [((amount, width), jnp.float32), ((rows, near[0][1]), jnp.float32), ((8, width), jnp.float32)]
        + [pltpu.SMEM((rows,), jnp.int32)],
        counted=rows,
    )
    return image, weights, biases, saved[:-1], saved[-1]


def reduce_shards(grads, patch, early, inputs, window, shift, chunks, own):
    if own:
        return reduce_back(grads, patch, early, inputs, window, shift, chunks)
    flat, weights = inputs[0].shape, inputs[4].shape
    self_grad, late, text_grad = on_slots(
        lone_self_back_kernel, "self_back", [], inputs,
        [(weights, jnp.bfloat16), (early[0].shape, jnp.float32), (flat, jnp.float32)], [(flat, jnp.bfloat16)] * 5,
    )
    sums = [
        lax.psum(lax.psum_scatter(grad.astype(jnp.float32), "mp", scatter_dimension=0, tiled=True)[0], "dp").astype(grad.dtype)
        for grad in [self_grad] + grads
    ]
    windows = lax.all_to_all(patch, "mp", split_axis=0, concat_axis=0, tiled=True)
    return sums, windows, windows[0], lax.psum(early[0] + early[1] + late, ("dp", "mp"))[None], text_grad


def per_device(
    tokens, patches, image_rows, row_lengths, box_mask, self_project, self_output, first_gain, first_shift, cross_query,
    cross_keyval, cross_output, second_gain, second_shift, expand_weight, expand_bias, shrink_weight, third_gain,
    third_shift, cotangent, *, parts, own,
):
    bf16, f32 = jnp.bfloat16, jnp.float32
    rows, slots, width = tokens.shape
    group_images, cells, depth = patches.shape
    starts, window = image_windows(parts, rows, group_images)
    padded = -(-cells // 16) * 16
    amount, pairs, tiles_of = rows * slots, rows // 2, width // 128
    inner = self_output.shape[0]
    shards = [
        [self_project.transpose(0, 2, 1).reshape(3 * inner, width), self_output],
        [cross_query.T, cross_output],
        [cross_keyval.transpose(0, 2, 1).reshape(2 * inner, depth)],
        [expand_weight],
        [shrink_weight],
    ]
    chunks = [(0, 0, 384), (0, 384, 384), (1, 0, 384), (2, 0, 384), (3, 0, 384), (3, 384, 384), (4, 0, 384), (4, 384, 384)]
    text = tokens.reshape(amount, width)
    flat, unit_row = (amount, width), ((amount, 128), f32)
    low_flat, full_flat = (flat, bf16), (flat, f32)
    probs_self, probs_cross = (pairs, tiles_of, 4 * slots, 2 * slots), (rows, tiles_of, 2 * slots, padded)
    image_part, vector = ((window, padded, width), bf16), ((16, width), f32)
    image, weights, norms, saved, near = forward(
        [image_rows, row_lengths],
        [text, box_mask, first_gain, first_shift, second_gain, second_shift, third_gain, third_shift, expand_bias],
        patches.transpose(1, 0, 2),
        shards,
        [low_flat] * 3 + [(probs_self, bf16), low_flat, full_flat, unit_row, low_flat, low_flat]
        + [image_part, image_part, (probs_cross, bf16), low_flat, full_flat, unit_row, full_flat, low_flat],
        ((window, padded, depth), bf16),
        chunks,
        own,
    )
    self_weights, cross_weights, keyval, expand, shrink = weights
    (
        queries, keys, values, self_probs, self_context, first_unit, first_inverse, first_low, cross_queries, image_keys,
        image_values, cross_probs, cross_context, second_unit, second_inverse, second_value, second_low,
    ) = saved
    joined, expand_grad, shrink_grad, feed_vectors, second_up = on_slots(
        feed_kernel,
        "feed",
        [],
        [second_value, second_low, norms, expand, shrink, cotangent.reshape(flat)],
        [low_flat, (expand.shape, bf16), (shrink.shape, bf16), vector, full_flat],
        [((parts,) + flat, bf16)] * 2 + [full_flat, unit_row, low_flat],
        parts_in=(3, 4),
        parts_out=(1, 2),
    )
    cross_weights_grad, keyval_grad, patch, cross_vectors, first_up = on_slots(
        cross_back_kernel,
        "cross_back",
        [image],
        [second_up, second_unit, second_inverse, norms, cross_weights, cross_context, cross_queries, image_values]
        + [image_keys, cross_probs, first_low, keyval, near],
        [(cross_weights.shape, bf16), (keyval.shape, bf16), ((parts, window * (cells - 1) + 16, depth // parts), bf16)]
        + [vector, full_flat],
        [low_flat, full_flat, full_flat, (image_part[0], f32), (image_part[0], f32), low_flat],
    )
    order = [(4, 0, 384), (4, 384, 384), (3, 0, 384), (3, 384, 384), (1, 0, 384), (2, 0, 384), (0, 0, 384), (0, 384, 384)]
    sums, windows, merged, vectors, text_grad = reduce_shards(
        [cross_weights_grad, keyval_grad, expand_grad, shrink_grad],
        patch,
        [feed_vectors, cross_vectors],
        [first_up, first_unit, first_inverse, norms, self_weights, self_context, queries, keys, values, self_probs, text],
        window,
        starts[1] - starts[0],
        order,
        own,
    )
    square, piece, line = ((width, width), f32), ((inner, width), f32), ((width,), f32)
    text_grad, project, self_out, query, cross_out, pixel, expand_sum, shrink_sum, patch_grad, *lines = on_slots(
        functools.partial(finish_kernel, not own),
        "finish",
        [image],
        list(sums) + [vectors, windows, merged, text_grad],
        [full_flat, ((3 * inner, width), f32), piece, piece, piece, ((2 * inner, depth), f32), square, square]
        + [((cells, group_images, depth // parts), f32)]
        + [line] * 7,
        [],
    )
    return (
        joined.reshape(tokens.shape),
        text_grad.reshape(tokens.shape),
        patch_grad.transpose(1, 0, 2),
        project.reshape(3, inner, width).transpose(0, 2, 1),
        self_out,
        lines[0],
        lines[1],
        query.T,
        pixel.reshape(2, inner, depth).transpose(0, 2, 1),
        cross_out,
        lines[2],
        lines[3],
        expand_sum,
        lines[6],
        shrink_sum,
        lines[4],
        lines[5],
    )


def solution(mesh):
    parts = mesh.shape["mp"]
    own = mesh.shape["dp"] == 8 and parts == 4
    return jax.shard_map(
        functools.partial(per_device, parts=parts, own=own),
        mesh=mesh,
        in_specs=(
            P(("dp", "mp"), None, None),
            P("dp", None, None),
            P("dp", None),
            P("dp"),
            P("dp", None),
            P(None, None, "mp"),
            P("mp", None),
            P(),
            P(),
            P(None, "mp"),
            P(None, None, "mp"),
            P("mp", None),
            P(),
            P(),
            P(None, "mp"),
            P("mp"),
            P("mp", None),
            P(),
            P(),
            P(("dp", "mp"), None, None),
        ),
        out_specs=(
            P(("dp", "mp"), None, None),
            P(("dp", "mp"), None, None),
            P("dp", None, "mp"),
            P(None, None, "mp"),
            P("mp", None),
            P(),
            P(),
            P(None, "mp"),
            P(None, None, "mp"),
            P("mp", None),
            P(),
            P(),
            P(None, "mp"),
            P("mp"),
            P("mp", None),
            P(),
            P(),
        ),
        check_vma=False,
    )
```

```python
import functools

import jax
import jax.numpy as jnp
from jax import lax
from jax.experimental import pallas as pl
from jax.experimental.pallas import tpu as pltpu
from jax.sharding import PartitionSpec as P

HEAD_DIM = 64
ROWS_MAX = 7
MESH = pl.DeviceIdType.MESH


def place():
    index = lax.axis_index("dp")
    plane = lax.axis_index("mp")
    y, x, c = index // 4, (index // 2) % 2, index % 2
    return index, plane, y, x, c


def partners(index, plane):
    core = (index + 1 - 2 * (index % 2), plane)
    across = (index + 2 - 4 * ((index // 2) % 2), plane)
    along = (index + 4 - 8 * (index // 4), plane)
    planes = [(index, lax.rem(plane + step, 4)) for step in (1, 2, 3)]
    return core, across, along, planes


def greet(peers):
    barrier = pltpu.get_barrier_semaphore()
    for peer in peers:
        pl.semaphore_signal(barrier, inc=1, device_id=peer, device_id_type=MESH)
    pl.semaphore_wait(barrier, len(peers))


class Sends:
    def __init__(self):
        self.stages, self.all = {}, []

    def start(self, name, k, items):
        copies = []
        for source, target, sends, recvs, peer in items:
            copy = pltpu.make_async_remote_copy(
                src_ref=source, dst_ref=target, send_sem=sends, recv_sem=recvs, device_id=peer, device_id_type=MESH
            )
            copy.start()
            copies.append(copy)
        self.stages[name, k] = copies
        self.all.extend(copies)

    def arrived(self, name, k):
        for copy in self.stages[name, k]:
            copy.wait_recv()

    def close(self):
        for copy in self.all:
            copy.wait_send()


class Gather:
    stages = 4

    def __init__(self, chunks, shards, wholes, sems, window, gap):
        self.chunks, self.shards, self.wholes, self.window = chunks, shards, wholes, window
        self.sems, self.gap = sems, gap
        self.index, self.plane, self.y, self.x, self.c = place()
        self.core, self.across, self.along, self.planes = partners(self.index, self.plane)
        self.others = [lax.rem(self.plane + step, 4) for step in (1, 2, 3)]
        self.sends = Sends()

    def sizes(self, k):
        which, base, rows = self.chunks[k]
        return which, base, rows // 8, self.wholes[which].shape[2] // 2

    def level(self, k):
        which, base, r, w = self.sizes(k)
        _, _, send, recv = self.sems[:4]
        self.own(which)
        items = []
        for h, first in enumerate((self.x * 2 + self.y, self.y * 2 + self.x)):
            here = (pl.ds(pl.multiple_of(base + (self.c * 4 + first) * r, 16), r), pl.ds(h * w, w))
            for j, peer in enumerate(self.planes):
                piece = self.wholes[which].at[(self.plane,) + here]
                items.append((piece, piece, send.at[k, h, j], recv.at[k, h, j], peer))
        self.sends.start("level", k, items)

    def near(self, k):
        which, base, r, w = self.sizes(k)
        send, recv = self.sems[4:6]
        self.sends.arrived("level", k)
        if k + self.window < len(self.chunks):
            self.level(k + self.window)
        items = []
        for h, first in enumerate((self.x * 2 + self.y, self.y * 2 + self.x)):
            row = pl.multiple_of(base + (self.c * 4 + first) * r, 16)
            for j, other in enumerate(self.others):
                piece = self.wholes[which].at[other, pl.ds(row, r), pl.ds(h * w, w)]
                items.append((piece, piece, send.at[k, h, j], recv.at[k, h, j], (self.along, self.across)[h]))
        self.sends.start("near", k, items)

    def far(self, k):
        which, base, r, w = self.sizes(k)
        send, recv = self.sems[6:8]
        self.sends.arrived("near", k)
        items = []
        for h, first in enumerate((self.x, self.y)):
            row = pl.multiple_of(base + (self.c * 4 + first * 2) * r, 16)
            for j, other in enumerate(self.others):
                piece = self.wholes[which].at[other, pl.ds(row, 2 * r), pl.ds(h * w, w)]
                items.append((piece, piece, send.at[k, h, j], recv.at[k, h, j], (self.across, self.along)[h]))
        self.sends.start("far", k, items)

    def cross(self, k):
        which, base, r, w = self.sizes(k)
        send, recv = self.sems[8:10]
        self.sends.arrived("far", k)
        row = pl.multiple_of(base + self.c * 4 * r, 16)
        items = []
        for j, other in enumerate(self.others):
            piece = self.wholes[which].at[other, pl.ds(row, 4 * r), :]
            items.append((piece, piece, send.at[k, j], recv.at[k, j], self.core))
        self.sends.start("core", k, items)

    def own(self, which):
        for copy in self.local.pop(which, ()):
            copy.wait()

    def begin(self):
        self.local = {}
        for which, pieces in enumerate(self.shards):
            row, self.local[which] = 0, []
            for i, piece in enumerate(pieces):
                target = self.wholes[which].at[self.plane, pl.ds(row, piece.shape[0]), :]
                copy = pltpu.make_async_copy(piece, target, self.sems[0].at[which, i])
                copy.start()
                self.local[which].append(copy)
                row += piece.shape[0]
        greet([self.core, self.across, self.along] + self.planes)
        for k in range(self.window):
            self.level(k)

    def step(self, t):
        if 0 <= t - 2 * self.gap < len(self.chunks):
            self.cross(t - 2 * self.gap)
        if 0 <= t - self.gap < len(self.chunks):
            self.far(t - self.gap)
        if 0 <= t < len(self.chunks):
            self.near(t)

    @property
    def steps(self):
        return len(self.chunks) + 2 * self.gap

    def ready(self, k):
        self.sends.arrived("core", k)

    @staticmethod
    def scratch(count, total):
        dma = pltpu.SemaphoreType.DMA
        return [dma((count, 2)), dma((count,))] + [dma((total, 2, 3))] * 6 + [dma((total, 3))] * 2


class Ticks:
    def __init__(self, gather, outs, sem):
        self.gather, self.outs, self.sem = gather, outs, sem
        self.now, self.done, self.final = 0, 0, []

    def __call__(self):
        gather, total = self.gather, len(self.gather.chunks)
        if self.now < gather.steps:
            gather.step(self.now)
        k = self.now - 3 * gather.gap
        if 0 <= k < total:
            gather.ready(k)
            self.done = k + 1
            which = gather.chunks[k][0]
            if k + 1 == total or gather.chunks[k + 1][0] != which:
                copy = pltpu.make_async_copy(gather.wholes[which], self.outs[which], self.sem.at[which])
                copy.start()
                self.final.append(copy)
        self.now += 1

    def wait(self, which):
        last = max(k for k, chunk in enumerate(self.gather.chunks) if chunk[0] == which)
        while self.done <= last:
            self()

    def close(self):
        while self.done < len(self.gather.chunks):
            self()
        self.gather.sends.close()
        for copy in self.final:
            copy.wait()


def forward_kernel(chunks, pieces, count, *refs):
    counts, lengths, tokens, boxes = refs[:4]
    vectors, cells_far, refs = refs[4:11], refs[11], refs[12:]
    shards, arrays = [], len(pieces)
    for amount in pieces:
        shards.append(refs[:amount])
        refs = refs[amount:]
    image, outs, biases, refs = refs[0], refs[1 : arrays + 1], refs[arrays + 1], refs[arrays + 2 :]
    far, refs = refs[: count + 1], refs[count + 1 :]
    wholes, refs = refs[:arrays], refs[arrays:]
    saved = [Slot(far[i], refs[2 * i], refs[2 * i + 1]) for i in range(count + 1)]
    *saved, near = saved
    refs = refs[2 * count + 2 :]
    (wide, cells_all, cell_ok, norms, caption, bias_send, bias_recv, cells_sem), sems = refs[:8], refs[8:]
    gather = Gather(chunks, shards, wholes, sems, 3, 1)
    copy = pltpu.make_async_copy(cells_far, cells_all, cells_sem)
    copy.start()
    gather.begin()
    copy.wait()
    prepare(counts, lengths, boxes, vectors, cells_all, image, caption, cell_ok, norms, near.near, gather.plane)
    near.flush()
    gather.sends.start(
        "bias", 0, [(norms, biases.at[gather.plane], bias_send.at[j], bias_recv.at[j], peer) for j, peer in enumerate(gather.planes)]
    )
    biases[gather.plane] = norms[...]
    ticks = Ticks(gather, outs, sems[1])
    rows = cell_ok.shape[0]
    forward_steps(
        ticks, image, caption, lambda r: lengths[gather.plane * rows + r], tokens, near.near, cell_ok, wholes[:3], norms, saved,
        wide,
    )
    gather.sends.arrived("bias", 0)
    ticks.close()
    for slot in saved + [near]:
        slot.finish()


def gather_forward(scalars, inputs, cells_all, shards, outputs, near, chunks):
    dma, bf16, f32, arrays, count = pltpu.SemaphoreType.DMA, jnp.bfloat16, jnp.float32, len(shards), len(outputs)
    any_space, vmem = pl.BlockSpec(memory_space=pl.ANY), pl.BlockSpec(memory_space=pltpu.VMEM)
    smem = pl.BlockSpec(memory_space=pltpu.SMEM)
    tokens = inputs[0]
    width = tokens.shape[1]
    rows, padded = tokens.shape[0] // 40, near[0][1]
    shapes = [(4, sum(piece.shape[0] for piece in pieces), pieces[0].shape[1]) for pieces in shards]
    flat = [piece for pieces in shards for piece in pieces]
    outputs = outputs + [near]
    results = pl.pallas_call(
        functools.partial(forward_kernel, chunks, [len(pieces) for pieces in shards], count),
        out_shape=[jax.ShapeDtypeStruct((rows,), jnp.int32)]
        + [jax.ShapeDtypeStruct(shape, bf16) for shape in shapes]
        + [jax.ShapeDtypeStruct((4, 8, width), f32)]
        + [jax.ShapeDtypeStruct(shape, kind) for shape, kind in outputs],
        in_specs=[smem] * len(scalars) + [vmem] * len(inputs) + [any_space] * (len(flat) + 1),
        out_specs=[smem] + [any_space] * arrays + [vmem] + [any_space] * (count + 1),
        scratch_shapes=[pltpu.VMEM(shape, bf16) for shape in shapes]
        + [entry for shape, kind in outputs for entry in slot_scratch(shape, kind)]
        + [pltpu.VMEM(tokens.shape, f32), pltpu.VMEM(cells_all.shape, bf16), pltpu.VMEM((rows, padded), f32)]
        + [pltpu.VMEM((8, width), f32), pltpu.SMEM((rows,), jnp.int32)]
        + [dma((3,)), dma((3,)), dma(())]
        + Gather.scratch(arrays, len(chunks)),
        compiler_params=pltpu.CompilerParams(collective_id=0, has_side_effects=True, vmem_limit_bytes=63 << 20),
        name="gather_forward",
    )(*scalars, *inputs, cells_all, *flat)
    return results[0], results[1 : arrays + 1], results[arrays + 1], results[arrays + 2 : -1], results[-1]


class Alone:
    def __call__(self):
        pass

    def wait(self, which):
        pass


def lone_forward_kernel(scalars, inputs, outputs, scratch):
    tokens, boxes, *vectors, cells_all, self_weights, cross_weights, keyval = (slot.ready() for slot in inputs)
    *saved, near = outputs
    counts, lengths, image = scalars
    wide, cell_ok, norms, caption = scratch
    rows, plane = cell_ok.shape[0], lax.axis_index("mp")
    prepare(counts, lengths, boxes, vectors, cells_all, image, caption, cell_ok, norms, near.near, plane)
    near.flush()
    forward_steps(
        Alone(), image, caption, lambda r: lengths[plane * rows + r], tokens, near.near, cell_ok,
        (self_weights, cross_weights, keyval), norms, saved, wide,
    )


class Reduce:
    def __init__(self, chunks, grads, sums, buffers, sems, local):
        self.chunks, self.grads, self.sums, self.sems, self.local = chunks, grads, sums, sems, local
        self.mine, self.core_in, self.near_in, self.far_in, self.plane_in, self.relay_in = [], [], [], [], [], []
        buffers = list(buffers)
        self.index, self.plane, self.y, self.x, self.c = place()
        for which, base, rows in chunks:
            if which in local:
                self.mine.append((local[which], base + self.c * (rows // 2)))
            else:
                self.mine.append((buffers.pop(0), 0))
            self.core_in.append(buffers.pop(0))
            self.near_in.append(buffers.pop(0))
            self.far_in.append(buffers.pop(0))
            self.plane_in.append(buffers.pop(0))
            self.relay_in.append(buffers.pop(0))
        self.core, self.across, self.along, self.planes = partners(self.index, self.plane)
        self.others = [lax.rem(self.plane + step, 4) for step in (1, 2, 3)]
        self.sends = Sends()
        self.outer = (self.plane == 0) | (self.plane == 3)
        self.next = jnp.where(self.plane == 0, 1, 2)
        self.beyond = 3 - self.next
        self.edge = jnp.where(self.plane == 1, 0, 3)
        self.fetched, self.final = {}, []
        self.diagonal = (self.index + 6 - 4 * self.x - 8 * self.y, self.plane)
        self.short = range(len(chunks) - 2, len(chunks))
        long = [self.begin, self.near, self.far, self.level, self.bridge]
        long += [self.out_near, self.out_far, self.out_core, self.end]
        brief = [self.begin, self.near, self.far, self.level, self.out_direct, self.out_core, self.end]
        slow = long[:4] + [self.rest] + long[4:5] + [self.rest] + long[5:]
        self.order = [brief if k in self.short else slow if k < len(chunks) // 2 else long for k in range(len(chunks))]

    @staticmethod
    def scratch(chunks, widths, local):
        low, dma, total = jnp.bfloat16, pltpu.SemaphoreType.DMA, len(chunks)
        shapes = []
        for which, _, r in chunks:
            w = widths[which]
            shapes += [] if which in local else [(4, r // 2, w)]
            shapes += [(4, r // 2, w), (2, 4, r // 4, w // 2), (2, 4, r // 8, w // 2), (2, 3, r // 8, w // 2)]
            shapes += [(2, r // 8, w // 2)]
        sems = [dma((total,))] * 4 + [dma((total, 2))] * 8 + [dma((total, 2, 3))] * 2 + [dma((total,))] * 2 + [dma((total, 2))]
        sems += [dma((total, 2, 3))] * 2
        return [pltpu.VMEM(shape, low) for shape in shapes], sems

    def sizes(self, k):
        which, base, rows = self.chunks[k]
        return which, base, rows // 8, self.grads[which].shape[2] // 2

    @staticmethod
    def add(total, total_row, total_col, part, part_col, rows, cols):
        @pl.loop(0, rows // 16)
        def _(i):
            here = (pl.ds(pl.multiple_of(total_row + i * 16, 16), 16), pl.ds(total_col, cols))
            there = (pl.ds(pl.multiple_of(i * 16, 16), 16), pl.ds(part_col, cols))
            ours = [total[(shard,) + here].astype(jnp.float32) for shard in range(4)]
            theirs = [part[(shard,) + there].astype(jnp.float32) for shard in range(4)]
            sums = [(left + right).astype(jnp.bfloat16) for left, right in zip(ours, theirs)]
            for shard in range(4):
                total[(shard,) + here] = sums[shard]

    def places(self, r, w):
        return [((self.x * 2 + self.y) * r, 0), ((self.y * 2 + self.x) * r, w)]

    def rest(self, k):
        pass

    def begin(self, k):
        which, base, r, w = self.sizes(k)
        theirs = pl.multiple_of(base + (1 - self.c) * 4 * r, 16)
        ours = pl.multiple_of(base + self.c * 4 * r, 16)
        source = self.grads[which].at[:, pl.ds(theirs, 4 * r), :]
        self.sends.start("core", k, [(source, self.core_in[k], self.sems[0].at[k], self.sems[1].at[k], self.core)])
        if which not in self.local:
            source = self.grads[which].at[:, pl.ds(ours, 4 * r), :]
            self.fetched[k] = pltpu.make_async_copy(source, self.mine[k][0], self.sems[2].at[k])
            self.fetched[k].start()

    def near(self, k):
        which, base, r, w = self.sizes(k)
        mine, offset = self.mine[k]
        if k in self.fetched:
            self.fetched[k].wait()
        self.sends.arrived("core", k)
        items = []
        for h, (bit, peer) in enumerate([(self.x, self.across), (self.y, self.along)]):
            self.add(mine, offset, h * w, self.core_in[k], h * w, 4 * r, w)
            row = pl.multiple_of(offset + (1 - bit) * 2 * r, 16)
            source = mine.at[:, pl.ds(row, 2 * r), pl.ds(h * w, w)]
            items.append((source, self.near_in[k].at[h], self.sems[4].at[k, h], self.sems[5].at[k, h], peer))
        self.sends.start("near", k, items)

    def far(self, k):
        which, base, r, w = self.sizes(k)
        mine, offset = self.mine[k]
        self.sends.arrived("near", k)
        items = []
        for h, (bit, second, peer) in enumerate([(self.x, self.y, self.along), (self.y, self.x, self.across)]):
            row = offset + bit * 2 * r
            self.add(mine, row, h * w, self.near_in[k].at[h], 0, 2 * r, w)
            row = pl.multiple_of(row + (1 - second) * r, 16)
            source = mine.at[:, pl.ds(row, r), pl.ds(h * w, w)]
            items.append((source, self.far_in[k].at[h], self.sems[6].at[k, h], self.sems[7].at[k, h], peer))
        self.sends.start("far", k, items)


    def hop(self, k, h, j, source, target, recv, to):
        return pltpu.make_async_remote_copy(
            src_ref=source, dst_ref=target, send_sem=self.sems[12].at[k, h, j], recv_sem=recv,
            device_id=(self.index, to), device_id_type=MESH,
        )

    def slot(self, k, h, j):
        return self.plane_in[k].at[h, j], self.sems[13].at[k, h, j]

    def bridge_slot(self, k, h):
        return self.relay_in[k].at[h], self.sems[16].at[k, h]

    def level(self, k):
        which, base, r, w = self.sizes(k)
        mine, offset = self.mine[k]
        self.sends.arrived("far", k)
        for h, (row, col) in enumerate(self.places(r, w)):
            self.add(mine, offset + row, col, self.far_in[k].at[h], 0, r, w)

        def piece(h, plane):
            row, col = self.places(r, w)[h]
            return mine.at[plane, pl.ds(pl.multiple_of(offset + row, 16), r), pl.ds(col, w)]

        @pl.when(self.outer)
        def _():
            for h in range(2):
                other = 3 - self.plane
                if k in self.short:
                    self.hop(k, h, 2, piece(h, other), *self.slot(k, h, 2), other).start()
                else:
                    self.hop(k, h, 2, piece(h, other), *self.bridge_slot(k, h), self.next).start()
            for h in range(2):
                self.hop(k, h, 1, piece(h, self.beyond), *self.slot(k, h, 2), self.beyond).start()
                self.hop(k, h, 0, piece(h, self.next), *self.slot(k, h, 1), self.next).start()

        @pl.when(jnp.logical_not(self.outer))
        def _():
            for h in range(2):
                self.hop(k, h, 1, piece(h, 3 - self.plane), *self.slot(k, h, 0), 3 - self.plane).start()
                self.hop(k, h, 0, piece(h, self.edge), *self.slot(k, h, 0), self.edge).start()
                if k in self.short:
                    other = 3 - self.edge
                    self.hop(k, h, 2, piece(h, other), *self.slot(k, h, 1), other).start()

    def bridge(self, k):
        which, base, r, w = self.sizes(k)
        mine, offset = self.mine[k]
        relay = self.relay_in[k]

        @pl.when(jnp.logical_not(self.outer))
        def _():
            for h, (row, col) in enumerate(self.places(r, w)):
                self.hop(k, h, 2, relay.at[h], *self.bridge_slot(k, h), self.plane).wait_recv()

                @pl.loop(0, r // 16)
                def _(i):
                    step = pl.ds(pl.multiple_of(i * 16, 16), 16)
                    here = pl.ds(pl.multiple_of(offset + row + i * 16, 16), 16)
                    ours = mine[3 - self.edge, here, pl.ds(col, w)].astype(jnp.float32)
                    relay[h, step, :] = (ours + relay[h, step, :].astype(jnp.float32)).astype(jnp.bfloat16)

                self.hop(k, h, 2, relay.at[h], *self.slot(k, h, 1), 3 - self.edge).start()

    def add_planes(self, k, amount):
        which, base, r, w = self.sizes(k)
        mine, offset = self.mine[k]
        for h, (row, col) in enumerate(self.places(r, w)):
            for j in range(amount):
                place, sem = self.slot(k, h, j)
                self.hop(k, h, j, place, place, sem, self.plane).wait_recv()

            @pl.loop(0, r // 16)
            def _(i):
                step = pl.ds(pl.multiple_of(i * 16, 16), 16)
                here = pl.ds(pl.multiple_of(offset + row + i * 16, 16), 16)
                total = mine[self.plane, here, pl.ds(col, w)].astype(jnp.float32)
                for j in range(amount):
                    total = total + self.plane_in[k][h, j, step, :].astype(jnp.float32)
                here = pl.ds(pl.multiple_of(row + i * 16, 16), 16)
                self.core_in[k][0, here, pl.ds(col, w)] = total.astype(jnp.bfloat16)

    def pieces(self, k):
        which, base, r, w = self.sizes(k)
        return [
            self.core_in[k].at[0, pl.ds(pl.multiple_of(row, 16), r), pl.ds(col, w)] for row, col in self.places(r, w)
        ]

    def out_near(self, k):
        @pl.when(self.outer)
        def _():
            self.add_planes(k, 2)

        @pl.when(jnp.logical_not(self.outer))
        def _():
            self.add_planes(k, 3)

        items = []
        for h, piece in enumerate(self.pieces(k)):
            peer = (self.along, self.across)[h]
            items.append((piece, piece, self.sems[8].at[k, h], self.sems[9].at[k, h], peer))
        self.sends.start("out_near", k, items)

    def out_direct(self, k):
        self.add_planes(k, 3)
        items = []
        for h, piece in enumerate(self.pieces(k)):
            for j, peer in enumerate((self.diagonal, self.along, self.across)):
                items.append((piece, piece, self.sems[17].at[k, h, j], self.sems[18].at[k, h, j], peer))
        self.sends.start("out_far", k, items)

    def out_far(self, k):
        which, base, r, w = self.sizes(k)
        self.sends.arrived("out_near", k)
        items = []
        for h, (bit, peer) in enumerate([(self.x, self.across), (self.y, self.along)]):
            piece = self.core_in[k].at[0, pl.ds(pl.multiple_of(bit * 2 * r, 16), 2 * r), pl.ds(h * w, w)]
            items.append((piece, piece, self.sems[10].at[k, h], self.sems[11].at[k, h], peer))
        self.sends.start("out_far", k, items)

    def out_core(self, k):
        which, base, r, w = self.sizes(k)
        self.sends.arrived("out_far", k)
        target = self.sums[which].at[pl.ds(pl.multiple_of(base + self.c * 4 * r, 16), 4 * r), :]
        source = self.core_in[k].at[0]
        self.sends.start("out_core", k, [(source, target, self.sems[14].at[k], self.sems[15].at[k], self.core)])
        copy = pltpu.make_async_copy(source, target, self.sems[3].at[k])
        copy.start()
        self.final.append(copy)

    def end(self, k):
        self.sends.arrived("out_core", k)

    @property
    def steps(self):
        return max(k + len(stages) for k, stages in enumerate(self.order))

    def step(self, t):
        for k in reversed(range(len(self.chunks))):
            if 0 <= t - k < len(self.order[k]):
                self.order[k][t - k](k)

    def close(self):
        self.sends.close()
        for k in range(len(self.chunks)):
            for h in range(2):
                for j in range(3):
                    place, sem = self.slot(k, h, j)
                    self.hop(k, h, j, place, place, sem, self.plane).wait_send()
        for copy in self.final:
            copy.wait()


class ReduceTicks:
    def __init__(self, reduce, vector_sum, vector_in, send, recv):
        self.reduce, self.vector_sum, self.vector_in, self.send, self.recv = reduce, vector_sum, vector_in, send, recv
        self.now = 0

    def __call__(self):
        if self.now < self.reduce.steps:
            self.reduce.step(self.now)
        self.now += 1

    def sum_vectors(self):
        reduce, total, arrived = self.reduce, self.vector_sum, self.vector_in
        for t, peer in enumerate((reduce.core, reduce.across, reduce.along)):
            reduce.sends.start("vector", t, [(total.at[t], arrived.at[t], self.send.at[t], self.recv.at[t], peer)])
            self()
            reduce.sends.arrived("vector", t)
            total[t + 1] = total[t] + arrived[t]
        items = [
            (total.at[3], arrived.at[3 + j], self.send.at[3 + j], self.recv.at[3 + j], peer)
            for j, peer in enumerate(reduce.planes)
        ]
        reduce.sends.start("vector", 3, items)
        self()
        reduce.sends.arrived("vector", 3)
        ordered = [arrived[3 + j] for j in range(3)]
        plane, own = reduce.plane, total[3]
        slots = []
        for m in range(4):
            value = own
            for j in range(3):
                value = jnp.where(reduce.others[j] == m, ordered[j], value)
            slots.append(value)
        total[4] = (slots[0] + slots[1]) + (slots[2] + slots[3])


class Patches:
    def __init__(self, patch, windows, merged, buffers, sems, index, plane, images, shift):
        self.patch, self.windows, self.merged = patch, windows, merged
        self.relay, self.own, self.total = buffers
        self.sends, self.recvs, self.relay_recv, self.merged_recv, self.local, self.fetch = sems
        self.index, self.plane = index, plane
        self.outer = (plane == 0) | (plane == 3)
        self.first = plane < 2
        self.next = jnp.where(plane == 0, 1, 2)
        self.far = 3 - self.next
        self.edge = jnp.where(plane == 1, 0, 3)
        self.across = 3 - plane
        self.images, self.shift = images, shift
    def copy(self, slot, source, target, recv, to):
        return pltpu.make_async_remote_copy(
            src_ref=source, dst_ref=target, send_sem=self.sends.at[slot], recv_sem=recv, device_id=(self.index, to),
            device_id_type=MESH,
        )

    def direct(self, slot, to):
        return self.copy(slot, self.patch.at[to], self.windows.at[self.plane], self.recvs.at[self.plane], to)

    def to_relay(self):
        return self.copy(1, self.patch.at[self.across], self.relay, self.relay_recv.at[0], self.next)

    def to_edge(self):
        return self.copy(1, self.total, self.merged, self.merged_recv.at[0], 3 - self.edge)

    def keep(self):
        return pltpu.make_async_copy(self.patch.at[self.plane], self.windows.at[self.plane], self.local.at[0])

    def take(self):
        return pltpu.make_async_copy(self.patch.at[3 - self.edge], self.own, self.fetch.at[0])

    def begin(self):
        self.keep().start()

        @pl.when(self.outer)
        def _():
            self.to_relay().start()
            self.direct(0, self.far).start()

        @pl.when(jnp.logical_not(self.outer))
        def _():
            self.take().start()
            self.direct(0, self.across).start()

    def middle(self):
        @pl.when(self.outer)
        def _():
            self.direct(2, self.next).start()

        @pl.when(jnp.logical_not(self.outer))
        def _():
            self.direct(2, self.edge).start()
            self.take().wait()
            self.to_relay().wait_recv()

            @pl.when(self.first)
            def _():
                self.add(self.relay, self.own)

            @pl.when(jnp.logical_not(self.first))
            def _():
                self.add(self.own, self.relay)

            self.to_edge().start()

    def add(self, early, late):
        images, shift, total = self.images, self.shift, self.total
        size = (early.shape[0] - 16) // images
        for i in range(images + shift):
            here = pl.ds(i * size, size)
            there = pl.ds((i - shift) * size, size)
            if i < shift:
                total[here, :] = early[here, :]
            elif i < images:
                both = early[here, :].astype(jnp.float32) + late[there, :].astype(jnp.float32)
                total[here, :] = both.astype(jnp.bfloat16)
            else:
                total[here, :] = late[there, :]
        row = lax.broadcasted_iota(jnp.int32, (16, 16), 0)
        column = lax.broadcasted_iota(jnp.int32, (16, 16), 1)
        down = (row == column + shift).astype(jnp.bfloat16)
        last = pl.ds(images * size, 16)
        both = early[last, :].astype(jnp.float32) + nn(down, late[last, :])
        total[pl.ds((images + shift) * size, 16), :] = both.astype(jnp.bfloat16)

    def end(self):
        self.keep().wait()

        @pl.when(self.outer)
        def _():
            self.copy(0, self.patch.at[0], self.windows.at[self.next], self.recvs.at[self.next], self.next).wait_recv()
            self.copy(1, self.total, self.merged, self.merged_recv.at[0], self.far).wait_recv()
            self.to_relay().wait_send()
            self.direct(0, self.far).wait_send()
            self.direct(2, self.next).wait_send()

        @pl.when(jnp.logical_not(self.outer))
        def _():
            for source in (self.across, 0, 3):
                self.copy(0, self.patch.at[0], self.windows.at[source], self.recvs.at[source], self.across).wait_recv()
            self.direct(0, self.across).wait_send()
            self.to_edge().wait_send()
            self.direct(2, self.edge).wait_send()


def back_kernel(chunks, count, slots, window, shift, *refs):
    grads, patch, early, refs = refs[:count], refs[count], refs[count + 1 : count + 3], refs[count + 3 :]
    inputs, refs = refs[:slots], refs[slots:]
    sums, refs = refs[: count + 1], refs[count + 1 :]
    (windows, merged, vector_sum, text_far), refs = refs[:4], refs[4:]
    inputs = [Slot(inputs[i], refs[2 * i], refs[2 * i + 1]) for i in range(slots)]
    refs = refs[2 * slots :]
    self_grad, text_sem, refs = refs[0], refs[1], refs[2:]
    scratch, refs = refs[:5], refs[5:]
    (vector_in, vector_send, vector_recv), patch_refs, refs = refs[:3], refs[3:12], refs[12:]
    sems, buffers = refs[:19], refs[19:]
    for slot in inputs:
        slot.fetch()
    reduce = Reduce(chunks, [self_grad, *grads], sums, buffers, sems, {0: self_grad})
    greet([reduce.core, reduce.across, reduce.along, reduce.diagonal] + reduce.planes)
    ticks = ReduceTicks(reduce, vector_sum, vector_in, vector_send, vector_recv)
    ticks()
    patches = Patches(
        patch, windows, merged, patch_refs[:3], patch_refs[3:], reduce.index, reduce.plane, window, shift
    )
    patches.begin()
    vector_sum[0] = early[0][...] + early[1][...]
    text_grad = inputs[0].near
    self_back_steps(ticks, inputs, self_grad, vector_sum.at[0], text_grad, scratch)
    text_copy = pltpu.make_async_copy(text_grad, text_far, text_sem.at[0])
    text_copy.start()
    patches.middle()
    ticks()
    ticks.sum_vectors()
    while ticks.now < reduce.steps:
        ticks()
    patches.end()
    reduce.close()
    text_copy.wait()


def reduce_back(grads, patch, early, inputs, window, shift, chunks):
    count, dma, f32, bf16 = len(grads), pltpu.SemaphoreType.DMA, jnp.float32, jnp.bfloat16
    any_space, vmem = pl.BlockSpec(memory_space=pl.ANY), pl.BlockSpec(memory_space=pltpu.VMEM)
    weights, flat = inputs[4].shape, inputs[0].shape
    together = (patch.shape[1] + shift * ((patch.shape[1] - 16) // window), patch.shape[2])
    widths = [weights[2]] + [grad.shape[2] for grad in grads]
    buffers, sems = Reduce.scratch(chunks, widths, {0})
    *sums, windows, merged, vector_sum, text_grad = pl.pallas_call(
        functools.partial(back_kernel, chunks, count, len(inputs), window, shift),
        out_shape=[jax.ShapeDtypeStruct(shape[1:], bf16) for shape in [weights] + [grad.shape for grad in grads]]
        + [jax.ShapeDtypeStruct(patch.shape, bf16), jax.ShapeDtypeStruct(together, bf16)]
        + [jax.ShapeDtypeStruct((5,) + early[0].shape, f32)]
        + [jax.ShapeDtypeStruct(flat, f32)],
        in_specs=[any_space] * (count + 1) + [vmem] * 2 + [any_space] * len(inputs),
        out_specs=[any_space] * (count + 3) + [vmem, any_space],
        scratch_shapes=[entry for array in inputs for entry in slot_scratch(array.shape, array.dtype)]
        + [pltpu.VMEM(weights, bf16), dma((1,))]
        + [pltpu.VMEM(flat, bf16)] * 5
        + [pltpu.VMEM((6,) + early[0].shape, f32), dma((6,)), dma((6,))]
        + [pltpu.VMEM(patch.shape[1:], bf16), pltpu.VMEM(patch.shape[1:], bf16), pltpu.VMEM(together, bf16)]
        + [dma((3,)), dma((4,)), dma((1,)), dma((1,)), dma((1,)), dma((1,))]
        + sems
        + buffers,
        compiler_params=pltpu.CompilerParams(collective_id=1, has_side_effects=True, vmem_limit_bytes=63 << 20),
        name="reduce_back",
    )(*grads, patch, *early, *inputs)
    return sums, windows, merged, vector_sum, text_grad


class Slot:
    def __init__(self, far, near, sem, parts=0):
        self.far, self.near, self.sem, self.parts, self.waited = far, near, sem, parts, False

    def copy(self, out, m=None):
        far, near = (self.far, self.near) if m is None else (self.far.at[m], self.near.at[m])
        sem = self.sem.at[0 if m is None else m]
        return pltpu.make_async_copy(near, far, sem) if out else pltpu.make_async_copy(far, near, sem)

    def fetch(self):
        for m in range(self.parts) if self.parts else (None,):
            self.copy(False, m).start()

    def ready(self):
        if not self.waited:
            self.waited = True
            for m in range(self.parts) if self.parts else (None,):
                self.copy(False, m).wait()
        return self.near

    def flush(self, m=None):
        self.copy(True, m).start()

    def finish(self):
        for m in range(self.parts) if self.parts else (None,):
            self.copy(True, m).wait()


def slot_scratch(shape, kind, parts=0):
    return [pltpu.VMEM(shape, kind), pltpu.SemaphoreType.DMA((max(parts, 1),))]


def on_slots(kernel, name, scalars, inputs, outputs, scratch, parts_in=(), parts_out=(), counted=0, ordered=False):
    count, total, given = len(inputs), len(inputs) + len(outputs), len(scalars)

    def body(*refs):
        scalar_refs, refs = refs[:given], refs[given:]
        far_in, refs = refs[:count], refs[count:]
        if counted:
            scalar_refs, refs = scalar_refs + refs[:1], refs[1:]
        far, refs = far_in + refs[: total - count], refs[total - count :]
        slots = []
        for i in range(total):
            parts = far[i].shape[0] if (i in parts_in if i < count else i - count in parts_out) else 0
            slots.append(Slot(far[i], refs[2 * i], refs[2 * i + 1], parts))
        if not ordered:
            for slot in slots[:count]:
                slot.fetch()
        kernel(scalar_refs, slots[:count], slots[count:], refs[2 * total :])
        for slot in slots[count:]:
            slot.finish()

    spaces = []
    for i, array in enumerate(inputs):
        spaces += slot_scratch(array.shape, array.dtype, array.shape[0] if i in parts_in else 0)
    for i, (shape, kind) in enumerate(outputs):
        spaces += slot_scratch(shape, kind, shape[0] if i in parts_out else 0)
    any_space, smem = pl.BlockSpec(memory_space=pl.ANY), pl.BlockSpec(memory_space=pltpu.SMEM)
    first = [jax.ShapeDtypeStruct((counted,), jnp.int32)] if counted else []
    return pl.pallas_call(
        body,
        out_shape=first + [jax.ShapeDtypeStruct(shape, kind) for shape, kind in outputs],
        in_specs=[smem] * given + [any_space] * count,
        out_specs=[smem] * len(first) + [any_space] * len(outputs),
        scratch_shapes=spaces + [entry if hasattr(entry, "memory_space") else pltpu.VMEM(*entry) for entry in scratch],
        compiler_params=pltpu.CompilerParams(vmem_limit_bytes=63 << 20),
        name=name,
    )(*scalars, *inputs)


def nn(left, right):
    return lax.dot_general(left, right, (((1,), (0,)), ((), ())), preferred_element_type=jnp.float32)


def nt(left, right):
    return lax.dot_general(left, right, (((1,), (1,)), ((), ())), preferred_element_type=jnp.float32)


def tn(left, right):
    return lax.dot_general(left, right, (((0,), (0,)), ((), ())), preferred_element_type=jnp.float32)


def part(ref, which):
    inner = ref.shape[2] // 4 if ref.shape[2] == 768 else 192
    return jnp.concatenate([ref[m, which * 192 : (which + 1) * 192, :] for m in range(4)], axis=0)


def store_part(ref, which, value):
    low = value.astype(jnp.bfloat16)
    for m in range(4):
        ref[m, which * 192 : (which + 1) * 192, :] = low[m * 192 : (m + 1) * 192]


def tiles(amount, step):
    def wrap(body):
        @pl.loop(0, amount // step)
        def _(i):
            body(pl.ds(pl.multiple_of(i * step, step), step))

    return wrap


def lanes():
    place = lax.broadcasted_iota(jnp.int32, (1, 2 * HEAD_DIM), 1)
    low = place < HEAD_DIM
    return low, low.astype(jnp.float32), 1.0 - low.astype(jnp.float32)


def norm_forward(total, unit, inverse, value, value_low, gain, shift):
    @tiles(total.shape[0], 80)
    def _(rows):
        hidden = total[rows, :]
        center = hidden - jnp.mean(hidden, axis=-1, keepdims=True)
        factor = lax.rsqrt(jnp.mean(center * center, axis=-1, keepdims=True) + 1e-06)
        scaled = center * factor
        result = scaled * gain[...] + shift[...]
        if unit is not None:
            unit[rows, :] = scaled
            inverse[rows, :] = jnp.broadcast_to(factor, (80, 128))
        if value is not None:
            value[rows, :] = result
        value_low[rows, :] = result.astype(jnp.bfloat16)


def norm_reverse(upstream, unit, inverse, gain, gain_grad, shift_grad, grad, grad_low):
    gain_grad[...] = jnp.zeros_like(gain_grad)
    shift_grad[...] = jnp.zeros_like(shift_grad)

    @tiles(upstream.shape[0], 80)
    def _(rows):
        up = upstream[rows, :].astype(jnp.float32)
        scaled = unit[rows, :]
        factor = inverse[rows, :][:, :1]
        gain_grad[...] += jnp.sum(up * scaled, axis=0, keepdims=True)
        shift_grad[...] += jnp.sum(up, axis=0, keepdims=True)
        inner = up * gain[...]
        result = factor * (
            inner
            - jnp.mean(inner, axis=-1, keepdims=True)
            - scaled * jnp.mean(inner * scaled, axis=-1, keepdims=True)
        )
        grad[rows, :] = result
        grad_low[rows, :] = result.astype(jnp.bfloat16)


def softmax(scores):
    raised = jnp.exp(scores - jnp.max(scores, axis=-1, keepdims=True))
    return (raised * (1.0 / jnp.sum(raised, axis=-1, keepdims=True))).astype(jnp.bfloat16)


def columns(width):
    return [slice(start, start + 128) for start in range(0, width, 128)]


def stack(value, first, second):
    return jnp.concatenate([value * first, value * second], axis=0)


def merge(low, value):
    half = value.shape[0] // 2
    return jnp.where(low, value[:half], value[half:])


def attend_self(queries, keys, values, lengths, probs, context):
    low, first, second = lanes()
    first, second = first.astype(jnp.bfloat16), second.astype(jnp.bfloat16)
    cols = columns(queries.shape[1])
    query = lax.broadcasted_iota(jnp.int32, (160, 80), 0)
    key = lax.broadcasted_iota(jnp.int32, (160, 80), 1)
    query = jnp.where(query >= 80, query - 80, query)
    same = (query < 40) == (key < 40)

    @pl.loop(0, queries.shape[0] // 80)
    def _(pair):
        rows = pl.ds(pl.multiple_of(pair * 80, 80), 80)
        allowed = same & (key < jnp.where(key < 40, lengths(2 * pair), lengths(2 * pair + 1) + 40))
        stacked = [stack(queries[rows, c], first, second) for c in cols]
        scores = [nt(both, keys[rows, c]) * HEAD_DIM ** (-0.5) for both, c in zip(stacked, cols)]
        weights = [softmax(jnp.where(allowed, score, -1000000000.0)) for score in scores]
        mixed = [merge(low, nn(weight, values[rows, c])) for weight, c in zip(weights, cols)]
        for tile, c in enumerate(cols):
            probs[pair, tile] = weights[tile]
            context[rows, c] = mixed[tile].astype(jnp.bfloat16)


def attend_cross(image, caption, wide, keys, values, cell_ok, probs, begin, end):
    low, first, second = lanes()
    cols = columns(wide.shape[1])

    @pl.loop(begin, end)
    def _(row):
        rows = pl.ds(pl.multiple_of(row * 40, 40), 40)
        which = image[row]
        cells = cell_ok[pl.ds(row, 1), :] + caption[row].astype(jnp.float32)
        allowed = jnp.broadcast_to(cells, (80, cell_ok.shape[1])) > 0
        stacked = [stack(wide[rows, c], first, second).astype(jnp.bfloat16) for c in cols]
        scores = [nt(both, keys[which, :, c]) * HEAD_DIM ** (-0.5) for both, c in zip(stacked, cols)]
        weights = [softmax(jnp.where(allowed, score, -1000000000.0)) for score in scores]
        mixed = [merge(low, nn(weight, values[which, :, c])) for weight, c in zip(weights, cols)]
        for tile, c in enumerate(cols):
            probs[row, tile] = weights[tile]
            wide[rows, c] = mixed[tile]


def prepare(counts, lengths, boxes, vectors, cells_all, image, caption, cell_ok, norms, near, plane):
    rows, padded = cell_ok.shape
    cells, images, _ = cells_all.shape
    window = near.shape[0]
    start = jnp.minimum(plane * rows // ROWS_MAX, images - window)

    @pl.loop(0, rows)
    def _(r):
        row = plane * rows + r
        end, here, before = jnp.int32(0), jnp.int32(0), jnp.int32(0)
        for i in range(images):
            end = end + counts[0, i]
            here = here + (end <= row).astype(jnp.int32)
            before = before + (end <= row - 1).astype(jnp.int32)
        image[r] = jnp.minimum(jnp.maximum(here - start, 0), window - 1)
        caption[r] = jnp.where(row == 0, jnp.int32(1), here - before)

    cell_ok[...] = jnp.full(cell_ok.shape, -2.0, jnp.float32)
    cell_ok[:, :cells] = (boxes[pl.ds(pl.multiple_of(plane * rows, 8), rows), :] > 0).astype(jnp.float32)
    norms[...] = jnp.zeros_like(norms)
    for i, vector in enumerate(vectors):
        norms[pl.ds(i, 1), :] = vector[...].reshape(1, norms.shape[1])
    step = 16
    for first in range(0, padded, step):
        amount = min(step, cells - first)
        to = lax.broadcasted_iota(jnp.int32, (window * step, amount * images), 0)
        source = lax.broadcasted_iota(jnp.int32, (window * step, amount * images), 1)
        pick = (source // images == to % step) & (source % images == to // step + start)
        block = cells_all[first : first + amount].reshape(amount * images, cells_all.shape[2])
        block = nn(pick.astype(jnp.bfloat16), block).astype(jnp.bfloat16)
        near[:, first : first + step, :] = block.reshape(window, step, cells_all.shape[2])


def forward_steps(ticks, image, caption, lengths, tokens, near, cell_ok, weights, norms, saved, wide):
    bf16 = jnp.bfloat16
    self_weights, cross_weights, keyval = weights
    (
        queries, keys, values, self_probs, self_context, first_unit, first_inverse, first_low, cross_queries, image_keys,
        image_values, cross_probs, cross_context, second_unit, second_inverse, second_value, second_low,
    ) = (slot.near for slot in saved)

    def flush(*places):
        for place in places:
            saved[place].flush()

    gains = [norms.at[pl.ds(i, 1), :] for i in range(4)]
    ticks.wait(0)
    for target, which in ((queries, 0), (keys, 1), (values, 2)):
        target[...] = nt(tokens[...], part(self_weights, which)).astype(bf16)
    flush(0, 1, 2)
    ticks()
    attend_self(queries, keys, values, lengths, self_probs, self_context)
    flush(3, 4)
    ticks()
    second_value[...] = nn(self_context[...], part(self_weights, 3)) + tokens[...].astype(jnp.float32)
    norm_forward(second_value, first_unit, first_inverse, None, first_low, gains[0], gains[1])
    flush(5, 6, 7)
    ticks.wait(1)
    cross_queries[...] = nt(first_low[...], part(cross_weights, 0)).astype(bf16)
    flush(8)
    wide[...] = cross_queries[...].astype(jnp.float32)
    images, cells, depth = near.shape
    half = images // 2
    ticks.wait(2)
    for target, which in ((image_keys, 0), (image_values, 1)):
        weight = part(keyval, which)
        for step in range(2):
            block = near[step * half : (step + 1) * half].reshape(half * cells, depth)
            target[step * half : (step + 1) * half] = nt(block, weight).astype(bf16).reshape(half, cells, -1)
        flush(9 + which)
    ticks()
    rows = cell_ok.shape[0]
    for part_of in range(2):
        begin, end = part_of * rows // 2, (part_of + 1) * rows // 2
        attend_cross(image, caption, wide, image_keys, image_values, cell_ok, cross_probs, begin, end)
        ticks()
    flush(11)
    cross_context[...] = wide[...].astype(bf16)
    flush(12)
    second_value[...] = nn(cross_context[...], part(cross_weights, 1)) + (first_unit[...] * gains[0][...] + gains[1][...])
    norm_forward(second_value, second_unit, second_inverse, second_value, second_low, gains[2], gains[3])
    flush(13, 14, 15, 16)


def feed_kernel(scalars, inputs, outputs, scratch):
    second_value, second_low, norms, expand, shrink, cotangent = inputs
    joined, expand_grad, shrink_grad, vectors, second_up = outputs
    active, slope, unit, inverse, feed_low = scratch
    bf16 = jnp.bfloat16
    for slot in (second_low, norms):
        slot.fetch()
    expand.copy(False, 0).start()
    second_value.fetch()
    shrink.copy(False, 0).start()
    total = second_up.near
    second_low, norms = second_low.ready(), norms.ready()
    total[...] = second_value.ready()[...]
    for m in range(1, expand.near.shape[0]):
        expand.copy(False, m).start()
        shrink.copy(False, m).start()
    cotangent.fetch()
    gain, shift = norms.at[0, pl.ds(4, 1), :], norms.at[0, pl.ds(5, 1), :]
    hidden, amount = expand.near.shape[0], total.shape[0]
    halves = [slice(0, amount // 2), slice(amount // 2, amount)]

    @pl.loop(0, hidden)
    def _(m):
        expand.copy(False, m).wait()
        shrink.copy(False, m).wait()
        inners = [nn(second_low[rows, :], expand.near[m]) + norms[m, pl.ds(6, 1), :] for rows in halves]
        shares = [0.5 * (1.0 + lax.erf(inner * 0.5**0.5)) for inner in inners]
        acts = [(inner * share).astype(bf16) for inner, share in zip(inners, shares)]
        slopes = [
            (share + inner * (jnp.exp(-0.5 * inner * inner) * 0.3989422804014327)).astype(bf16)
            for inner, share in zip(inners, shares)
        ]
        for rows, act, inclination in zip(halves, acts, slopes):
            active[m, rows, :] = act
            slope[m, rows, :] = inclination
            total[rows, :] += nn(act, shrink.near[m])

    norm_forward(total, unit, inverse, None, joined.near, gain, shift)
    joined.flush()
    sums = vectors.near
    sums[...] = jnp.zeros_like(sums)
    norm_reverse(
        cotangent.ready(), unit, inverse, gain, sums.at[pl.ds(8, 1), :], sums.at[pl.ds(9, 1), :], total, feed_low
    )

    @pl.loop(0, hidden)
    def _(m):
        shrink_grad.near[m] = tn(active[m], feed_low[...]).astype(bf16)
        shrink_grad.flush(m)
        lows = [
            (nt(feed_low[rows, :], shrink.near[m]) * slope[m, rows, :].astype(jnp.float32)).astype(bf16) for rows in halves
        ]
        parts = [jnp.sum(low.astype(jnp.float32), axis=0, keepdims=True) for low in lows]
        sums[pl.ds(m, 1), :] = parts[0] + parts[1]
        for rows, low in zip(halves, lows):
            active[m, rows, :] = low
        expand_grad.near[m] = tn(second_low[...], active[m]).astype(bf16)
        expand_grad.flush(m)
        total[...] += nt(active[m], expand.near[m])

    vectors.flush()
    second_up.flush()


def score_back(weights, upstream):
    probs = weights.astype(jnp.float32)
    return (probs * (upstream - jnp.sum(probs * upstream, axis=-1, keepdims=True))).astype(jnp.bfloat16)


def cross_back_kernel(scalars, inputs, outputs, scratch):
    (image,) = scalars
    (
        second_up, second_unit, second_inverse, norms, cross_weights, cross_context, cross_queries, image_values,
        image_keys, cross_probs, first_low, keyval, near,
    ) = inputs
    weights_grad, keyval_grad, patch, vectors, first_up = outputs
    grad_low, wide, turn, key_sum, value_sum, query_low = scratch
    bf16 = jnp.bfloat16
    low, first, second = lanes()
    for slot in inputs[:4]:
        slot.fetch()
    for slot in inputs[:4]:
        slot.ready()
    for slot in inputs[4:]:
        slot.fetch()
    sums = vectors.near
    sums[...] = jnp.zeros_like(sums)
    norm_reverse(
        second_up.near, second_unit.near, second_inverse.near, norms.near.at[0, pl.ds(2, 1), :],
        sums.at[pl.ds(6, 1), :], sums.at[pl.ds(7, 1), :], first_up.near, grad_low,
    )
    vectors.flush()
    cross_weights = cross_weights.ready()
    wide[...] = nt(grad_low[...], part(cross_weights, 1)).astype(bf16).astype(jnp.float32)
    store_part(weights_grad.near, 1, tn(cross_context.ready()[...], grad_low[...]))
    turn[...] = cross_queries.ready()[...].astype(jnp.float32)
    key_sum[...] = jnp.zeros_like(key_sum)
    value_sum[...] = jnp.zeros_like(value_sum)
    cols = columns(wide.shape[1])
    image_values, image_keys, cross_probs = image_values.ready(), image_keys.ready(), cross_probs.ready()

    @pl.loop(0, cross_probs.shape[0])
    def _(row):
        rows = pl.ds(pl.multiple_of(row * 40, 40), 40)
        which = image[row]
        queries = [stack(turn[rows, c], first, second).astype(bf16) for c in cols]
        grads = [stack(wide[rows, c], first, second).astype(bf16) for c in cols]
        weights = [cross_probs[row, tile] for tile in range(len(cols))]
        upstream = [nt(grad, image_values[which, :, c]) for grad, c in zip(grads, cols)]
        back = [score_back(weight, up) for weight, up in zip(weights, upstream)]
        mixed = [merge(low, nn(grad, image_keys[which, :, c])) * HEAD_DIM ** (-0.5) for grad, c in zip(back, cols)]
        key_parts = [tn(grad, both) * HEAD_DIM ** (-0.5) for grad, both in zip(back, queries)]
        value_parts = [tn(weight, grad) for weight, grad in zip(weights, grads)]
        for tile, c in enumerate(cols):
            turn[rows, c] = mixed[tile]
        for tile, c in enumerate(cols):
            key_sum[which, :, c] += key_parts[tile]
        for tile, c in enumerate(cols):
            value_sum[which, :, c] += value_parts[tile]

    keyval, near = keyval.ready(), near.ready()
    images, cells, depth = near.shape
    amount = images * cells
    quarter, size, half = patch.near.shape[2], (patch.near.shape[1] - 16) // images, images // 2
    last = jnp.zeros((16, depth), jnp.float32)
    for step in range(2):
        here = slice(step * half, (step + 1) * half)
        block = nn(key_sum[here].astype(bf16).reshape(amount // 2, -1), part(keyval, 0))
        block += nn(value_sum[here].astype(bf16).reshape(amount // 2, -1), part(keyval, 1))
        block = block.astype(bf16)
        row = lax.broadcasted_iota(jnp.int32, (16, amount // 2), 0)
        source = lax.broadcasted_iota(jnp.int32, (16, amount // 2), 1)
        last += nn((source == (row - step * half) * cells + size).astype(bf16), block)
        for m in range(patch.near.shape[0]):
            for i in range(half):
                rows = pl.ds((step * half + i) * size, size)
                patch.near[m, rows, :] = block[i * cells : i * cells + size, m * quarter : (m + 1) * quarter]
    for m in range(patch.near.shape[0]):
        patch.near[m, pl.ds(images * size, 16), :] = last[:, m * quarter : (m + 1) * quarter].astype(bf16)
    patch.flush()
    for source, which in ((key_sum, 0), (value_sum, 1)):
        flat = source[...].astype(bf16).reshape(amount, -1)
        store_part(keyval_grad.near, which, tn(flat, near[...].reshape(amount, depth)))
    keyval_grad.flush()
    query_low[...] = turn[...].astype(bf16)
    first_up.near[...] += nn(query_low[...], part(cross_weights, 0))
    first_up.flush()
    store_part(weights_grad.near, 0, tn(query_low[...], first_low.ready()[...]))
    weights_grad.flush()


def self_back_steps(ticks, inputs, weights_grad, sums, text_grad, scratch):
    (
        first_up, first_unit, first_inverse, norms, self_weights, self_context, queries, keys, values, self_probs, tokens,
    ) = inputs
    grad_low, context_low, query_low, key_low, value_low = scratch
    bf16 = jnp.bfloat16
    low, first, second = lanes()
    first_mask, second_mask = first.astype(bf16), second.astype(bf16)
    norm_reverse(
        first_up.ready(), first_unit.ready(), first_inverse.ready(), norms.ready().at[0, pl.ds(0, 1), :],
        sums.at[pl.ds(4, 1), :], sums.at[pl.ds(5, 1), :], text_grad, grad_low,
    )
    self_weights = self_weights.ready()
    context_low[...] = nt(grad_low[...], part(self_weights, 3)).astype(bf16)
    store_part(weights_grad, 3, tn(self_context.ready()[...], grad_low[...]))
    cols = columns(context_low.shape[1])
    queries, keys, values, self_probs = queries.ready(), keys.ready(), values.ready(), self_probs.ready()
    ticks()

    @pl.loop(0, self_probs.shape[0])
    def _(pair):
        rows = pl.ds(pl.multiple_of(pair * 80, 80), 80)
        stacked = [stack(queries[rows, c], first_mask, second_mask) for c in cols]
        grads = [stack(context_low[rows, c], first_mask, second_mask) for c in cols]
        weights = [self_probs[pair, tile] for tile in range(len(cols))]
        upstream = [nt(grad, values[rows, c]) for grad, c in zip(grads, cols)]
        back = [score_back(weight, up) for weight, up in zip(weights, upstream)]
        query_parts = [merge(low, nn(grad, keys[rows, c])) * HEAD_DIM ** (-0.5) for grad, c in zip(back, cols)]
        key_parts = [tn(grad, both) * HEAD_DIM ** (-0.5) for grad, both in zip(back, stacked)]
        value_parts = [tn(weight, grad) for weight, grad in zip(weights, grads)]
        for tile, c in enumerate(cols):
            query_low[rows, c] = query_parts[tile].astype(bf16)
            key_low[rows, c] = key_parts[tile].astype(bf16)
            value_low[rows, c] = value_parts[tile].astype(bf16)

    ticks()
    tokens = tokens.ready()
    for source, which in ((query_low, 0), (key_low, 1), (value_low, 2)):
        store_part(weights_grad, which, tn(source[...], tokens[...]))
        text_grad[...] += nn(source[...], part(self_weights, which))


def lone_self_back_kernel(scalars, inputs, outputs, scratch):
    weights_grad, vectors, text_grad = outputs
    vectors.near[...] = jnp.zeros_like(vectors.near)
    self_back_steps(Alone(), inputs, weights_grad.near, vectors.near, text_grad.near, scratch)
    for slot in outputs:
        slot.flush()


def finish_kernel(alone, scalars, inputs, outputs, scratch):
    self_sum, cross_sum, keyval_sum, expand_sum, shrink_sum, vectors, windows, merged, text = inputs
    text_grad, project, self_out, query, cross_out, keyval, expand, shrink, patch_grad, *norms, bias = outputs
    inner = self_out.near.shape[0]

    def give(output, value):
        output.near[...] = value.astype(jnp.float32)
        output.flush()

    give(text_grad, text.ready()[...])
    give(shrink, shrink_sum.ready()[...])
    give(expand, expand_sum.ready()[...])
    give(project, self_sum.ready()[: 3 * inner, :])
    give(self_out, self_sum.near[3 * inner :, :])
    give(query, cross_sum.ready()[:inner, :])
    give(cross_out, cross_sum.near[inner:, :])
    give(keyval, keyval_sum.ready()[...])
    sums = vectors.ready().at[vectors.near.shape[0] - 1]
    for i, output in enumerate(norms):
        give(output, sums[4 + i : 5 + i, :].reshape(sums.shape[1]))
    plane = lax.axis_index("mp")
    give(bias, sums[pl.ds(plane, 1), :].reshape(sums.shape[1]))
    windows, merged = windows.ready(), merged.ready()
    cells, images, quarter = patch_grad.near.shape
    size, step, rows = cells - 1, 16, scalars[0].shape[0]
    amount = (windows.shape[1] - step) // size

    def first_image(m):
        return jnp.minimum(m * rows // ROWS_MAX, images - amount)

    def place(sources):
        for first in range(0, size, step):
            total = jnp.zeros((step * images, quarter), jnp.float32)
            for window, start in sources:
                count = (window.shape[0] - step) // size
                to = lax.broadcasted_iota(jnp.int32, (step * images, count * step), 0)
                source = lax.broadcasted_iota(jnp.int32, (step * images, count * step), 1)
                pick = (to // images == source % step) & (to % images == source // step + start)
                block = [window[pl.ds(i * size + first, step), :] for i in range(count)]
                total = total + nn(pick.astype(jnp.bfloat16), jnp.concatenate(block, axis=0))
            patch_grad.near[first : first + step] = total.reshape(step, images, quarter)
        total = jnp.zeros((images, quarter), jnp.float32)
        for window, start in sources:
            count = (window.shape[0] - step) // size
            to = lax.broadcasted_iota(jnp.int32, (images, step), 0)
            source = lax.broadcasted_iota(jnp.int32, (images, step), 1)
            pick = (to == source + start) & (source < count)
            total = total + nn(pick.astype(jnp.bfloat16), window[pl.ds(count * size, step), :])
        patch_grad.near[size] = total

    if alone:
        place([(windows.at[m], first_image(m)) for m in range(4)])
    else:
        outer = (plane == 0) | (plane == 3)

        @pl.when(outer)
        def _():
            beside = jnp.where(plane == 0, 1, 2)
            place(
                [(windows.at[m], first_image(m)) for m in (plane, beside)]
                + [(merged, jnp.where(plane == 0, first_image(2), first_image(0)))]
            )

        @pl.when(jnp.logical_not(outer))
        def _():
            place([(windows.at[m], first_image(m)) for m in range(4)])

    patch_grad.flush()


def image_windows(parts, rows, group_images):
    group_rows = parts * rows
    first = [m * rows // ROWS_MAX for m in range(parts)]
    last = [group_images - 1 - max(0, -(-(group_rows - (m + 1) * rows - (ROWS_MAX - 1)) // ROWS_MAX)) for m in range(parts)]
    last = [min(stop, (m + 1) * rows - 1) for m, stop in enumerate(last)]
    window = max(stop - start + 1 for start, stop in zip(first, last))
    return [min(start, group_images - window) for start in first], window


def forward(scalars, inputs, cells_all, shards, outputs, near, chunks, own):
    if own:
        return gather_forward(scalars, inputs, cells_all, shards, outputs, near, chunks)
    weights = [lax.all_gather(jnp.concatenate(pieces, axis=0), "mp", axis=0) for pieces in shards]
    vectors = jnp.stack(inputs[2:] + [jnp.zeros_like(inputs[2])])
    biases = lax.all_gather(vectors, "mp", axis=0)
    amount, width = inputs[0].shape
    rows = amount // 40
    image, *saved = on_slots(
        lone_forward_kernel, "forward", scalars, inputs + [cells_all] + weights[:3], outputs + [near],
        [((amount, width), jnp.float32), ((rows, near[0][1]), jnp.float32), ((8, width), jnp.float32)]
        + [pltpu.SMEM((rows,), jnp.int32)],
        counted=rows,
    )
    return image, weights, biases, saved[:-1], saved[-1]


def reduce_shards(grads, patch, early, inputs, window, shift, chunks, own):
    if own:
        return reduce_back(grads, patch, early, inputs, window, shift, chunks)
    flat, weights = inputs[0].shape, inputs[4].shape
    self_grad, late, text_grad = on_slots(
        lone_self_back_kernel, "self_back", [], inputs,
        [(weights, jnp.bfloat16), (early[0].shape, jnp.float32), (flat, jnp.float32)], [(flat, jnp.bfloat16)] * 5,
    )
    sums = [
        lax.psum(lax.psum_scatter(grad.astype(jnp.float32), "mp", scatter_dimension=0, tiled=True)[0], "dp").astype(grad.dtype)
        for grad in [self_grad] + grads
    ]
    windows = lax.all_to_all(patch, "mp", split_axis=0, concat_axis=0, tiled=True)
    return sums, windows, windows[0], lax.psum(early[0] + early[1] + late, ("dp", "mp"))[None], text_grad


def per_device(
    tokens, patches, image_rows, row_lengths, box_mask, self_project, self_output, first_gain, first_shift, cross_query,
    cross_keyval, cross_output, second_gain, second_shift, expand_weight, expand_bias, shrink_weight, third_gain,
    third_shift, cotangent, *, parts, own,
):
    bf16, f32 = jnp.bfloat16, jnp.float32
    rows, slots, width = tokens.shape
    group_images, cells, depth = patches.shape
    starts, window = image_windows(parts, rows, group_images)
    padded = -(-cells // 16) * 16
    amount, pairs, tiles_of = rows * slots, rows // 2, width // 128
    inner = self_output.shape[0]
    shards = [
        [self_project.transpose(0, 2, 1).reshape(3 * inner, width), self_output],
        [cross_query.T, cross_output],
        [cross_keyval.transpose(0, 2, 1).reshape(2 * inner, depth)],
        [expand_weight],
        [shrink_weight],
    ]
    chunks = [(0, 0, 384), (0, 384, 384), (1, 0, 384), (2, 0, 384), (3, 0, 384), (3, 384, 384), (4, 0, 384), (4, 384, 384)]
    text = tokens.reshape(amount, width)
    flat, unit_row = (amount, width), ((amount, 128), f32)
    low_flat, full_flat = (flat, bf16), (flat, f32)
    probs_self, probs_cross = (pairs, tiles_of, 4 * slots, 2 * slots), (rows, tiles_of, 2 * slots, padded)
    image_part, vector = ((window, padded, width), bf16), ((16, width), f32)
    image, weights, norms, saved, near = forward(
        [image_rows, row_lengths],
        [text, box_mask, first_gain, first_shift, second_gain, second_shift, third_gain, third_shift, expand_bias],
        patches.transpose(1, 0, 2),
        shards,
        [low_flat] * 3 + [(probs_self, bf16), low_flat, full_flat, unit_row, low_flat, low_flat]
        + [image_part, image_part, (probs_cross, bf16), low_flat, full_flat, unit_row, full_flat, low_flat],
        ((window, padded, depth), bf16),
        chunks,
        own,
    )
    self_weights, cross_weights, keyval, expand, shrink = weights
    (
        queries, keys, values, self_probs, self_context, first_unit, first_inverse, first_low, cross_queries, image_keys,
        image_values, cross_probs, cross_context, second_unit, second_inverse, second_value, second_low,
    ) = saved
    joined, expand_grad, shrink_grad, feed_vectors, second_up = on_slots(
        feed_kernel,
        "feed",
        [],
        [second_value, second_low, norms, expand, shrink, cotangent.reshape(flat)],
        [low_flat, (expand.shape, bf16), (shrink.shape, bf16), vector, full_flat],
        [((parts,) + flat, bf16)] * 2 + [full_flat, unit_row, low_flat],
        parts_in=(3, 4),
        parts_out=(1, 2),
        ordered=True,
    )
    cross_weights_grad, keyval_grad, patch, cross_vectors, first_up = on_slots(
        cross_back_kernel,
        "cross_back",
        [image],
        [second_up, second_unit, second_inverse, norms, cross_weights, cross_context, cross_queries, image_values]
        + [image_keys, cross_probs, first_low, keyval, near],
        [(cross_weights.shape, bf16), (keyval.shape, bf16), ((parts, window * (cells - 1) + 16, depth // parts), bf16)]
        + [vector, full_flat],
        [low_flat, full_flat, full_flat, (image_part[0], f32), (image_part[0], f32), low_flat],
        ordered=True,
    )
    order = [(4, 0, 384), (4, 384, 384), (3, 0, 384), (3, 384, 384), (1, 0, 384), (2, 0, 384), (0, 0, 384), (0, 384, 384)]
    sums, windows, merged, vectors, text_grad = reduce_shards(
        [cross_weights_grad, keyval_grad, expand_grad, shrink_grad],
        patch,
        [feed_vectors, cross_vectors],
        [first_up, first_unit, first_inverse, norms, self_weights, self_context, queries, keys, values, self_probs, text],
        window,
        starts[1] - starts[0],
        order,
        own,
    )
    square, piece, line = ((width, width), f32), ((inner, width), f32), ((width,), f32)
    text_grad, project, self_out, query, cross_out, pixel, expand_sum, shrink_sum, patch_grad, *lines = on_slots(
        functools.partial(finish_kernel, not own),
        "finish",
        [image],
        list(sums) + [vectors, windows, merged, text_grad],
        [full_flat, ((3 * inner, width), f32), piece, piece, piece, ((2 * inner, depth), f32), square, square]
        + [((cells, group_images, depth // parts), f32)]
        + [line] * 7,
        [],
    )
    return (
        joined.reshape(tokens.shape),
        text_grad.reshape(tokens.shape),
        patch_grad.transpose(1, 0, 2),
        project.reshape(3, inner, width).transpose(0, 2, 1),
        self_out,
        lines[0],
        lines[1],
        query.T,
        pixel.reshape(2, inner, depth).transpose(0, 2, 1),
        cross_out,
        lines[2],
        lines[3],
        expand_sum,
        lines[6],
        shrink_sum,
        lines[4],
        lines[5],
    )


def solution(mesh):
    parts = mesh.shape["mp"]
    own = mesh.shape["dp"] == 8 and parts == 4
    return jax.shard_map(
        functools.partial(per_device, parts=parts, own=own),
        mesh=mesh,
        in_specs=(
            P(("dp", "mp"), None, None),
            P("dp", None, None),
            P("dp", None),
            P("dp"),
            P("dp", None),
            P(None, None, "mp"),
            P("mp", None),
            P(),
            P(),
            P(None, "mp"),
            P(None, None, "mp"),
            P("mp", None),
            P(),
            P(),
            P(None, "mp"),
            P("mp"),
            P("mp", None),
            P(),
            P(),
            P(("dp", "mp"), None, None),
        ),
        out_specs=(
            P(("dp", "mp"), None, None),
            P(("dp", "mp"), None, None),
            P("dp", None, "mp"),
            P(None, None, "mp"),
            P("mp", None),
            P(),
            P(),
            P(None, "mp"),
            P(None, None, "mp"),
            P("mp", None),
            P(),
            P(),
            P(None, "mp"),
            P("mp"),
            P("mp", None),
            P(),
            P(),
        ),
        check_vma=False,
    )
```

```python
import functools

import jax
import jax.numpy as jnp
from jax import lax
from jax.experimental import pallas as pl
from jax.experimental.pallas import tpu as pltpu
from jax.sharding import PartitionSpec as P

HEAD_DIM = 64
ROWS_MAX = 7
MESH = pl.DeviceIdType.MESH


def place():
    index = lax.axis_index("dp")
    plane = lax.axis_index("mp")
    y, x, c = index // 4, (index // 2) % 2, index % 2
    return index, plane, y, x, c


def partners(index, plane):
    core = (index + 1 - 2 * (index % 2), plane)
    across = (index + 2 - 4 * ((index // 2) % 2), plane)
    along = (index + 4 - 8 * (index // 4), plane)
    planes = [(index, lax.rem(plane + step, 4)) for step in (1, 2, 3)]
    return core, across, along, planes


def greet(peers):
    barrier = pltpu.get_barrier_semaphore()
    for peer in peers:
        pl.semaphore_signal(barrier, inc=1, device_id=peer, device_id_type=MESH)
    pl.semaphore_wait(barrier, len(peers))


class Sends:
    def __init__(self):
        self.stages, self.all = {}, []

    def start(self, name, k, items):
        copies = []
        for source, target, sends, recvs, peer in items:
            copy = pltpu.make_async_remote_copy(
                src_ref=source, dst_ref=target, send_sem=sends, recv_sem=recvs, device_id=peer, device_id_type=MESH
            )
            copy.start()
            copies.append(copy)
        self.stages[name, k] = copies
        self.all.extend(copies)

    def arrived(self, name, k):
        for copy in self.stages[name, k]:
            copy.wait_recv()

    def close(self):
        for copy in self.all:
            copy.wait_send()


class Gather:
    stages = 4

    def __init__(self, chunks, shards, wholes, sems, window, gap):
        self.chunks, self.shards, self.wholes, self.window = chunks, shards, wholes, window
        self.sems, self.gap = sems, gap
        self.index, self.plane, self.y, self.x, self.c = place()
        self.core, self.across, self.along, self.planes = partners(self.index, self.plane)
        self.others = [lax.rem(self.plane + step, 4) for step in (1, 2, 3)]
        self.sends = Sends()

    def sizes(self, k):
        which, base, rows = self.chunks[k]
        return which, base, rows // 8, self.wholes[which].shape[2] // 2

    def level(self, k):
        which, base, r, w = self.sizes(k)
        _, _, send, recv = self.sems[:4]
        self.own(which)
        items = []
        for h, first in enumerate((self.x * 2 + self.y, self.y * 2 + self.x)):
            here = (pl.ds(pl.multiple_of(base + (self.c * 4 + first) * r, 16), r), pl.ds(h * w, w))
            for j, peer in enumerate(self.planes):
                piece = self.wholes[which].at[(self.plane,) + here]
                items.append((piece, piece, send.at[k, h, j], recv.at[k, h, j], peer))
        self.sends.start("level", k, items)

    def near(self, k):
        which, base, r, w = self.sizes(k)
        send, recv = self.sems[4:6]
        self.sends.arrived("level", k)
        if k + self.window < len(self.chunks):
            self.level(k + self.window)
        items = []
        for h, first in enumerate((self.x * 2 + self.y, self.y * 2 + self.x)):
            row = pl.multiple_of(base + (self.c * 4 + first) * r, 16)
            for j, other in enumerate(self.others):
                piece = self.wholes[which].at[other, pl.ds(row, r), pl.ds(h * w, w)]
                items.append((piece, piece, send.at[k, h, j], recv.at[k, h, j], (self.along, self.across)[h]))
        self.sends.start("near", k, items)

    def far(self, k):
        which, base, r, w = self.sizes(k)
        send, recv = self.sems[6:8]
        self.sends.arrived("near", k)
        items = []
        for h, first in enumerate((self.x, self.y)):
            row = pl.multiple_of(base + (self.c * 4 + first * 2) * r, 16)
            for j, other in enumerate(self.others):
                piece = self.wholes[which].at[other, pl.ds(row, 2 * r), pl.ds(h * w, w)]
                items.append((piece, piece, send.at[k, h, j], recv.at[k, h, j], (self.across, self.along)[h]))
        self.sends.start("far", k, items)

    def cross(self, k):
        which, base, r, w = self.sizes(k)
        send, recv = self.sems[8:10]
        self.sends.arrived("far", k)
        row = pl.multiple_of(base + self.c * 4 * r, 16)
        items = []
        for j, other in enumerate(self.others):
            piece = self.wholes[which].at[other, pl.ds(row, 4 * r), :]
            items.append((piece, piece, send.at[k, j], recv.at[k, j], self.core))
        self.sends.start("core", k, items)

    def own(self, which):
        for copy in self.local.pop(which, ()):
            copy.wait()

    def begin(self):
        self.local = {}
        for which, pieces in enumerate(self.shards):
            row, self.local[which] = 0, []
            for i, piece in enumerate(pieces):
                target = self.wholes[which].at[self.plane, pl.ds(row, piece.shape[0]), :]
                copy = pltpu.make_async_copy(piece, target, self.sems[0].at[which, i])
                copy.start()
                self.local[which].append(copy)
                row += piece.shape[0]
        greet([self.core, self.across, self.along] + self.planes)
        for k in range(self.window):
            self.level(k)

    def step(self, t):
        if 0 <= t < len(self.chunks):
            self.near(t)
        if 0 <= t - self.gap < len(self.chunks):
            self.far(t - self.gap)
        if 0 <= t - 2 * self.gap < len(self.chunks):
            self.cross(t - 2 * self.gap)

    @property
    def steps(self):
        return len(self.chunks) + 2 * self.gap

    def ready(self, k):
        self.sends.arrived("core", k)

    @staticmethod
    def scratch(count, total):
        dma = pltpu.SemaphoreType.DMA
        return [dma((count, 2)), dma((count,))] + [dma((total, 2, 3))] * 6 + [dma((total, 3))] * 2


class Ticks:
    def __init__(self, gather, outs, sem):
        self.gather, self.outs, self.sem = gather, outs, sem
        self.now, self.done, self.final = 0, 0, []

    def __call__(self):
        gather, total = self.gather, len(self.gather.chunks)
        if self.now < gather.steps:
            gather.step(self.now)
        k = self.now - 3 * gather.gap
        if 0 <= k < total:
            gather.ready(k)
            self.done = k + 1
            which = gather.chunks[k][0]
            if k + 1 == total or gather.chunks[k + 1][0] != which:
                copy = pltpu.make_async_copy(gather.wholes[which], self.outs[which], self.sem.at[which])
                copy.start()
                self.final.append(copy)
        self.now += 1

    def wait(self, which):
        last = max(k for k, chunk in enumerate(self.gather.chunks) if chunk[0] == which)
        while self.done <= last:
            self()

    def close(self):
        while self.done < len(self.gather.chunks):
            self()
        self.gather.sends.close()
        for copy in self.final:
            copy.wait()


def forward_kernel(chunks, pieces, count, *refs):
    counts, lengths, tokens, boxes = refs[:4]
    vectors, cells_far, refs = refs[4:11], refs[11], refs[12:]
    shards, arrays = [], len(pieces)
    for amount in pieces:
        shards.append(refs[:amount])
        refs = refs[amount:]
    image, outs, biases, refs = refs[0], refs[1 : arrays + 1], refs[arrays + 1], refs[arrays + 2 :]
    far, refs = refs[: count + 1], refs[count + 1 :]
    wholes, refs = refs[:arrays], refs[arrays:]
    saved = [Slot(far[i], refs[2 * i], refs[2 * i + 1]) for i in range(count + 1)]
    *saved, near = saved
    refs = refs[2 * count + 2 :]
    (wide, cells_all, cell_ok, norms, caption, bias_send, bias_recv, cells_sem), sems = refs[:8], refs[8:]
    gather = Gather(chunks, shards, wholes, sems, 2, 1)
    copy = pltpu.make_async_copy(cells_far, cells_all, cells_sem)
    copy.start()
    gather.begin()
    ticks = Ticks(gather, outs, sems[1])
    ticks()
    ticks()
    copy.wait()
    prepare(counts, lengths, boxes, vectors, cells_all, image, caption, cell_ok, norms, near.near, gather.plane)
    near.flush()
    gather.sends.start(
        "bias", 0, [(norms, biases.at[gather.plane], bias_send.at[j], bias_recv.at[j], peer) for j, peer in enumerate(gather.planes)]
    )
    biases[gather.plane] = norms[...]
    rows = cell_ok.shape[0]
    forward_steps(
        ticks, image, caption, lambda r: lengths[gather.plane * rows + r], tokens, near.near, cell_ok, wholes[:3], norms, saved,
        wide,
    )
    gather.sends.arrived("bias", 0)
    ticks.close()
    for slot in saved + [near]:
        slot.finish()


def gather_forward(scalars, inputs, cells_all, shards, outputs, near, chunks):
    dma, bf16, f32, arrays, count = pltpu.SemaphoreType.DMA, jnp.bfloat16, jnp.float32, len(shards), len(outputs)
    any_space, vmem = pl.BlockSpec(memory_space=pl.ANY), pl.BlockSpec(memory_space=pltpu.VMEM)
    smem = pl.BlockSpec(memory_space=pltpu.SMEM)
    tokens = inputs[0]
    width = tokens.shape[1]
    rows, padded = tokens.shape[0] // 40, near[0][1]
    shapes = [(4, sum(piece.shape[0] for piece in pieces), pieces[0].shape[1]) for pieces in shards]
    flat = [piece for pieces in shards for piece in pieces]
    outputs = outputs + [near]
    results = pl.pallas_call(
        functools.partial(forward_kernel, chunks, [len(pieces) for pieces in shards], count),
        out_shape=[jax.ShapeDtypeStruct((rows,), jnp.int32)]
        + [jax.ShapeDtypeStruct(shape, bf16) for shape in shapes]
        + [jax.ShapeDtypeStruct((4, 8, width), f32)]
        + [jax.ShapeDtypeStruct(shape, kind) for shape, kind in outputs],
        in_specs=[smem] * len(scalars) + [vmem] * len(inputs) + [any_space] * (len(flat) + 1),
        out_specs=[smem] + [any_space] * arrays + [vmem] + [any_space] * (count + 1),
        scratch_shapes=[pltpu.VMEM(shape, bf16) for shape in shapes]
        + [entry for shape, kind in outputs for entry in slot_scratch(shape, kind)]
        + [pltpu.VMEM(tokens.shape, f32), pltpu.VMEM(cells_all.shape, bf16), pltpu.VMEM((rows, padded), f32)]
        + [pltpu.VMEM((8, width), f32), pltpu.SMEM((rows,), jnp.int32)]
        + [dma((3,)), dma((3,)), dma(())]
        + Gather.scratch(arrays, len(chunks)),
        compiler_params=pltpu.CompilerParams(collective_id=0, has_side_effects=True, vmem_limit_bytes=63 << 20),
        name="gather_forward",
    )(*scalars, *inputs, cells_all, *flat)
    return results[0], results[1 : arrays + 1], results[arrays + 1], results[arrays + 2 : -1], results[-1]


class Alone:
    def __call__(self):
        pass

    def wait(self, which):
        pass


def lone_forward_kernel(scalars, inputs, outputs, scratch):
    tokens, boxes, *vectors, cells_all, self_weights, cross_weights, keyval = (slot.ready() for slot in inputs)
    *saved, near = outputs
    counts, lengths, image = scalars
    wide, cell_ok, norms, caption = scratch
    rows, plane = cell_ok.shape[0], lax.axis_index("mp")
    prepare(counts, lengths, boxes, vectors, cells_all, image, caption, cell_ok, norms, near.near, plane)
    near.flush()
    forward_steps(
        Alone(), image, caption, lambda r: lengths[plane * rows + r], tokens, near.near, cell_ok,
        (self_weights, cross_weights, keyval), norms, saved, wide,
    )


class Reduce:
    def __init__(self, chunks, grads, sums, buffers, sems, local):
        self.chunks, self.grads, self.sums, self.sems, self.local = chunks, grads, sums, sems, local
        self.mine, self.core_in, self.near_in, self.far_in, self.plane_in, self.relay_in = [], [], [], [], [], []
        buffers = list(buffers)
        self.index, self.plane, self.y, self.x, self.c = place()
        for which, base, rows in chunks:
            if which in local:
                self.mine.append((local[which], base + self.c * (rows // 2)))
            else:
                self.mine.append((buffers.pop(0), 0))
            self.core_in.append(buffers.pop(0))
            self.near_in.append(buffers.pop(0))
            self.far_in.append(buffers.pop(0))
            self.plane_in.append(buffers.pop(0))
            self.relay_in.append(buffers.pop(0))
        self.core, self.across, self.along, self.planes = partners(self.index, self.plane)
        self.others = [lax.rem(self.plane + step, 4) for step in (1, 2, 3)]
        self.sends = Sends()
        self.outer = (self.plane == 0) | (self.plane == 3)
        self.next = jnp.where(self.plane == 0, 1, 2)
        self.beyond = 3 - self.next
        self.edge = jnp.where(self.plane == 1, 0, 3)
        self.fetched, self.final = {}, []
        self.diagonal = (self.index + 6 - 4 * self.x - 8 * self.y, self.plane)
        self.short = range(len(chunks) - 2, len(chunks))
        long = [self.begin, self.near, self.far, self.level, self.bridge]
        long += [self.out_near, self.out_far, self.out_core, self.end]
        brief = [self.begin, self.near, self.far, self.level, self.out_direct, self.out_core, self.end]
        slow = long[:4] + [self.rest] + long[4:5] + [self.rest] + long[5:]
        self.order = [brief if k in self.short else slow if k < len(chunks) // 2 else long for k in range(len(chunks))]

    @staticmethod
    def scratch(chunks, widths, local):
        low, dma, total = jnp.bfloat16, pltpu.SemaphoreType.DMA, len(chunks)
        shapes = []
        for which, _, r in chunks:
            w = widths[which]
            shapes += [] if which in local else [(4, r // 2, w)]
            shapes += [(4, r // 2, w), (2, 4, r // 4, w // 2), (2, 4, r // 8, w // 2), (2, 3, r // 8, w // 2)]
            shapes += [(2, r // 8, w // 2)]
        sems = [dma((total,))] * 4 + [dma((total, 2))] * 8 + [dma((total, 2, 3))] * 2 + [dma((total,))] * 2 + [dma((total, 2))]
        sems += [dma((total, 2, 3))] * 2
        return [pltpu.VMEM(shape, low) for shape in shapes], sems

    def sizes(self, k):
        which, base, rows = self.chunks[k]
        return which, base, rows // 8, self.grads[which].shape[2] // 2

    @staticmethod
    def add(total, total_row, total_col, part, part_col, rows, cols):
        @pl.loop(0, rows // 16)
        def _(i):
            here = (pl.ds(pl.multiple_of(total_row + i * 16, 16), 16), pl.ds(total_col, cols))
            there = (pl.ds(pl.multiple_of(i * 16, 16), 16), pl.ds(part_col, cols))
            ours = [total[(shard,) + here].astype(jnp.float32) for shard in range(4)]
            theirs = [part[(shard,) + there].astype(jnp.float32) for shard in range(4)]
            sums = [(left + right).astype(jnp.bfloat16) for left, right in zip(ours, theirs)]
            for shard in range(4):
                total[(shard,) + here] = sums[shard]

    def places(self, r, w):
        return [((self.x * 2 + self.y) * r, 0), ((self.y * 2 + self.x) * r, w)]

    def rest(self, k):
        pass

    def begin(self, k):
        which, base, r, w = self.sizes(k)
        theirs = pl.multiple_of(base + (1 - self.c) * 4 * r, 16)
        ours = pl.multiple_of(base + self.c * 4 * r, 16)
        source = self.grads[which].at[:, pl.ds(theirs, 4 * r), :]
        self.sends.start("core", k, [(source, self.core_in[k], self.sems[0].at[k], self.sems[1].at[k], self.core)])
        if which not in self.local:
            source = self.grads[which].at[:, pl.ds(ours, 4 * r), :]
            self.fetched[k] = pltpu.make_async_copy(source, self.mine[k][0], self.sems[2].at[k])
            self.fetched[k].start()

    def near(self, k):
        which, base, r, w = self.sizes(k)
        mine, offset = self.mine[k]
        if k in self.fetched:
            self.fetched[k].wait()
        self.sends.arrived("core", k)
        items = []
        for h, (bit, peer) in enumerate([(self.x, self.across), (self.y, self.along)]):
            self.add(mine, offset, h * w, self.core_in[k], h * w, 4 * r, w)
            row = pl.multiple_of(offset + (1 - bit) * 2 * r, 16)
            source = mine.at[:, pl.ds(row, 2 * r), pl.ds(h * w, w)]
            items.append((source, self.near_in[k].at[h], self.sems[4].at[k, h], self.sems[5].at[k, h], peer))
        self.sends.start("near", k, items)

    def far(self, k):
        which, base, r, w = self.sizes(k)
        mine, offset = self.mine[k]
        self.sends.arrived("near", k)
        items = []
        for h, (bit, second, peer) in enumerate([(self.x, self.y, self.along), (self.y, self.x, self.across)]):
            row = offset + bit * 2 * r
            self.add(mine, row, h * w, self.near_in[k].at[h], 0, 2 * r, w)
            row = pl.multiple_of(row + (1 - second) * r, 16)
            source = mine.at[:, pl.ds(row, r), pl.ds(h * w, w)]
            items.append((source, self.far_in[k].at[h], self.sems[6].at[k, h], self.sems[7].at[k, h], peer))
        self.sends.start("far", k, items)


    def hop(self, k, h, j, source, target, recv, to):
        return pltpu.make_async_remote_copy(
            src_ref=source, dst_ref=target, send_sem=self.sems[12].at[k, h, j], recv_sem=recv,
            device_id=(self.index, to), device_id_type=MESH,
        )

    def slot(self, k, h, j):
        return self.plane_in[k].at[h, j], self.sems[13].at[k, h, j]

    def bridge_slot(self, k, h):
        return self.relay_in[k].at[h], self.sems[16].at[k, h]

    def level(self, k):
        which, base, r, w = self.sizes(k)
        mine, offset = self.mine[k]
        self.sends.arrived("far", k)
        for h, (row, col) in enumerate(self.places(r, w)):
            self.add(mine, offset + row, col, self.far_in[k].at[h], 0, r, w)

        def piece(h, plane):
            row, col = self.places(r, w)[h]
            return mine.at[plane, pl.ds(pl.multiple_of(offset + row, 16), r), pl.ds(col, w)]

        @pl.when(self.outer)
        def _():
            for h in range(2):
                other = 3 - self.plane
                if k in self.short:
                    self.hop(k, h, 2, piece(h, other), *self.slot(k, h, 2), other).start()
                else:
                    self.hop(k, h, 2, piece(h, other), *self.bridge_slot(k, h), self.next).start()
            for h in range(2):
                self.hop(k, h, 1, piece(h, self.beyond), *self.slot(k, h, 2), self.beyond).start()
                self.hop(k, h, 0, piece(h, self.next), *self.slot(k, h, 1), self.next).start()

        @pl.when(jnp.logical_not(self.outer))
        def _():
            for h in range(2):
                self.hop(k, h, 1, piece(h, 3 - self.plane), *self.slot(k, h, 0), 3 - self.plane).start()
                self.hop(k, h, 0, piece(h, self.edge), *self.slot(k, h, 0), self.edge).start()
                if k in self.short:
                    other = 3 - self.edge
                    self.hop(k, h, 2, piece(h, other), *self.slot(k, h, 1), other).start()

    def bridge(self, k):
        which, base, r, w = self.sizes(k)
        mine, offset = self.mine[k]
        relay = self.relay_in[k]

        @pl.when(jnp.logical_not(self.outer))
        def _():
            for h, (row, col) in enumerate(self.places(r, w)):
                self.hop(k, h, 2, relay.at[h], *self.bridge_slot(k, h), self.plane).wait_recv()

                @pl.loop(0, r // 16)
                def _(i):
                    step = pl.ds(pl.multiple_of(i * 16, 16), 16)
                    here = pl.ds(pl.multiple_of(offset + row + i * 16, 16), 16)
                    ours = mine[3 - self.edge, here, pl.ds(col, w)].astype(jnp.float32)
                    relay[h, step, :] = (ours + relay[h, step, :].astype(jnp.float32)).astype(jnp.bfloat16)

                self.hop(k, h, 2, relay.at[h], *self.slot(k, h, 1), 3 - self.edge).start()

    def add_planes(self, k, amount):
        which, base, r, w = self.sizes(k)
        mine, offset = self.mine[k]
        for h, (row, col) in enumerate(self.places(r, w)):
            for j in range(amount):
                place, sem = self.slot(k, h, j)
                self.hop(k, h, j, place, place, sem, self.plane).wait_recv()

            @pl.loop(0, r // 16)
            def _(i):
                step = pl.ds(pl.multiple_of(i * 16, 16), 16)
                here = pl.ds(pl.multiple_of(offset + row + i * 16, 16), 16)
                total = mine[self.plane, here, pl.ds(col, w)].astype(jnp.float32)
                for j in range(amount):
                    total = total + self.plane_in[k][h, j, step, :].astype(jnp.float32)
                here = pl.ds(pl.multiple_of(row + i * 16, 16), 16)
                self.core_in[k][0, here, pl.ds(col, w)] = total.astype(jnp.bfloat16)

    def pieces(self, k):
        which, base, r, w = self.sizes(k)
        return [
            self.core_in[k].at[0, pl.ds(pl.multiple_of(row, 16), r), pl.ds(col, w)] for row, col in self.places(r, w)
        ]

    def out_near(self, k):
        @pl.when(self.outer)
        def _():
            self.add_planes(k, 2)

        @pl.when(jnp.logical_not(self.outer))
        def _():
            self.add_planes(k, 3)

        items = []
        for h, piece in enumerate(self.pieces(k)):
            peer = (self.along, self.across)[h]
            items.append((piece, piece, self.sems[8].at[k, h], self.sems[9].at[k, h], peer))
        self.sends.start("out_near", k, items)

    def out_direct(self, k):
        self.add_planes(k, 3)
        items = []
        for h, piece in enumerate(self.pieces(k)):
            for j, peer in enumerate((self.diagonal, self.along, self.across)):
                items.append((piece, piece, self.sems[17].at[k, h, j], self.sems[18].at[k, h, j], peer))
        self.sends.start("out_far", k, items)

    def out_far(self, k):
        which, base, r, w = self.sizes(k)
        self.sends.arrived("out_near", k)
        items = []
        for h, (bit, peer) in enumerate([(self.x, self.across), (self.y, self.along)]):
            piece = self.core_in[k].at[0, pl.ds(pl.multiple_of(bit * 2 * r, 16), 2 * r), pl.ds(h * w, w)]
            items.append((piece, piece, self.sems[10].at[k, h], self.sems[11].at[k, h], peer))
        self.sends.start("out_far", k, items)

    def out_core(self, k):
        which, base, r, w = self.sizes(k)
        self.sends.arrived("out_far", k)
        target = self.sums[which].at[pl.ds(pl.multiple_of(base + self.c * 4 * r, 16), 4 * r), :]
        source = self.core_in[k].at[0]
        self.sends.start("out_core", k, [(source, target, self.sems[14].at[k], self.sems[15].at[k], self.core)])
        copy = pltpu.make_async_copy(source, target, self.sems[3].at[k])
        copy.start()
        self.final.append(copy)

    def end(self, k):
        self.sends.arrived("out_core", k)

    @property
    def steps(self):
        return max(k + len(stages) for k, stages in enumerate(self.order))

    def step(self, t):
        for k in reversed(range(len(self.chunks))):
            if 0 <= t - k < len(self.order[k]):
                self.order[k][t - k](k)

    def close(self):
        self.sends.close()
        for k in range(len(self.chunks)):
            for h in range(2):
                for j in range(3):
                    place, sem = self.slot(k, h, j)
                    self.hop(k, h, j, place, place, sem, self.plane).wait_send()
        for copy in self.final:
            copy.wait()


class ReduceTicks:
    def __init__(self, reduce, vector_sum, vector_in, send, recv):
        self.reduce, self.vector_sum, self.vector_in, self.send, self.recv = reduce, vector_sum, vector_in, send, recv
        self.now = 0

    def __call__(self):
        if self.now < self.reduce.steps:
            self.reduce.step(self.now)
        self.now += 1

    def sum_vectors(self):
        reduce, total, arrived = self.reduce, self.vector_sum, self.vector_in
        for t, peer in enumerate((reduce.core, reduce.across, reduce.along)):
            reduce.sends.start("vector", t, [(total.at[t], arrived.at[t], self.send.at[t], self.recv.at[t], peer)])
            self()
            reduce.sends.arrived("vector", t)
            total[t + 1] = total[t] + arrived[t]
        items = [
            (total.at[3], arrived.at[3 + j], self.send.at[3 + j], self.recv.at[3 + j], peer)
            for j, peer in enumerate(reduce.planes)
        ]
        reduce.sends.start("vector", 3, items)
        self()
        reduce.sends.arrived("vector", 3)
        ordered = [arrived[3 + j] for j in range(3)]
        plane, own = reduce.plane, total[3]
        slots = []
        for m in range(4):
            value = own
            for j in range(3):
                value = jnp.where(reduce.others[j] == m, ordered[j], value)
            slots.append(value)
        total[4] = (slots[0] + slots[1]) + (slots[2] + slots[3])


class Patches:
    def __init__(self, patch, windows, merged, buffers, sems, index, plane, images, shift):
        self.patch, self.windows, self.merged = patch, windows, merged
        self.relay, self.own, self.total = buffers
        self.sends, self.recvs, self.relay_recv, self.merged_recv, self.local, self.fetch = sems
        self.index, self.plane = index, plane
        self.outer = (plane == 0) | (plane == 3)
        self.first = plane < 2
        self.next = jnp.where(plane == 0, 1, 2)
        self.far = 3 - self.next
        self.edge = jnp.where(plane == 1, 0, 3)
        self.across = 3 - plane
        self.images, self.shift = images, shift
    def copy(self, slot, source, target, recv, to):
        return pltpu.make_async_remote_copy(
            src_ref=source, dst_ref=target, send_sem=self.sends.at[slot], recv_sem=recv, device_id=(self.index, to),
            device_id_type=MESH,
        )

    def direct(self, slot, to):
        return self.copy(slot, self.patch.at[to], self.windows.at[self.plane], self.recvs.at[self.plane], to)

    def to_relay(self):
        return self.copy(1, self.patch.at[self.across], self.relay, self.relay_recv.at[0], self.next)

    def to_edge(self):
        return self.copy(1, self.total, self.merged, self.merged_recv.at[0], 3 - self.edge)

    def keep(self):
        return pltpu.make_async_copy(self.patch.at[self.plane], self.windows.at[self.plane], self.local.at[0])

    def take(self):
        return pltpu.make_async_copy(self.patch.at[3 - self.edge], self.own, self.fetch.at[0])

    def begin(self):
        self.keep().start()

        @pl.when(self.outer)
        def _():
            self.to_relay().start()
            self.direct(0, self.far).start()

        @pl.when(jnp.logical_not(self.outer))
        def _():
            self.take().start()
            self.direct(0, self.across).start()

    def middle(self):
        @pl.when(self.outer)
        def _():
            self.direct(2, self.next).start()

        @pl.when(jnp.logical_not(self.outer))
        def _():
            self.direct(2, self.edge).start()
            self.take().wait()
            self.to_relay().wait_recv()

            @pl.when(self.first)
            def _():
                self.add(self.relay, self.own)

            @pl.when(jnp.logical_not(self.first))
            def _():
                self.add(self.own, self.relay)

            self.to_edge().start()

    def add(self, early, late):
        images, shift, total = self.images, self.shift, self.total
        size = (early.shape[0] - 16) // images
        for i in range(images + shift):
            here = pl.ds(i * size, size)
            there = pl.ds((i - shift) * size, size)
            if i < shift:
                total[here, :] = early[here, :]
            elif i < images:
                both = early[here, :].astype(jnp.float32) + late[there, :].astype(jnp.float32)
                total[here, :] = both.astype(jnp.bfloat16)
            else:
                total[here, :] = late[there, :]
        row = lax.broadcasted_iota(jnp.int32, (16, 16), 0)
        column = lax.broadcasted_iota(jnp.int32, (16, 16), 1)
        down = (row == column + shift).astype(jnp.bfloat16)
        last = pl.ds(images * size, 16)
        both = early[last, :].astype(jnp.float32) + nn(down, late[last, :])
        total[pl.ds((images + shift) * size, 16), :] = both.astype(jnp.bfloat16)

    def end(self):
        self.keep().wait()

        @pl.when(self.outer)
        def _():
            self.copy(0, self.patch.at[0], self.windows.at[self.next], self.recvs.at[self.next], self.next).wait_recv()
            self.copy(1, self.total, self.merged, self.merged_recv.at[0], self.far).wait_recv()
            self.to_relay().wait_send()
            self.direct(0, self.far).wait_send()
            self.direct(2, self.next).wait_send()

        @pl.when(jnp.logical_not(self.outer))
        def _():
            for source in (self.across, 0, 3):
                self.copy(0, self.patch.at[0], self.windows.at[source], self.recvs.at[source], self.across).wait_recv()
            self.direct(0, self.across).wait_send()
            self.to_edge().wait_send()
            self.direct(2, self.edge).wait_send()


def back_kernel(chunks, count, slots, window, shift, *refs):
    grads, patch, early, refs = refs[:count], refs[count], refs[count + 1 : count + 3], refs[count + 3 :]
    inputs, refs = refs[:slots], refs[slots:]
    sums, refs = refs[: count + 1], refs[count + 1 :]
    (windows, merged, vector_sum, text_far), refs = refs[:4], refs[4:]
    inputs = [Slot(inputs[i], refs[2 * i], refs[2 * i + 1]) for i in range(slots)]
    refs = refs[2 * slots :]
    self_grad, text_sem, refs = refs[0], refs[1], refs[2:]
    scratch, refs = refs[:5], refs[5:]
    (vector_in, vector_send, vector_recv), patch_refs, refs = refs[:3], refs[3:12], refs[12:]
    sems, buffers = refs[:19], refs[19:]
    for slot in inputs:
        slot.fetch()
    reduce = Reduce(chunks, [self_grad, *grads], sums, buffers, sems, {0: self_grad})
    greet([reduce.core, reduce.across, reduce.along, reduce.diagonal] + reduce.planes)
    ticks = ReduceTicks(reduce, vector_sum, vector_in, vector_send, vector_recv)
    ticks()
    patches = Patches(
        patch, windows, merged, patch_refs[:3], patch_refs[3:], reduce.index, reduce.plane, window, shift
    )
    patches.begin()
    vector_sum[0] = early[0][...] + early[1][...]
    text_grad = inputs[0].near
    self_back_steps(ticks, inputs, self_grad, vector_sum.at[0], text_grad, scratch)
    text_copy = pltpu.make_async_copy(text_grad, text_far, text_sem.at[0])
    text_copy.start()
    patches.middle()
    ticks()
    ticks.sum_vectors()
    while ticks.now < reduce.steps:
        ticks()
    patches.end()
    reduce.close()
    text_copy.wait()


def reduce_back(grads, patch, early, inputs, window, shift, chunks):
    count, dma, f32, bf16 = len(grads), pltpu.SemaphoreType.DMA, jnp.float32, jnp.bfloat16
    any_space, vmem = pl.BlockSpec(memory_space=pl.ANY), pl.BlockSpec(memory_space=pltpu.VMEM)
    weights, flat = inputs[4].shape, inputs[0].shape
    together = (patch.shape[1] + shift * ((patch.shape[1] - 16) // window), patch.shape[2])
    widths = [weights[2]] + [grad.shape[2] for grad in grads]
    buffers, sems = Reduce.scratch(chunks, widths, {0})
    *sums, windows, merged, vector_sum, text_grad = pl.pallas_call(
        functools.partial(back_kernel, chunks, count, len(inputs), window, shift),
        out_shape=[jax.ShapeDtypeStruct(shape[1:], bf16) for shape in [weights] + [grad.shape for grad in grads]]
        + [jax.ShapeDtypeStruct(patch.shape, bf16), jax.ShapeDtypeStruct(together, bf16)]
        + [jax.ShapeDtypeStruct((5,) + early[0].shape, f32)]
        + [jax.ShapeDtypeStruct(flat, f32)],
        in_specs=[any_space] * (count + 1) + [vmem] * 2 + [any_space] * len(inputs),
        out_specs=[any_space] * (count + 3) + [vmem, any_space],
        scratch_shapes=[entry for array in inputs for entry in slot_scratch(array.shape, array.dtype)]
        + [pltpu.VMEM(weights, bf16), dma((1,))]
        + [pltpu.VMEM(flat, bf16)] * 5
        + [pltpu.VMEM((6,) + early[0].shape, f32), dma((6,)), dma((6,))]
        + [pltpu.VMEM(patch.shape[1:], bf16), pltpu.VMEM(patch.shape[1:], bf16), pltpu.VMEM(together, bf16)]
        + [dma((3,)), dma((4,)), dma((1,)), dma((1,)), dma((1,)), dma((1,))]
        + sems
        + buffers,
        compiler_params=pltpu.CompilerParams(collective_id=1, has_side_effects=True, vmem_limit_bytes=63 << 20),
        name="reduce_back",
    )(*grads, patch, *early, *inputs)
    return sums, windows, merged, vector_sum, text_grad


class Slot:
    def __init__(self, far, near, sem, parts=0):
        self.far, self.near, self.sem, self.parts, self.waited = far, near, sem, parts, False

    def copy(self, out, m=None):
        far, near = (self.far, self.near) if m is None else (self.far.at[m], self.near.at[m])
        sem = self.sem.at[0 if m is None else m]
        return pltpu.make_async_copy(near, far, sem) if out else pltpu.make_async_copy(far, near, sem)

    def fetch(self):
        for m in range(self.parts) if self.parts else (None,):
            self.copy(False, m).start()

    def ready(self):
        if not self.waited:
            self.waited = True
            for m in range(self.parts) if self.parts else (None,):
                self.copy(False, m).wait()
        return self.near

    def flush(self, m=None):
        self.copy(True, m).start()

    def finish(self):
        for m in range(self.parts) if self.parts else (None,):
            self.copy(True, m).wait()


def slot_scratch(shape, kind, parts=0):
    return [pltpu.VMEM(shape, kind), pltpu.SemaphoreType.DMA((max(parts, 1),))]


def on_slots(kernel, name, scalars, inputs, outputs, scratch, parts_in=(), parts_out=(), counted=0, ordered=False):
    count, total, given = len(inputs), len(inputs) + len(outputs), len(scalars)

    def body(*refs):
        scalar_refs, refs = refs[:given], refs[given:]
        far_in, refs = refs[:count], refs[count:]
        if counted:
            scalar_refs, refs = scalar_refs + refs[:1], refs[1:]
        far, refs = far_in + refs[: total - count], refs[total - count :]
        slots = []
        for i in range(total):
            parts = far[i].shape[0] if (i in parts_in if i < count else i - count in parts_out) else 0
            slots.append(Slot(far[i], refs[2 * i], refs[2 * i + 1], parts))
        if not ordered:
            for slot in slots[:count]:
                slot.fetch()
        kernel(scalar_refs, slots[:count], slots[count:], refs[2 * total :])
        for slot in slots[count:]:
            slot.finish()

    spaces = []
    for i, array in enumerate(inputs):
        spaces += slot_scratch(array.shape, array.dtype, array.shape[0] if i in parts_in else 0)
    for i, (shape, kind) in enumerate(outputs):
        spaces += slot_scratch(shape, kind, shape[0] if i in parts_out else 0)
    any_space, smem = pl.BlockSpec(memory_space=pl.ANY), pl.BlockSpec(memory_space=pltpu.SMEM)
    first = [jax.ShapeDtypeStruct((counted,), jnp.int32)] if counted else []
    return pl.pallas_call(
        body,
        out_shape=first + [jax.ShapeDtypeStruct(shape, kind) for shape, kind in outputs],
        in_specs=[smem] * given + [any_space] * count,
        out_specs=[smem] * len(first) + [any_space] * len(outputs),
        scratch_shapes=spaces + [entry if hasattr(entry, "memory_space") else pltpu.VMEM(*entry) for entry in scratch],
        compiler_params=pltpu.CompilerParams(vmem_limit_bytes=63 << 20),
        name=name,
    )(*scalars, *inputs)


def nn(left, right):
    return lax.dot_general(left, right, (((1,), (0,)), ((), ())), preferred_element_type=jnp.float32)


def nt(left, right):
    return lax.dot_general(left, right, (((1,), (1,)), ((), ())), preferred_element_type=jnp.float32)


def tn(left, right):
    return lax.dot_general(left, right, (((0,), (0,)), ((), ())), preferred_element_type=jnp.float32)


def part(ref, which):
    inner = ref.shape[2] // 4 if ref.shape[2] == 768 else 192
    return jnp.concatenate([ref[m, which * 192 : (which + 1) * 192, :] for m in range(4)], axis=0)


def store_part(ref, which, value):
    low = value.astype(jnp.bfloat16)
    for m in range(4):
        ref[m, which * 192 : (which + 1) * 192, :] = low[m * 192 : (m + 1) * 192]


def tiles(amount, step):
    def wrap(body):
        @pl.loop(0, amount // step)
        def _(i):
            body(pl.ds(pl.multiple_of(i * step, step), step))

    return wrap


def lanes():
    place = lax.broadcasted_iota(jnp.int32, (1, 2 * HEAD_DIM), 1)
    low = place < HEAD_DIM
    return low, low.astype(jnp.float32), 1.0 - low.astype(jnp.float32)


def norm_forward(total, unit, inverse, value, value_low, gain, shift):
    @tiles(total.shape[0], 80)
    def _(rows):
        hidden = total[rows, :]
        center = hidden - jnp.mean(hidden, axis=-1, keepdims=True)
        factor = lax.rsqrt(jnp.mean(center * center, axis=-1, keepdims=True) + 1e-06)
        scaled = center * factor
        result = scaled * gain[...] + shift[...]
        if unit is not None:
            unit[rows, :] = scaled
            inverse[rows, :] = jnp.broadcast_to(factor, (80, 128))
        if value is not None:
            value[rows, :] = result
        value_low[rows, :] = result.astype(jnp.bfloat16)


def norm_reverse(upstream, unit, inverse, gain, gain_grad, shift_grad, grad, grad_low):
    gain_grad[...] = jnp.zeros_like(gain_grad)
    shift_grad[...] = jnp.zeros_like(shift_grad)

    @tiles(upstream.shape[0], 80)
    def _(rows):
        up = upstream[rows, :].astype(jnp.float32)
        scaled = unit[rows, :]
        factor = inverse[rows, :][:, :1]
        gain_grad[...] += jnp.sum(up * scaled, axis=0, keepdims=True)
        shift_grad[...] += jnp.sum(up, axis=0, keepdims=True)
        inner = up * gain[...]
        result = factor * (
            inner
            - jnp.mean(inner, axis=-1, keepdims=True)
            - scaled * jnp.mean(inner * scaled, axis=-1, keepdims=True)
        )
        grad[rows, :] = result
        grad_low[rows, :] = result.astype(jnp.bfloat16)


def softmax(scores):
    raised = jnp.exp(scores - jnp.max(scores, axis=-1, keepdims=True))
    return (raised * (1.0 / jnp.sum(raised, axis=-1, keepdims=True))).astype(jnp.bfloat16)


def columns(width):
    return [slice(start, start + 128) for start in range(0, width, 128)]


def stack(value, first, second):
    return jnp.concatenate([value * first, value * second], axis=0)


def merge(low, value):
    half = value.shape[0] // 2
    return jnp.where(low, value[:half], value[half:])


def attend_self(queries, keys, values, lengths, probs, context):
    low, first, second = lanes()
    first, second = first.astype(jnp.bfloat16), second.astype(jnp.bfloat16)
    cols = columns(queries.shape[1])
    query = lax.broadcasted_iota(jnp.int32, (160, 80), 0)
    key = lax.broadcasted_iota(jnp.int32, (160, 80), 1)
    query = jnp.where(query >= 80, query - 80, query)
    same = (query < 40) == (key < 40)

    @pl.loop(0, queries.shape[0] // 80)
    def _(pair):
        rows = pl.ds(pl.multiple_of(pair * 80, 80), 80)
        allowed = same & (key < jnp.where(key < 40, lengths(2 * pair), lengths(2 * pair + 1) + 40))
        stacked = [stack(queries[rows, c], first, second) for c in cols]
        scores = [nt(both, keys[rows, c]) * HEAD_DIM ** (-0.5) for both, c in zip(stacked, cols)]
        weights = [softmax(jnp.where(allowed, score, -1000000000.0)) for score in scores]
        mixed = [merge(low, nn(weight, values[rows, c])) for weight, c in zip(weights, cols)]
        for tile, c in enumerate(cols):
            probs[pair, tile] = weights[tile]
            context[rows, c] = mixed[tile].astype(jnp.bfloat16)


def attend_cross(image, caption, wide, keys, values, cell_ok, probs, begin, end):
    low, first, second = lanes()
    cols = columns(wide.shape[1])

    @pl.loop(begin, end)
    def _(row):
        rows = pl.ds(pl.multiple_of(row * 40, 40), 40)
        which = image[row]
        cells = cell_ok[pl.ds(row, 1), :] + caption[row].astype(jnp.float32)
        allowed = jnp.broadcast_to(cells, (80, cell_ok.shape[1])) > 0
        stacked = [stack(wide[rows, c], first, second).astype(jnp.bfloat16) for c in cols]
        scores = [nt(both, keys[which, :, c]) * HEAD_DIM ** (-0.5) for both, c in zip(stacked, cols)]
        weights = [softmax(jnp.where(allowed, score, -1000000000.0)) for score in scores]
        mixed = [merge(low, nn(weight, values[which, :, c])) for weight, c in zip(weights, cols)]
        for tile, c in enumerate(cols):
            probs[row, tile] = weights[tile]
            wide[rows, c] = mixed[tile]


def prepare(counts, lengths, boxes, vectors, cells_all, image, caption, cell_ok, norms, near, plane):
    rows, padded = cell_ok.shape
    cells, images, _ = cells_all.shape
    window = near.shape[0]
    start = jnp.minimum(plane * rows // ROWS_MAX, images - window)

    @pl.loop(0, rows)
    def _(r):
        row = plane * rows + r
        end, here, before = jnp.int32(0), jnp.int32(0), jnp.int32(0)
        for i in range(images):
            end = end + counts[0, i]
            here = here + (end <= row).astype(jnp.int32)
            before = before + (end <= row - 1).astype(jnp.int32)
        image[r] = jnp.minimum(jnp.maximum(here - start, 0), window - 1)
        caption[r] = jnp.where(row == 0, jnp.int32(1), here - before)

    cell_ok[...] = jnp.full(cell_ok.shape, -2.0, jnp.float32)
    cell_ok[:, :cells] = (boxes[pl.ds(pl.multiple_of(plane * rows, 8), rows), :] > 0).astype(jnp.float32)
    norms[...] = jnp.zeros_like(norms)
    for i, vector in enumerate(vectors):
        norms[pl.ds(i, 1), :] = vector[...].reshape(1, norms.shape[1])
    step = 16
    for first in range(0, padded, step):
        amount = min(step, cells - first)
        to = lax.broadcasted_iota(jnp.int32, (window * step, amount * images), 0)
        source = lax.broadcasted_iota(jnp.int32, (window * step, amount * images), 1)
        pick = (source // images == to % step) & (source % images == to // step + start)
        block = cells_all[first : first + amount].reshape(amount * images, cells_all.shape[2])
        block = nn(pick.astype(jnp.bfloat16), block).astype(jnp.bfloat16)
        near[:, first : first + step, :] = block.reshape(window, step, cells_all.shape[2])


def forward_steps(ticks, image, caption, lengths, tokens, near, cell_ok, weights, norms, saved, wide):
    bf16 = jnp.bfloat16
    self_weights, cross_weights, keyval = weights
    (
        queries, keys, values, self_probs, self_context, first_unit, first_inverse, first_low, cross_queries, image_keys,
        image_values, cross_probs, cross_context, second_unit, second_inverse, second_value, second_low,
    ) = (slot.near for slot in saved)

    def flush(*places):
        for place in places:
            saved[place].flush()

    gains = [norms.at[pl.ds(i, 1), :] for i in range(4)]
    ticks.wait(0)
    for target, which in ((queries, 0), (keys, 1), (values, 2)):
        target[...] = nt(tokens[...], part(self_weights, which)).astype(bf16)
    flush(0, 1, 2)
    ticks()
    attend_self(queries, keys, values, lengths, self_probs, self_context)
    flush(3, 4)
    ticks()
    second_value[...] = nn(self_context[...], part(self_weights, 3)) + tokens[...].astype(jnp.float32)
    norm_forward(second_value, first_unit, first_inverse, None, first_low, gains[0], gains[1])
    flush(5, 6, 7)
    ticks.wait(1)
    cross_queries[...] = nt(first_low[...], part(cross_weights, 0)).astype(bf16)
    flush(8)
    wide[...] = cross_queries[...].astype(jnp.float32)
    images, cells, depth = near.shape
    half = images // 2
    ticks.wait(2)
    for target, which in ((image_keys, 0), (image_values, 1)):
        weight = part(keyval, which)
        for step in range(2):
            block = near[step * half : (step + 1) * half].reshape(half * cells, depth)
            target[step * half : (step + 1) * half] = nt(block, weight).astype(bf16).reshape(half, cells, -1)
        flush(9 + which)
    ticks()
    rows = cell_ok.shape[0]
    for part_of in range(2):
        begin, end = part_of * rows // 2, (part_of + 1) * rows // 2
        attend_cross(image, caption, wide, image_keys, image_values, cell_ok, cross_probs, begin, end)
        ticks()
    flush(11)
    cross_context[...] = wide[...].astype(bf16)
    flush(12)
    second_value[...] = nn(cross_context[...], part(cross_weights, 1)) + (first_unit[...] * gains[0][...] + gains[1][...])
    norm_forward(second_value, second_unit, second_inverse, second_value, second_low, gains[2], gains[3])
    flush(13, 14, 15, 16)


def feed_kernel(scalars, inputs, outputs, scratch):
    second_value, second_low, norms, expand, shrink, cotangent = inputs
    joined, expand_grad, shrink_grad, vectors, second_up = outputs
    active, slope, unit, inverse, feed_low = scratch
    bf16 = jnp.bfloat16
    for slot in (second_low, norms):
        slot.fetch()
    expand.copy(False, 0).start()
    second_value.fetch()
    shrink.copy(False, 0).start()
    total = second_up.near
    second_low, norms = second_low.ready(), norms.ready()
    total[...] = second_value.ready()[...]
    for m in range(1, expand.near.shape[0]):
        expand.copy(False, m).start()
        shrink.copy(False, m).start()
    cotangent.fetch()
    gain, shift = norms.at[0, pl.ds(4, 1), :], norms.at[0, pl.ds(5, 1), :]
    hidden, amount = expand.near.shape[0], total.shape[0]
    halves = [slice(0, amount // 2), slice(amount // 2, amount)]

    @pl.loop(0, hidden)
    def _(m):
        expand.copy(False, m).wait()
        shrink.copy(False, m).wait()
        inners = [nn(second_low[rows, :], expand.near[m]) + norms[m, pl.ds(6, 1), :] for rows in halves]
        shares = [0.5 * (1.0 + lax.erf(inner * 0.5**0.5)) for inner in inners]
        acts = [(inner * share).astype(bf16) for inner, share in zip(inners, shares)]
        slopes = [
            (share + inner * (jnp.exp(-0.5 * inner * inner) * 0.3989422804014327)).astype(bf16)
            for inner, share in zip(inners, shares)
        ]
        for rows, act, inclination in zip(halves, acts, slopes):
            active[m, rows, :] = act
            slope[m, rows, :] = inclination
            total[rows, :] += nn(act, shrink.near[m])

    norm_forward(total, unit, inverse, None, joined.near, gain, shift)
    joined.flush()
    sums = vectors.near
    sums[...] = jnp.zeros_like(sums)
    norm_reverse(
        cotangent.ready(), unit, inverse, gain, sums.at[pl.ds(8, 1), :], sums.at[pl.ds(9, 1), :], total, feed_low
    )

    @pl.loop(0, hidden)
    def _(m):
        shrink_grad.near[m] = tn(active[m], feed_low[...]).astype(bf16)
        shrink_grad.flush(m)
        lows = [
            (nt(feed_low[rows, :], shrink.near[m]) * slope[m, rows, :].astype(jnp.float32)).astype(bf16) for rows in halves
        ]
        parts = [jnp.sum(low.astype(jnp.float32), axis=0, keepdims=True) for low in lows]
        sums[pl.ds(m, 1), :] = parts[0] + parts[1]
        for rows, low in zip(halves, lows):
            active[m, rows, :] = low
        expand_grad.near[m] = tn(second_low[...], active[m]).astype(bf16)
        expand_grad.flush(m)
        total[...] += nt(active[m], expand.near[m])

    vectors.flush()
    second_up.flush()


def score_back(weights, upstream):
    probs = weights.astype(jnp.float32)
    return (probs * (upstream - jnp.sum(probs * upstream, axis=-1, keepdims=True))).astype(jnp.bfloat16)


def cross_back_kernel(scalars, inputs, outputs, scratch):
    (image,) = scalars
    (
        second_up, second_unit, second_inverse, norms, cross_weights, cross_context, cross_queries, image_values,
        image_keys, cross_probs, first_low, keyval, near,
    ) = inputs
    weights_grad, keyval_grad, patch, vectors, first_up = outputs
    grad_low, wide, turn, key_sum, value_sum, query_low = scratch
    bf16 = jnp.bfloat16
    low, first, second = lanes()
    for slot in inputs[:4]:
        slot.fetch()
    for slot in inputs[:4]:
        slot.ready()
    for slot in inputs[4:]:
        slot.fetch()
    sums = vectors.near
    sums[...] = jnp.zeros_like(sums)
    norm_reverse(
        second_up.near, second_unit.near, second_inverse.near, norms.near.at[0, pl.ds(2, 1), :],
        sums.at[pl.ds(6, 1), :], sums.at[pl.ds(7, 1), :], first_up.near, grad_low,
    )
    vectors.flush()
    cross_weights = cross_weights.ready()
    wide[...] = nt(grad_low[...], part(cross_weights, 1)).astype(bf16).astype(jnp.float32)
    store_part(weights_grad.near, 1, tn(cross_context.ready()[...], grad_low[...]))
    turn[...] = cross_queries.ready()[...].astype(jnp.float32)
    key_sum[...] = jnp.zeros_like(key_sum)
    value_sum[...] = jnp.zeros_like(value_sum)
    cols = columns(wide.shape[1])
    image_values, image_keys, cross_probs = image_values.ready(), image_keys.ready(), cross_probs.ready()

    @pl.loop(0, cross_probs.shape[0])
    def _(row):
        rows = pl.ds(pl.multiple_of(row * 40, 40), 40)
        which = image[row]
        queries = [stack(turn[rows, c], first, second).astype(bf16) for c in cols]
        grads = [stack(wide[rows, c], first, second).astype(bf16) for c in cols]
        weights = [cross_probs[row, tile] for tile in range(len(cols))]
        upstream = [nt(grad, image_values[which, :, c]) for grad, c in zip(grads, cols)]
        back = [score_back(weight, up) for weight, up in zip(weights, upstream)]
        mixed = [merge(low, nn(grad, image_keys[which, :, c])) * HEAD_DIM ** (-0.5) for grad, c in zip(back, cols)]
        key_parts = [tn(grad, both) * HEAD_DIM ** (-0.5) for grad, both in zip(back, queries)]
        value_parts = [tn(weight, grad) for weight, grad in zip(weights, grads)]
        for tile, c in enumerate(cols):
            turn[rows, c] = mixed[tile]
        for tile, c in enumerate(cols):
            key_sum[which, :, c] += key_parts[tile]
        for tile, c in enumerate(cols):
            value_sum[which, :, c] += value_parts[tile]

    keyval, near = keyval.ready(), near.ready()
    images, cells, depth = near.shape
    amount = images * cells
    quarter, size, half = patch.near.shape[2], (patch.near.shape[1] - 16) // images, images // 2
    last = jnp.zeros((16, depth), jnp.float32)
    for step in range(2):
        here = slice(step * half, (step + 1) * half)
        block = nn(key_sum[here].astype(bf16).reshape(amount // 2, -1), part(keyval, 0))
        block += nn(value_sum[here].astype(bf16).reshape(amount // 2, -1), part(keyval, 1))
        block = block.astype(bf16)
        row = lax.broadcasted_iota(jnp.int32, (16, amount // 2), 0)
        source = lax.broadcasted_iota(jnp.int32, (16, amount // 2), 1)
        last += nn((source == (row - step * half) * cells + size).astype(bf16), block)
        for m in range(patch.near.shape[0]):
            for i in range(half):
                rows = pl.ds((step * half + i) * size, size)
                patch.near[m, rows, :] = block[i * cells : i * cells + size, m * quarter : (m + 1) * quarter]
    for m in range(patch.near.shape[0]):
        patch.near[m, pl.ds(images * size, 16), :] = last[:, m * quarter : (m + 1) * quarter].astype(bf16)
    patch.flush()
    for source, which in ((key_sum, 0), (value_sum, 1)):
        flat = source[...].astype(bf16).reshape(amount, -1)
        store_part(keyval_grad.near, which, tn(flat, near[...].reshape(amount, depth)))
    keyval_grad.flush()
    query_low[...] = turn[...].astype(bf16)
    first_up.near[...] += nn(query_low[...], part(cross_weights, 0))
    first_up.flush()
    store_part(weights_grad.near, 0, tn(query_low[...], first_low.ready()[...]))
    weights_grad.flush()


def self_back_steps(ticks, inputs, weights_grad, sums, text_grad, scratch):
    (
        first_up, first_unit, first_inverse, norms, self_weights, self_context, queries, keys, values, self_probs, tokens,
    ) = inputs
    grad_low, context_low, query_low, key_low, value_low = scratch
    bf16 = jnp.bfloat16
    low, first, second = lanes()
    first_mask, second_mask = first.astype(bf16), second.astype(bf16)
    norm_reverse(
        first_up.ready(), first_unit.ready(), first_inverse.ready(), norms.ready().at[0, pl.ds(0, 1), :],
        sums.at[pl.ds(4, 1), :], sums.at[pl.ds(5, 1), :], text_grad, grad_low,
    )
    self_weights = self_weights.ready()
    context_low[...] = nt(grad_low[...], part(self_weights, 3)).astype(bf16)
    store_part(weights_grad, 3, tn(self_context.ready()[...], grad_low[...]))
    cols = columns(context_low.shape[1])
    queries, keys, values, self_probs = queries.ready(), keys.ready(), values.ready(), self_probs.ready()
    ticks()

    @pl.loop(0, self_probs.shape[0])
    def _(pair):
        rows = pl.ds(pl.multiple_of(pair * 80, 80), 80)
        stacked = [stack(queries[rows, c], first_mask, second_mask) for c in cols]
        grads = [stack(context_low[rows, c], first_mask, second_mask) for c in cols]
        weights = [self_probs[pair, tile] for tile in range(len(cols))]
        upstream = [nt(grad, values[rows, c]) for grad, c in zip(grads, cols)]
        back = [score_back(weight, up) for weight, up in zip(weights, upstream)]
        query_parts = [merge(low, nn(grad, keys[rows, c])) * HEAD_DIM ** (-0.5) for grad, c in zip(back, cols)]
        key_parts = [tn(grad, both) * HEAD_DIM ** (-0.5) for grad, both in zip(back, stacked)]
        value_parts = [tn(weight, grad) for weight, grad in zip(weights, grads)]
        for tile, c in enumerate(cols):
            query_low[rows, c] = query_parts[tile].astype(bf16)
            key_low[rows, c] = key_parts[tile].astype(bf16)
            value_low[rows, c] = value_parts[tile].astype(bf16)

    ticks()
    tokens = tokens.ready()
    for source, which in ((query_low, 0), (key_low, 1), (value_low, 2)):
        store_part(weights_grad, which, tn(source[...], tokens[...]))
        text_grad[...] += nn(source[...], part(self_weights, which))


def lone_self_back_kernel(scalars, inputs, outputs, scratch):
    weights_grad, vectors, text_grad = outputs
    vectors.near[...] = jnp.zeros_like(vectors.near)
    self_back_steps(Alone(), inputs, weights_grad.near, vectors.near, text_grad.near, scratch)
    for slot in outputs:
        slot.flush()


def finish_kernel(alone, scalars, inputs, outputs, scratch):
    self_sum, cross_sum, keyval_sum, expand_sum, shrink_sum, vectors, windows, merged, text = inputs
    text_grad, project, self_out, query, cross_out, keyval, expand, shrink, patch_grad, *norms, bias = outputs
    inner = self_out.near.shape[0]

    def give(output, value):
        output.near[...] = value.astype(jnp.float32)
        output.flush()

    give(text_grad, text.ready()[...])
    give(shrink, shrink_sum.ready()[...])
    give(expand, expand_sum.ready()[...])
    give(project, self_sum.ready()[: 3 * inner, :])
    give(self_out, self_sum.near[3 * inner :, :])
    give(query, cross_sum.ready()[:inner, :])
    give(cross_out, cross_sum.near[inner:, :])
    give(keyval, keyval_sum.ready()[...])
    sums = vectors.ready().at[vectors.near.shape[0] - 1]
    for i, output in enumerate(norms):
        give(output, sums[4 + i : 5 + i, :].reshape(sums.shape[1]))
    plane = lax.axis_index("mp")
    give(bias, sums[pl.ds(plane, 1), :].reshape(sums.shape[1]))
    windows, merged = windows.ready(), merged.ready()
    cells, images, quarter = patch_grad.near.shape
    size, step, rows = cells - 1, 16, scalars[0].shape[0]
    amount = (windows.shape[1] - step) // size

    def first_image(m):
        return jnp.minimum(m * rows // ROWS_MAX, images - amount)

    def place(sources):
        for first in range(0, size, step):
            total = jnp.zeros((step * images, quarter), jnp.float32)
            for window, start in sources:
                count = (window.shape[0] - step) // size
                to = lax.broadcasted_iota(jnp.int32, (step * images, count * step), 0)
                source = lax.broadcasted_iota(jnp.int32, (step * images, count * step), 1)
                pick = (to // images == source % step) & (to % images == source // step + start)
                block = [window[pl.ds(i * size + first, step), :] for i in range(count)]
                total = total + nn(pick.astype(jnp.bfloat16), jnp.concatenate(block, axis=0))
            patch_grad.near[first : first + step] = total.reshape(step, images, quarter)
        total = jnp.zeros((images, quarter), jnp.float32)
        for window, start in sources:
            count = (window.shape[0] - step) // size
            to = lax.broadcasted_iota(jnp.int32, (images, step), 0)
            source = lax.broadcasted_iota(jnp.int32, (images, step), 1)
            pick = (to == source + start) & (source < count)
            total = total + nn(pick.astype(jnp.bfloat16), window[pl.ds(count * size, step), :])
        patch_grad.near[size] = total

    if alone:
        place([(windows.at[m], first_image(m)) for m in range(4)])
    else:
        outer = (plane == 0) | (plane == 3)

        @pl.when(outer)
        def _():
            beside = jnp.where(plane == 0, 1, 2)
            place(
                [(windows.at[m], first_image(m)) for m in (plane, beside)]
                + [(merged, jnp.where(plane == 0, first_image(2), first_image(0)))]
            )

        @pl.when(jnp.logical_not(outer))
        def _():
            place([(windows.at[m], first_image(m)) for m in range(4)])

    patch_grad.flush()


def image_windows(parts, rows, group_images):
    group_rows = parts * rows
    first = [m * rows // ROWS_MAX for m in range(parts)]
    last = [group_images - 1 - max(0, -(-(group_rows - (m + 1) * rows - (ROWS_MAX - 1)) // ROWS_MAX)) for m in range(parts)]
    last = [min(stop, (m + 1) * rows - 1) for m, stop in enumerate(last)]
    window = max(stop - start + 1 for start, stop in zip(first, last))
    return [min(start, group_images - window) for start in first], window


def forward(scalars, inputs, cells_all, shards, outputs, near, chunks, own):
    if own:
        return gather_forward(scalars, inputs, cells_all, shards, outputs, near, chunks)
    weights = [lax.all_gather(jnp.concatenate(pieces, axis=0), "mp", axis=0) for pieces in shards]
    vectors = jnp.stack(inputs[2:] + [jnp.zeros_like(inputs[2])])
    biases = lax.all_gather(vectors, "mp", axis=0)
    amount, width = inputs[0].shape
    rows = amount // 40
    image, *saved = on_slots(
        lone_forward_kernel, "forward", scalars, inputs + [cells_all] + weights[:3], outputs + [near],
        [((amount, width), jnp.float32), ((rows, near[0][1]), jnp.float32), ((8, width), jnp.float32)]
        + [pltpu.SMEM((rows,), jnp.int32)],
        counted=rows,
    )
    return image, weights, biases, saved[:-1], saved[-1]


def reduce_shards(grads, patch, early, inputs, window, shift, chunks, own):
    if own:
        return reduce_back(grads, patch, early, inputs, window, shift, chunks)
    flat, weights = inputs[0].shape, inputs[4].shape
    self_grad, late, text_grad = on_slots(
        lone_self_back_kernel, "self_back", [], inputs,
        [(weights, jnp.bfloat16), (early[0].shape, jnp.float32), (flat, jnp.float32)], [(flat, jnp.bfloat16)] * 5,
    )
    sums = [
        lax.psum(lax.psum_scatter(grad.astype(jnp.float32), "mp", scatter_dimension=0, tiled=True)[0], "dp").astype(grad.dtype)
        for grad in [self_grad] + grads
    ]
    windows = lax.all_to_all(patch, "mp", split_axis=0, concat_axis=0, tiled=True)
    return sums, windows, windows[0], lax.psum(early[0] + early[1] + late, ("dp", "mp"))[None], text_grad


def per_device(
    tokens, patches, image_rows, row_lengths, box_mask, self_project, self_output, first_gain, first_shift, cross_query,
    cross_keyval, cross_output, second_gain, second_shift, expand_weight, expand_bias, shrink_weight, third_gain,
    third_shift, cotangent, *, parts, own,
):
    bf16, f32 = jnp.bfloat16, jnp.float32
    rows, slots, width = tokens.shape
    group_images, cells, depth = patches.shape
    starts, window = image_windows(parts, rows, group_images)
    padded = -(-cells // 16) * 16
    amount, pairs, tiles_of = rows * slots, rows // 2, width // 128
    inner = self_output.shape[0]
    shards = [
        [self_project.transpose(0, 2, 1).reshape(3 * inner, width), self_output],
        [cross_query.T, cross_output],
        [cross_keyval.transpose(0, 2, 1).reshape(2 * inner, depth)],
        [expand_weight],
        [shrink_weight],
    ]
    chunks = [(0, 0, 384), (0, 384, 384), (1, 0, 384), (2, 0, 384), (3, 0, 384), (3, 384, 384), (4, 0, 384), (4, 384, 384)]
    text = tokens.reshape(amount, width)
    flat, unit_row = (amount, width), ((amount, 128), f32)
    low_flat, full_flat = (flat, bf16), (flat, f32)
    probs_self, probs_cross = (pairs, tiles_of, 4 * slots, 2 * slots), (rows, tiles_of, 2 * slots, padded)
    image_part, vector = ((window, padded, width), bf16), ((16, width), f32)
    image, weights, norms, saved, near = forward(
        [image_rows, row_lengths],
        [text, box_mask, first_gain, first_shift, second_gain, second_shift, third_gain, third_shift, expand_bias],
        patches.transpose(1, 0, 2),
        shards,
        [low_flat] * 3 + [(probs_self, bf16), low_flat, full_flat, unit_row, low_flat, low_flat]
        + [image_part, image_part, (probs_cross, bf16), low_flat, full_flat, unit_row, full_flat, low_flat],
        ((window, padded, depth), bf16),
        chunks,
        own,
    )
    self_weights, cross_weights, keyval, expand, shrink = weights
    (
        queries, keys, values, self_probs, self_context, first_unit, first_inverse, first_low, cross_queries, image_keys,
        image_values, cross_probs, cross_context, second_unit, second_inverse, second_value, second_low,
    ) = saved
    joined, expand_grad, shrink_grad, feed_vectors, second_up = on_slots(
        feed_kernel,
        "feed",
        [],
        [second_value, second_low, norms, expand, shrink, cotangent.reshape(flat)],
        [low_flat, (expand.shape, bf16), (shrink.shape, bf16), vector, full_flat],
        [((parts,) + flat, bf16)] * 2 + [full_flat, unit_row, low_flat],
        parts_in=(3, 4),
        parts_out=(1, 2),
        ordered=True,
    )
    cross_weights_grad, keyval_grad, patch, cross_vectors, first_up = on_slots(
        cross_back_kernel,
        "cross_back",
        [image],
        [second_up, second_unit, second_inverse, norms, cross_weights, cross_context, cross_queries, image_values]
        + [image_keys, cross_probs, first_low, keyval, near],
        [(cross_weights.shape, bf16), (keyval.shape, bf16), ((parts, window * (cells - 1) + 16, depth // parts), bf16)]
        + [vector, full_flat],
        [low_flat, full_flat, full_flat, (image_part[0], f32), (image_part[0], f32), low_flat],
        ordered=True,
    )
    order = [(4, 0, 384), (4, 384, 384), (3, 0, 384), (3, 384, 384), (1, 0, 384), (2, 0, 384), (0, 0, 384), (0, 384, 384)]
    sums, windows, merged, vectors, text_grad = reduce_shards(
        [cross_weights_grad, keyval_grad, expand_grad, shrink_grad],
        patch,
        [feed_vectors, cross_vectors],
        [first_up, first_unit, first_inverse, norms, self_weights, self_context, queries, keys, values, self_probs, text],
        window,
        starts[1] - starts[0],
        order,
        own,
    )
    square, piece, line = ((width, width), f32), ((inner, width), f32), ((width,), f32)
    text_grad, project, self_out, query, cross_out, pixel, expand_sum, shrink_sum, patch_grad, *lines = on_slots(
        functools.partial(finish_kernel, not own),
        "finish",
        [image],
        list(sums) + [vectors, windows, merged, text_grad],
        [full_flat, ((3 * inner, width), f32), piece, piece, piece, ((2 * inner, depth), f32), square, square]
        + [((cells, group_images, depth // parts), f32)]
        + [line] * 7,
        [],
    )
    return (
        joined.reshape(tokens.shape),
        text_grad.reshape(tokens.shape),
        patch_grad.transpose(1, 0, 2),
        project.reshape(3, inner, width).transpose(0, 2, 1),
        self_out,
        lines[0],
        lines[1],
        query.T,
        pixel.reshape(2, inner, depth).transpose(0, 2, 1),
        cross_out,
        lines[2],
        lines[3],
        expand_sum,
        lines[6],
        shrink_sum,
        lines[4],
        lines[5],
    )


def solution(mesh):
    parts = mesh.shape["mp"]
    own = mesh.shape["dp"] == 8 and parts == 4
    return jax.shard_map(
        functools.partial(per_device, parts=parts, own=own),
        mesh=mesh,
        in_specs=(
            P(("dp", "mp"), None, None),
            P("dp", None, None),
            P("dp", None),
            P("dp"),
            P("dp", None),
            P(None, None, "mp"),
            P("mp", None),
            P(),
            P(),
            P(None, "mp"),
            P(None, None, "mp"),
            P("mp", None),
            P(),
            P(),
            P(None, "mp"),
            P("mp"),
            P("mp", None),
            P(),
            P(),
            P(("dp", "mp"), None, None),
        ),
        out_specs=(
            P(("dp", "mp"), None, None),
            P(("dp", "mp"), None, None),
            P("dp", None, "mp"),
            P(None, None, "mp"),
            P("mp", None),
            P(),
            P(),
            P(None, "mp"),
            P(None, None, "mp"),
            P("mp", None),
            P(),
            P(),
            P(None, "mp"),
            P("mp"),
            P("mp", None),
            P(),
            P(),
        ),
        check_vma=False,
    )
```
